32 devices in a mesh: seq: 8 (over z, y), fsdp: 4 (over x, core).
Axes of the slice: x: 2, y: 2, z: 4, core: 2. Of those that a mesh axis runs over, the one named last changes fastest.
Arguments:
- self_query: bfloat16 [4, 2048, 2048], P('fsdp', 'seq'), may hold values from -8 to 8, as said below
- self_key: bfloat16 [4, 2048, 2048], P('fsdp', 'seq'), may hold values from -8 to 8, as said below
- self_value: bfloat16 [4, 2048, 2048], P('fsdp', 'seq'), may hold values from -6 to 6
- cross_query: bfloat16 [4, 2048, 2048], P('fsdp', 'seq'), may hold values from -6 to 6
- neighbours: bfloat16 [4, 32, 256, 768], P('fsdp', 'seq'), may hold values from -6 to 6
- neighbour_count: int32 [4, 32], P('fsdp', 'seq'), may hold values from 1 to 2
- kv_weight: bfloat16 [768, 4096], P('fsdp'), may hold values from -0.21875 to 0.21875
- out_grad: bfloat16 [4, 2048, 2048], P('fsdp', 'seq'), may hold values from -6 to 6
Outputs:
- block_out: bfloat16 [4, 2048, 2048], P('fsdp', 'seq')
- query_grad: bfloat16 [4, 2048, 2048], P('fsdp', 'seq')
- key_grad: bfloat16 [4, 2048, 2048], P('fsdp', 'seq')
- value_grad: bfloat16 [4, 2048, 2048], P('fsdp', 'seq')
- cross_grad: bfloat16 [4, 2048, 2048], P('fsdp', 'seq')
- weight_grad: float32 [768, 4096], P(('seq', 'fsdp'))
The draws below stay inside these ranges and needn't reach their ends.
Inputs may be any that keep to these rules, and one draw needn't show every extreme that they name: `self_query`: entries of order one. `self_key`: entries of order one.
All inputs are finite; a program needn't handle non-finite values.
Results may differ from the reference program's by a relative error of at most 0.014.
Values may be sent and summed in bfloat16 or wider, within the bound.
No kernel may reach another device: no remote copies, remote signals or barrier semaphores. Data moves between devices by JAX's collectives and lax.ppermute only.
A program may use at most 192 MiB of HBM per device.

```python
import jax
import jax.numpy as jnp
from jax import lax

HEADS = 16
HD = 128
ENC = 768
GROUP = 64
NEIGH = 2
RLEN = 128
HW = 2048
NB = 256
WINDOW = 256
FILES = 4
SEQ_LEN = 2048
GROUPS = 32


def draw_self_query(key, part):
    values_drawn = jnp.clip(jax.random.normal(jax.random.fold_in(key, 1), (FILES, SEQ_LEN, HW), jnp.float32), -6.0, 6.0)
    return values_drawn.astype(jnp.bfloat16)


def draw_self_key(key, part):
    values_drawn = jnp.clip(jax.random.normal(jax.random.fold_in(key, 2), (FILES, SEQ_LEN, HW), jnp.float32), -6.0, 6.0)
    return values_drawn.astype(jnp.bfloat16)


def set_ends(values, own_key, least, high):
    longest = values.shape.index(max(values.shape))
    spots = []
    for shift in (0, 1):
        where = [jax.random.randint(jax.random.fold_in(own_key, axis), (), 0, length) for axis, length in enumerate(values.shape)]
        where[longest] = (where[longest] + shift) % values.shape[longest]
        spots.append(tuple(where))
    return values.at[spots[0]].set(least).at[spots[1]].set(high)


def with_spikes(entries, stream_key, source, target, shards_of, factor):
    def block_of(dim):
        return (jnp.arange(entries.shape[dim]) // (entries.shape[dim] // shards_of)).reshape((-1,) + (1,) * (entries.ndim - 1 - dim))

    one_side = jax.random.permutation(stream_key, shards_of)[block_of(target)]
    second = (block_of(target) + shards_of // 2) % shards_of
    return jnp.where((block_of(source) == one_side) | (block_of(source) == second), factor * entries, entries)


def levels(rng, shape, pieces, least, top_value):
    factor_of, own = 1.0, jax.random.fold_in(rng, 6)
    for axis_at, parts in pieces:
        draws = jnp.exp(jax.random.uniform(jax.random.fold_in(own, axis_at), (parts,), jnp.float32, least / len(pieces), top_value / len(pieces)))
        factor_of = factor_of * jnp.repeat(draws, shape[axis_at] // parts).reshape([-1 if axis == axis_at else 1 for axis in range(len(shape))])
    return factor_of


def centred(key, dims, deviation, most, cuts=(), kind=jnp.bfloat16):
    gain = levels(key, dims, cuts, -0.22, 0.18) if cuts else 1.0
    drawn = jax.random.normal(key, dims, jnp.float32) * deviation * gain
    return jnp.minimum(jnp.maximum(drawn, -most), most).astype(kind)


def gaussian_with(rng, extent, width, most, pieces, heavy, kind=jnp.bfloat16):
    entries = width * jax.random.normal(rng, extent, jnp.float32)
    if pieces:
        entries = entries * levels(rng, extent, pieces, -0.22, 0.18)
    return jnp.clip(with_spikes(entries, jax.random.fold_in(rng, 3), *heavy), -most, most).astype(kind)


def setup_inputs(seed: int = 0) -> dict:
    seeds = jax.random.split(jax.random.key(seed), 9)
    self_query = draw_self_query(jax.random.fold_in(seeds[8], 71), 0)
    self_key = draw_self_key(jax.random.fold_in(seeds[8], 71), 0)
    self_value = centred(seeds[2], (FILES, SEQ_LEN, HW), 1.0, 6.0, ((0, 4), (1, 8)))
    cross_query = centred(seeds[3], (FILES, SEQ_LEN, HW), 1.0, 6.0, ((0, 4), (1, 8)))
    neighbours = gaussian_with(seeds[4], (FILES, GROUPS, NB, ENC), 1.0, 6.0, ((0, 4), (1, 8)), (1, 3, 8, 2.0))
    neighbour_count = set_ends(jax.random.randint(seeds[5], (FILES, GROUPS), 1, NEIGH + 1), jax.random.fold_in(seeds[5], 1), 1, NEIGH).astype(jnp.int32)
    kv_weight = centred(seeds[6], (ENC, 2 * HW), ENC ** -0.5, 0.21875, ((0, 4),))
    out_grad = centred(seeds[7], (FILES, SEQ_LEN, HW), 1.0, 6.0, ((0, 4), (1, 8)))
    return {"self_query": self_query, "self_key": self_key, "self_value": self_value, "cross_query": cross_query, "neighbours": neighbours, "neighbour_count": neighbour_count, "kv_weight": kv_weight, "out_grad": out_grad}


neg_fill = -1e30


def attend(queries, keys_in, values_in, grads, allowed, scaling):
    query_full = queries.astype(jnp.float32)
    key_full = keys_in.astype(jnp.float32)
    value_full = values_in.astype(jnp.float32)
    grad_full = grads.astype(jnp.float32)
    scores = jnp.einsum("...qhd,...khd->...hqk", query_full, key_full) * scaling
    scores = jnp.where(allowed, scores, neg_fill)
    peaks = jnp.max(scores, axis=-1, keepdims=True)
    weights = jnp.exp(scores - peaks)
    probs = weights / jnp.sum(weights, axis=-1, keepdims=True)
    probs_low = lax.optimization_barrier(probs.astype(jnp.bfloat16)).astype(jnp.float32)
    output = jnp.einsum("...hqk,...khd->...qhd", probs_low, value_full)
    prob_grad = jnp.einsum("...qhd,...khd->...hqk", grad_full, value_full)
    row_delta = jnp.sum(probs * prob_grad, axis=-1, keepdims=True)
    score_grad = lax.optimization_barrier((probs * (prob_grad - row_delta) * scaling).astype(jnp.bfloat16)).astype(jnp.float32)
    query_grad = jnp.einsum("...hqk,...khd->...qhd", score_grad, key_full)
    key_grad = jnp.einsum("...hqk,...qhd->...khd", score_grad, query_full)
    value_grad = jnp.einsum("...hqk,...qhd->...khd", probs_low, grad_full)
    return output, query_grad, key_grad, value_grad


def self_file(query_file, key_file, value_file, grad_file):
    tok_rows = WINDOW
    blocks = SEQ_LEN // tok_rows
    scaling = HD ** -0.5

    def blocked(array):
        return array.reshape(blocks, tok_rows, HEADS, HD)

    zero_block = jnp.zeros((1, tok_rows, HEADS, HD), jnp.bfloat16)
    key_blocks = blocked(key_file)
    value_blocks = blocked(value_file)
    key_before = jnp.concatenate([zero_block, key_blocks[:-1]], 0)
    value_before = jnp.concatenate([zero_block, value_blocks[:-1]], 0)
    row_index = jnp.arange(tok_rows, dtype=jnp.int32)[:, None]
    col_index = jnp.arange(2 * tok_rows, dtype=jnp.int32)[None, :]

    def one_block(inputs):
        query_block, key_prev, key_own, value_prev, value_own, grad_block, block_id = inputs
        allowed = (col_index > row_index) & (col_index <= row_index + tok_rows) & ((col_index >= tok_rows) | (block_id > 0))
        return attend(query_block, jnp.concatenate([key_prev, key_own], 0), jnp.concatenate([value_prev, value_own], 0), grad_block, allowed[None], scaling)

    output, query_grad, key_terms, value_terms = lax.map(one_block, (blocked(query_file), key_before, key_blocks, value_before, value_blocks, blocked(grad_file), jnp.arange(blocks, dtype=jnp.int32)))
    zero_terms = jnp.zeros((1, tok_rows, HEADS, HD), jnp.float32)
    key_grad = key_terms[:, tok_rows:] + jnp.concatenate([key_terms[1:, :tok_rows], zero_terms], 0)
    value_grad = value_terms[:, tok_rows:] + jnp.concatenate([value_terms[1:, :tok_rows], zero_terms], 0)
    return output.reshape(SEQ_LEN, HW), query_grad.reshape(SEQ_LEN, HW), key_grad.reshape(SEQ_LEN, HW), value_grad.reshape(SEQ_LEN, HW)


def cross_file(query_file, grad_file, neigh_file, count_file, kv_weight):
    neigh_rows = NEIGH * RLEN
    scaling = HD ** -0.5
    flat_neigh = neigh_file.reshape(GROUPS * neigh_rows, ENC)
    kv_proj = jnp.dot(flat_neigh, kv_weight, preferred_element_type=jnp.float32).astype(jnp.bfloat16).reshape(GROUPS, neigh_rows, 2 * HW)
    keys_all = kv_proj[..., :HW].reshape(GROUPS, neigh_rows, HEADS, HD)
    values_all = kv_proj[..., HW:].reshape(GROUPS, neigh_rows, HEADS, HD)
    key_before = jnp.concatenate([keys_all[:1], keys_all[:-1]], 0)
    value_before = jnp.concatenate([values_all[:1], values_all[:-1]], 0)
    count_before = jnp.concatenate([count_file[:1], count_file[:-1]], 0)
    neighbour_of = jnp.arange(neigh_rows, dtype=jnp.int32) // RLEN

    def one_group(inputs):
        query_group, grad_group, key_group, value_group, count_group, group_id = inputs
        allowed = (neighbour_of < count_group)[None, None, :]
        output, query_grad, key_grad, value_grad = attend(query_group, key_group, value_group, grad_group, allowed, scaling)
        live = group_id > 0
        output = jnp.where(live, output, 0.0)
        query_grad = jnp.where(live, query_grad, 0.0)
        kv_grad = jnp.concatenate([key_grad.reshape(neigh_rows, HW), value_grad.reshape(neigh_rows, HW)], -1)
        kv_grad = jnp.where(live, kv_grad, 0.0).astype(jnp.bfloat16)
        return output, query_grad, kv_grad

    group_view = (GROUPS, GROUP, HEADS, HD)
    output, query_grad, kv_grads = lax.map(one_group, (query_file.reshape(group_view), grad_file.reshape(group_view), key_before, value_before, count_before, jnp.arange(GROUPS, dtype=jnp.int32)))
    kv_grad_group = jnp.concatenate([kv_grads[1:], jnp.zeros((1, neigh_rows, 2 * HW), jnp.bfloat16)], 0)
    weight_part = jnp.dot(flat_neigh.T, kv_grad_group.reshape(GROUPS * neigh_rows, 2 * HW), preferred_element_type=jnp.float32)
    return output.reshape(SEQ_LEN, HW), query_grad.reshape(SEQ_LEN, HW), weight_part


def reference(self_query, self_key, self_value, cross_query, neighbours, neighbour_count, kv_weight, out_grad):
    def one_file(inputs):
        query_file, key_file, value_file, cross_file_q, neigh_file, count_file, grad_file = inputs
        self_out, query_grad, key_grad, value_grad = self_file(query_file, key_file, value_file, grad_file)
        cross_out, cross_grad, weight_part = cross_file(cross_file_q, grad_file, neigh_file, count_file, kv_weight)
        block_out = (self_out + cross_out).astype(jnp.bfloat16)
        return block_out, query_grad.astype(jnp.bfloat16), key_grad.astype(jnp.bfloat16), value_grad.astype(jnp.bfloat16), cross_grad.astype(jnp.bfloat16), weight_part

    block_out, query_grad, key_grad, value_grad, cross_grad, weight_parts = lax.map(one_file, (self_query, self_key, self_value, cross_query, neighbours, neighbour_count, out_grad))
    weight_grad = jnp.sum(weight_parts, axis=0)
    return (block_out, query_grad, key_grad, value_grad, cross_grad, weight_grad)
```

```python
import functools

import numpy as np
import jax
import jax.numpy as jnp
from jax import lax
from jax.experimental import pallas as pl
from jax.experimental.pallas import tpu as pltpu
from jax.sharding import PartitionSpec as P

HEADS = 16
HD = 128
GROUP = 64
RLEN = 128
PAIR = 2 * HD
CHUNKS = 4
SCALE = HD ** (-0.5)
LOG2E = 1.4426950408889634
NEG = -1e30
BF = jnp.bfloat16
F32 = jnp.float32

NT = (((1,), (1,)), ((), ()))
TN = (((0,), (0,)), ((), ()))
NN = (((1,), (0,)), ((), ()))


def mm(a, b, dims):
    return lax.dot_general(a, b, dims, preferred_element_type=F32)


def shift(value, axis, steps):
    count = lax.axis_size(axis)
    first, last = max(0, -steps), min(count, count - steps)
    return lax.ppermute(value, axis, [(i, i + steps) for i in range(first, last)])


def swap(value, axis, bit):
    return lax.ppermute(value, axis, [(i, i ^ bit) for i in range(lax.axis_size(axis))])


def cross_kernel(
    pieces, groups, info_ref, count_ref, nb_ref, nbt_ref, *refs
):
    weights, refs = refs[: 2 * pieces], refs[2 * pieces :]
    cq_ref, do_ref, out_ref, dq_ref, keep_ref, send_ref, w_ref, kv_ref, dkv_ref = refs
    shard = info_ref[0]
    rows = weights[0].shape[0]
    for piece in range(pieces):
        at = pl.ds(pl.multiple_of((shard ^ piece) * rows, 16), rows)
        w_ref[at, :PAIR] = weights[2 * piece][...]
        w_ref[at, PAIR:] = weights[2 * piece + 1][...]
    kv_ref[...] = mm(nb_ref[...], w_ref[...], NN).astype(BF)
    per = 2 * RLEN
    zero = jnp.zeros((GROUP, HD), BF)

    def diagonal(ref, u):
        block = ref[u * GROUP : (u + 1) * GROUP, :]
        return jnp.concatenate(
            [
                jnp.concatenate([block[:, :HD], zero], 1),
                jnp.concatenate([zero, block[:, HD:]], 1),
            ],
            0,
        )

    for u in range(groups):
        count = count_ref[u]
        at = slice(u * per, (u + 1) * per)
        keys, values = kv_ref[at, :PAIR], kv_ref[at, PAIR:]
        queries, grads = diagonal(cq_ref, u), diagonal(do_ref, u)
        scores = mm(keys, queries, NT)
        prob_grad = mm(values, grads, NT)
        row = lax.broadcasted_iota(jnp.int32, (per, 2 * GROUP), 0)
        scores = jnp.where(row < count * RLEN, scores, NEG)
        peak = jnp.max(scores, axis=0, keepdims=True)
        weight = jnp.exp2((scores - peak) * (SCALE * LOG2E))
        total = jnp.sum(weight, axis=0, keepdims=True)
        inverse = jnp.where(count > 0, 1.0 / total, 0.0)
        probs = weight * inverse
        delta = jnp.sum(probs * prob_grad, axis=0, keepdims=True)
        score_grad = (probs * (prob_grad - delta)).astype(BF)
        low = probs.astype(BF)
        out = mm(low, values, TN).astype(BF)
        dq = (mm(score_grad, keys, TN) * SCALE).astype(BF)
        tok = slice(u * GROUP, (u + 1) * GROUP)
        out_ref[tok, :HD] = out[:GROUP, :HD]
        out_ref[tok, HD:] = out[GROUP:, HD:]
        dq_ref[tok, :HD] = dq[:GROUP, :HD]
        dq_ref[tok, HD:] = dq[GROUP:, HD:]
        dkv_ref[at, :PAIR] = (mm(score_grad, queries, NN) * SCALE).astype(BF)
        dkv_ref[at, PAIR:] = mm(low, grads, NN).astype(BF)
    half = keep_ref.shape[1]
    bit = shard & 1
    for ref, which in ((send_ref, 1 - bit), (keep_ref, bit)):
        at = pl.ds(pl.multiple_of(which * half, 16), half)
        part = mm(nbt_ref[at, :], dkv_ref[...], NN).astype(BF)
        ref[0] = part[:, :PAIR]
        ref[1] = part[:, PAIR:]


def cross(chunk, info, count, nb, nbt, weights, cq, do):
    pieces = len(weights)
    pairs = HEADS // 2 // CHUNKS
    first = chunk * pairs
    groups = cq.shape[0] // GROUP
    tokens, enc = cq.shape[0], nb.shape[1]
    shard_rows = enc // pieces
    whole = lambda p: (0, 0)
    here = lambda p: (0, first + p)
    specs, operands = [], []
    for piece in weights:
        width = piece.shape[1]
        start = first if width == 2 * HEADS * HD else 0
        other = width // PAIR // 2
        specs.append(pl.BlockSpec((shard_rows, PAIR), lambda p, s=start: (0, s + p)))
        specs.append(pl.BlockSpec((shard_rows, PAIR), lambda p, s=start + other: (0, s + p)))
        operands += [piece, piece]
    part = jax.ShapeDtypeStruct((2, enc // 2, pairs * PAIR), BF)
    part_spec = pl.BlockSpec((2, enc // 2, PAIR), lambda p: (0, 0, p))
    tok_spec = pl.BlockSpec((tokens, PAIR), lambda p: (0, p))
    tok_shape = jax.ShapeDtypeStruct((tokens, pairs * PAIR), BF)
    smem = pl.BlockSpec(memory_space=pltpu.SMEM)
    return pl.pallas_call(
        functools.partial(cross_kernel, pieces, groups),
        grid=(pairs,),
        in_specs=[smem, smem, pl.BlockSpec(nb.shape, whole), pl.BlockSpec(nbt.shape, whole)]
        + specs
        + [pl.BlockSpec((tokens, PAIR), here)] * 2,
        out_specs=[tok_spec, tok_spec, part_spec, part_spec],
        out_shape=[tok_shape, tok_shape, part, part],
        scratch_shapes=[
            pltpu.VMEM((enc, 2 * PAIR), BF),
            pltpu.VMEM((nb.shape[0], 2 * PAIR), BF),
            pltpu.VMEM((nb.shape[0], 2 * PAIR), BF),
        ],
        compiler_params=pltpu.CompilerParams(vmem_limit_bytes=40 * 2**20),
        cost_estimate=pl.CostEstimate(
            flops=pairs * 2_200_000_000, bytes_accessed=8_000_000, transcendentals=0
        ),
    )(info, count, nb, nbt, *operands, cq, do)


def self_kernel(
    heads, info_ref, q_ref, do_ref, kp_ref, ko_ref, vp_ref, vo_ref, co_ref,
    out_ref, dq_ref, dk_ref, dv_ref, stat_ref,
):
    later = info_ref[1] > 0
    tokens = q_ref.shape[0]
    half = tokens // 2
    key_at = lax.broadcasted_iota(jnp.int32, (half, half), 0)
    query_at = lax.broadcasted_iota(jnp.int32, (half, half), 1)
    above = jnp.logical_and(key_at > query_at, later)
    below = key_at <= query_at
    zero = jnp.zeros((half, half), BF)
    lo, hi = slice(0, half), slice(half, None)
    for head in range(heads):
        at = slice(head * HD, (head + 1) * HD)
        queries, grads = q_ref[:, at], do_ref[:, at]
        kp, ko, vp, vo = kp_ref[:, at], ko_ref[:, at], vp_ref[:, at], vo_ref[:, at]
        sp, so = mm(kp, queries, NT), mm(ko, queries, NT)
        gp, go = mm(vp, grads, NT), mm(vo, grads, NT)
        rows = []
        for a in (0, 1):
            if a == 0:
                blocks = (sp[lo, lo], sp[hi, lo], so[lo, lo])
                pgrads = (gp[lo, lo], gp[hi, lo], go[lo, lo])
                middle = jnp.where(later, blocks[1], NEG)
            else:
                blocks = (sp[hi, hi], so[lo, hi], so[hi, hi])
                pgrads = (gp[hi, hi], go[lo, hi], go[hi, hi])
                middle = blocks[1]
            scores = (jnp.where(above, blocks[0], NEG), middle, jnp.where(below, blocks[2], NEG))
            peak = jnp.max(
                jnp.maximum(jnp.maximum(scores[0], scores[1]), scores[2]), axis=0, keepdims=True
            )
            weight = [jnp.exp2((s - peak) * (SCALE * LOG2E)) for s in scores]
            total = jnp.sum(weight[0] + weight[1] + weight[2], axis=0, keepdims=True)
            inverse = 1.0 / total
            probs = [w * inverse for w in weight]
            delta = jnp.sum(
                probs[0] * pgrads[0] + probs[1] * pgrads[1] + probs[2] * pgrads[2],
                axis=0,
                keepdims=True,
            )
            score_grad = [(p * (g - delta)).astype(BF) for p, g in zip(probs, pgrads)]
            rows.append(([p.astype(BF) for p in probs], score_grad))
            lanes = slice(a * half, (a + 1) * half)
            stat_ref[head, 0:1, lanes] = peak * (SCALE * LOG2E) + jnp.log2(total)
            stat_ref[head, 1:2, lanes] = delta

        def spread(which):
            first, second = rows[0][which], rows[1][which]
            before = jnp.concatenate(
                [
                    jnp.concatenate([first[0], zero], 1),
                    jnp.concatenate([first[1], second[0]], 1),
                ],
                0,
            )
            own = jnp.concatenate(
                [
                    jnp.concatenate([first[2], second[1]], 1),
                    jnp.concatenate([zero, second[2]], 1),
                ],
                0,
            )
            return before, own

        (pp, po), (dp, do) = spread(0), spread(1)
        out = mm(pp, vp, TN) + mm(po, vo, TN) + co_ref[:, at].astype(F32)
        out_ref[:, at] = out.astype(BF)
        dq_ref[:, at] = ((mm(dp, kp, TN) + mm(do, ko, TN)) * SCALE).astype(BF)
        dk_ref[:, at] = mm(do, queries, NN) * SCALE
        dv_ref[:, at] = mm(po, grads, NN)


def self_part(info, q, do, kp, ko, vp, vo, co):
    heads = 2
    tokens, width = q.shape
    spec = pl.BlockSpec((tokens, heads * HD), lambda p: (0, p))
    shape = jax.ShapeDtypeStruct(q.shape, BF)
    wide = jax.ShapeDtypeStruct(q.shape, F32)
    return pl.pallas_call(
        functools.partial(self_kernel, heads),
        grid=(width // (heads * HD),),
        in_specs=[pl.BlockSpec(memory_space=pltpu.SMEM)] + [spec] * 7,
        out_specs=[spec] * 4 + [pl.BlockSpec((heads, 2, tokens), lambda p: (p, 0, 0))],
        out_shape=[shape, shape, wide, wide, jax.ShapeDtypeStruct((width // HD, 2, tokens), F32)],
        compiler_params=pltpu.CompilerParams(vmem_limit_bytes=40 * 2**20),
        cost_estimate=pl.CostEstimate(
            flops=10_000_000_000, bytes_accessed=14_000_000, transcendentals=0
        ),
    )(info, q, do, kp, ko, vp, vo, co)


def next_kernel(
    heads, q_ref, do_ref, k_ref, v_ref, stat_ref, dkp_ref, dvp_ref, dk_ref, dv_ref
):
    tokens = q_ref.shape[0]
    half = tokens // 2
    key_at = lax.broadcasted_iota(jnp.int32, (half, half), 0)
    query_at = lax.broadcasted_iota(jnp.int32, (half, half), 1)
    above = key_at > query_at
    zero = jnp.zeros((half, half), BF)
    lo, hi = slice(0, half), slice(half, None)
    for head in range(heads):
        at = slice(head * HD, (head + 1) * HD)
        queries, grads = q_ref[:, at], do_ref[:, at]
        scores = mm(k_ref[:, at], queries, NT)
        prob_grad = mm(v_ref[:, at], grads, NT)
        level, delta = stat_ref[head, 0:1, :], stat_ref[head, 1:2, :]

        def block(rows, lanes, mask):
            exponent = scores[rows, lanes] * (SCALE * LOG2E) - level[:, lanes]
            if mask:
                exponent = jnp.where(above, exponent, NEG)
            probs = jnp.exp2(exponent)
            return probs.astype(BF), (probs * (prob_grad[rows, lanes] - delta[:, lanes])).astype(BF)

        first, middle, last = block(lo, lo, True), block(hi, lo, False), block(hi, hi, True)
        low, score_grad = [
            jnp.concatenate(
                [
                    jnp.concatenate([first[i], zero], 1),
                    jnp.concatenate([middle[i], last[i]], 1),
                ],
                0,
            )
            for i in (0, 1)
        ]
        dk_ref[:, at] = (dkp_ref[:, at] + mm(score_grad, queries, NN) * SCALE).astype(BF)
        dv_ref[:, at] = (dvp_ref[:, at] + mm(low, grads, NN)).astype(BF)


def next_part(q, do, k, v, stats, dk, dv):
    heads = 2
    tokens, width = q.shape
    spec = pl.BlockSpec((tokens, heads * HD), lambda p: (0, p))
    shape = jax.ShapeDtypeStruct(q.shape, BF)
    return pl.pallas_call(
        functools.partial(next_kernel, heads),
        grid=(width // (heads * HD),),
        in_specs=[spec] * 4
        + [pl.BlockSpec((heads, 2, tokens), lambda p: (p, 0, 0))]
        + [spec] * 2,
        out_specs=[spec] * 2,
        out_shape=[shape, shape],
        compiler_params=pltpu.CompilerParams(vmem_limit_bytes=40 * 2**20),
        cost_estimate=pl.CostEstimate(
            flops=6_000_000_000, bytes_accessed=10_000_000, transcendentals=0
        ),
    )(q, do, k, v, stats, dk, dv)


def halving_order(fsdp, seq):
    bits = [("fsdp", 1 << i) for i in range(fsdp.bit_length() - 1)]
    seq_bits = [("seq", 1 << i) for i in range(seq.bit_length() - 1)]
    return bits + seq_bits[1:] + seq_bits[:1]


def row_order(fsdp, seq, rows):
    index = np.arange(rows).reshape(seq * fsdp, -1)
    block = np.arange(seq * fsdp)
    keys = []
    for axis, bit in halving_order(fsdp, seq):
        value = block % fsdp if axis == "fsdp" else block // fsdp
        keys.append((value // bit) % 2)
    order = np.lexsort(keys[::-1])
    return index[order].reshape(-1)


def take_half(value, upper):
    half = value.shape[1] // 2
    return lax.dynamic_slice_in_dim(value, upper * half, half, 1)


def halve(keep, received, bit, dtype):
    mine = take_half(keep, bit).astype(F32) + take_half(received, bit).astype(F32)
    other = take_half(keep, 1 - bit).astype(F32) + take_half(received, 1 - bit).astype(F32)
    return mine.astype(dtype), other.astype(BF)


def on_device(
    self_query, self_key, self_value, cross_query, neighbours, neighbour_count, kv_weight, out_grad
):
    fsdp, seq = lax.axis_size("fsdp"), lax.axis_size("seq")
    shard, slab = lax.axis_index("fsdp"), lax.axis_index("seq")
    q, k, v, cq, do = (x[0] for x in (self_query, self_key, self_value, cross_query, out_grad))
    nb, counts = neighbours[0], neighbour_count[0]
    tokens, width = q.shape
    groups, enc = nb.shape[0], nb.shape[2]
    info = jnp.stack([shard, slab]).astype(jnp.int32)

    nb_last, count_last = shift((nb[groups - 1], counts[groups - 1 :].astype(F32)), "seq", 1)
    rows = kv_weight.shape[0]
    per = width // CHUNKS
    columns = kv_weight.reshape(rows, 2, CHUNKS, per)
    pieces = [[kv_weight, swap(kv_weight, "fsdp", 1)] for _ in range(1)][0]
    far = []
    for chunk in range(CHUNKS):
        piece = columns[:, :, chunk].reshape(rows, 2 * per)
        if chunk >= 2:
            piece, _ = lax.optimization_barrier((piece, far[chunk - 2][0]))
        piece = swap(piece, "fsdp", 2)
        far.append((piece, swap(piece, "fsdp", 1)))
    k_before, v_before = shift((k, v), "seq", 1)
    q_late, do_late, _, _ = lax.optimization_barrier((q, do, k_before, v_before))
    q_after, do_after = shift((q_late, do_late), "seq", -1)

    nb_used = jnp.concatenate([nb_last[None], nb[: groups - 1]], 0).reshape(-1, enc)
    count_used = jnp.concatenate(
        [count_last.astype(jnp.int32), counts[: groups - 1]], 0
    )
    order = row_order(fsdp, seq, enc)
    pick = (jnp.asarray(order, jnp.int32)[:, None] == jnp.arange(enc, dtype=jnp.int32)).astype(BF)
    nb_turned = mm(pick, nb_used, NT).astype(BF)

    stages = halving_order(fsdp, seq)

    def my_bit(stage):
        axis, bit = stages[stage]
        return ((shard if axis == "fsdp" else slab) // bit) % 2

    cross_out, cross_grad, parts = [], [], []
    for chunk in range(CHUNKS):
        out, dq, keep, send = cross(
            chunk, info, count_used, nb_used, nb_turned, pieces + list(far[chunk]), cq, do
        )
        cross_out.append(out)
        cross_grad.append(dq)
        for stage in range(len(stages)):
            received = swap(send, *stages[stage])
            if stage + 1 < len(stages):
                keep, send = halve(keep, received, my_bit(stage + 1), BF)
            else:
                keep = keep.astype(F32) + received.astype(F32)
        parts.append(keep)
    weight_grad = jnp.concatenate(parts, -1).transpose(1, 0, 2).reshape(-1, 2 * width)
    cross_out = jnp.concatenate(cross_out, 1)
    cross_grad = jnp.concatenate(cross_grad, 1)

    block_out, query_grad, dk, dv, stats = self_part(
        info, q, do, k_before, k, v_before, v, cross_out
    )
    stats_after = shift(stats, "seq", -1)
    key_grad, value_grad = next_part(q_after, do_after, k, v, stats_after, dk, dv)
    return (
        block_out[None],
        query_grad[None],
        key_grad[None],
        value_grad[None],
        cross_grad[None],
        weight_grad,
    )


def solution(mesh):
    in_specs = (
        P("fsdp", "seq", None),
        P("fsdp", "seq", None),
        P("fsdp", "seq", None),
        P("fsdp", "seq", None),
        P("fsdp", "seq", None, None),
        P("fsdp", "seq"),
        P("fsdp", None),
        P("fsdp", "seq", None),
    )
    out_specs = (
        P("fsdp", "seq", None),
        P("fsdp", "seq", None),
        P("fsdp", "seq", None),
        P("fsdp", "seq", None),
        P("fsdp", "seq", None),
        P(("seq", "fsdp"), None),
    )
    return jax.shard_map(
        on_device, mesh=mesh, in_specs=in_specs, out_specs=out_specs, check_vma=False
    )
```

```python
import functools

import numpy as np
import jax
import jax.numpy as jnp
from jax import lax
from jax.experimental import pallas as pl
from jax.experimental.pallas import tpu as pltpu
from jax.sharding import PartitionSpec as P

HEADS = 16
HD = 128
GROUP = 64
RLEN = 128
PAIR = 2 * HD
CHUNKS = HEADS // 4
SPLIT = 2
VMEM = 60 * 2**20
SCALE = HD ** (-0.5)
LOG2E = 1.4426950408889634
NEG = -1e30
BF = jnp.bfloat16
F32 = jnp.float32
ANY = pl.BlockSpec(memory_space=pl.ANY)

NT = (((1,), (1,)), ((), ()))
TN = (((0,), (0,)), ((), ()))
NN = (((1,), (0,)), ((), ()))


def cost(micros):
    return pl.CostEstimate(flops=int(micros * 1e9), bytes_accessed=1000, transcendentals=0)


def mm(a, b, dims):
    return lax.dot_general(a, b, dims, preferred_element_type=F32)


def shift(value, axis, steps):
    count = lax.axis_size(axis)
    first, last = max(0, -steps), min(count, count - steps)
    return lax.ppermute(value, axis, [(i, i + steps) for i in range(first, last)])


def after(value, *others):
    return lax.optimization_barrier((value, *others))[0]


def swap(value, axis, bit):
    return lax.ppermute(value, axis, [(i, i ^ bit) for i in range(lax.axis_size(axis))])


def count_rows(count_ref, width):
    row = lax.broadcasted_iota(jnp.int32, (16, width), 0)
    tail = jnp.zeros((16, width), F32)
    for u in range(count_ref.shape[0]):
        tail = jnp.where(row == u, count_ref[u].astype(F32), tail)
    return tail.astype(BF)


def pack_kernel(count_ref, nb_ref, out_ref):
    per, enc = nb_ref.shape[1:]
    out_ref[:per, :] = nb_ref[0]
    out_ref[per:, :] = count_rows(count_ref, enc)


def pack(nb, counts):
    groups, per, enc = nb.shape
    return pl.pallas_call(
        pack_kernel,
        grid=(1,),
        in_specs=[
            pl.BlockSpec(memory_space=pltpu.SMEM),
            pl.BlockSpec((1, per, enc), lambda p: (groups - 1, 0, 0)),
        ],
        out_specs=pl.BlockSpec((per + 16, enc), lambda p: (0, 0)),
        out_shape=jax.ShapeDtypeStruct((per + 16, enc), BF),
        compiler_params=pltpu.CompilerParams(vmem_limit_bytes=VMEM),
        cost_estimate=cost(2),
    )(counts, nb)


def cut_kernel(info_ref, count_ref, *refs):
    sources, refs = refs[:6], refs[6:]
    parts, (first_ref, other_ref, pair_ref) = refs[:-3], refs[-3:]
    for which in (0, 1):
        keys, values = sources[2 * which : 2 * which + 2]
        for chunk in range(CHUNKS):
            at = slice(chunk * PAIR, (chunk + 1) * PAIR)
            part = jnp.concatenate([keys[:, at], values[:, at]], 1)
            if which:
                other_ref[chunk] = part
            else:
                parts[chunk][...] = part
            if which and not chunk:
                first_ref[...] = part
    tokens, width = sources[4].shape
    for index in (0, 1):
        pair_ref[index, :tokens, :] = sources[4 + index][...]
        pair_ref[index, tokens:, :] = count_rows(count_ref, width)


def cut(info, counts, weight, cq, do):
    rows = weight.shape[0]
    tokens, width = cq.shape
    whole = lambda p, info: (0, 0)
    part = jax.ShapeDtypeStruct((rows, 2 * PAIR), BF)
    parts = jax.ShapeDtypeStruct((CHUNKS, rows, 2 * PAIR), BF)
    half = jax.ShapeDtypeStruct((2, tokens + 16, width // 2), BF)

    def columns(height, other, value):
        return pl.BlockSpec(
            (height, width // 2), lambda p, info: (0, 2 * value + ((info[0] & 1) ^ other))
        )

    *mine, first, other, pair = pl.pallas_call(
        cut_kernel,
        grid_spec=pltpu.PrefetchScalarGridSpec(
            num_scalar_prefetch=1,
            grid=(1,),
            in_specs=[pl.BlockSpec(memory_space=pltpu.SMEM)]
            + [columns(rows, other, value) for other in (0, 1) for value in (0, 1)]
            + [columns(tokens, 1, 0)] * 2,
            out_specs=[pl.BlockSpec(part.shape, whole)] * (CHUNKS + 1)
            + [pl.BlockSpec(x.shape, lambda p, info: (0, 0, 0)) for x in (parts, half)],
        ),
        out_shape=[part] * (CHUNKS + 1) + [parts, half],
        compiler_params=pltpu.CompilerParams(vmem_limit_bytes=VMEM),
        cost_estimate=cost(3),
    )(info, counts, weight, weight, weight, weight, cq, do)
    return mine, first, other, pair


def stack_kernel(*refs):
    mine, near_ref, outs = refs[: CHUNKS - 1], refs[CHUNKS - 1], refs[CHUNKS:]
    for chunk, (ref, out) in enumerate(zip(mine, outs)):
        rows = ref.shape[0]
        out[:rows, :] = ref[...]
        out[rows:, :] = near_ref[chunk + 1]


def stack(mine, near):
    rows, width = mine[0].shape
    return pl.pallas_call(
        stack_kernel,
        out_shape=[jax.ShapeDtypeStruct((2 * rows, width), BF)] * (CHUNKS - 1),
        compiler_params=pltpu.CompilerParams(vmem_limit_bytes=VMEM),
        cost_estimate=cost(2),
    )(*mine[1:], near)


def join_kernel(first, second, *refs):
    for index, ref in enumerate(refs):
        width = ref.shape[1] // 2
        at = slice(index * width, (index + 1) * width)
        ref[:, :width] = first[:, at]
        ref[:, width:] = second[:, at]


def join(first, second, parts):
    tokens, width = first.shape
    rows = tokens // 4
    return pl.pallas_call(
        join_kernel,
        grid=(4,),
        in_specs=[pl.BlockSpec((rows, width), lambda p: (p, 0))] * 2,
        out_specs=[pl.BlockSpec((rows, 2 * width // parts), lambda p: (p, 0))] * parts,
        out_shape=[jax.ShapeDtypeStruct((tokens, 2 * width // parts), BF)] * parts,
        compiler_params=pltpu.CompilerParams(vmem_limit_bytes=VMEM),
        cost_estimate=cost(2),
    )(first, second)


def cross_kernel(chunk, slot, turns, pieces, info_ref, count_ref, *refs):
    (turn_ref, nb_last, nb_own, peer_last, nb_peer), refs = refs[:5], refs[5:]
    weights, refs = refs[:pieces], refs[pieces:]
    (cq_ref, do_ref, peer_ref), refs = refs[:3], refs[3:]
    refs = refs[len(refs) - 17 - turns :]
    (own_out, peer_out, keep_out, send_out), refs = refs[:4], refs[4:]
    turned_out, refs = (refs[0], refs[1:]) if turns else (None, refs)
    (w_ref, nb_ref, turned_ref, kv_ref, dkv_ref, q_ref, g_ref, tail_ref), refs = refs[:8], refs[8:]
    out_ref, dw_ref, pick_ref, sem, out_sem = refs
    shard = info_ref[0]
    enc = w_ref.shape[0]
    tokens = q_ref.shape[1]
    groups = tokens // GROUP
    per = 2 * RLEN
    size = groups * per
    rows = enc // 4
    loads = []

    def load(source, target):
        copy = pltpu.make_async_copy(source, target, sem.at[len(loads)])
        copy.start()
        loads.append(copy)
        return copy

    waits_w, piece = [], 0
    for ref in weights:
        source = ref.at[chunk] if len(ref.shape) == 3 else ref
        for start in range(0, source.shape[0], rows):
            at = pl.ds(pl.multiple_of((shard ^ piece) * rows, 16), rows)
            waits_w.append(load(source.at[start : start + rows, :], w_ref.at[at, :]))
            piece += 1
    waits_nb = [
        load(nb_last.at[:per, :], nb_ref.at[:per, :]),
        *[load(nb_own.at[u - 1], nb_ref.at[u * per : (u + 1) * per, :]) for u in range(1, groups)],
        load(peer_last.at[:per, :], nb_ref.at[size : size + per, :]),
        *[
            load(nb_peer.at[u - 1], nb_ref.at[size + u * per : size + (u + 1) * per, :])
            for u in range(1, groups)
        ],
    ]
    lanes = pl.ds(pl.multiple_of(((shard & 1) * CHUNKS + chunk) * PAIR, PAIR), PAIR)
    there = slice(chunk * PAIR, (chunk + 1) * PAIR)
    waits_q = [
        load(cq_ref.at[:, lanes], q_ref.at[0]),
        load(do_ref.at[:, lanes], g_ref.at[0]),
        load(peer_ref.at[0, :tokens, there], q_ref.at[1]),
        load(peer_ref.at[1, :tokens, there], g_ref.at[1]),
        load(nb_last.at[per:, : 2 * GROUP], tail_ref.at[0]),
        load(peer_last.at[per:, : 2 * GROUP], tail_ref.at[1]),
        load(peer_ref.at[0, tokens:, : 2 * GROUP], tail_ref.at[2]),
    ]
    wait_turn = load(turn_ref, pick_ref if turns else turned_ref)
    for copy in waits_w:
        copy.wait()
    for file in (0, 1):
        for start, stop in ((0, 1), (1, groups)):
            for copy in waits_nb[file * groups + start : file * groups + stop]:
                copy.wait()
            at = slice(file * size + start * per, file * size + stop * per)
            kv_ref[at, :] = mm(nb_ref[at, :], w_ref[...], NN).astype(BF)
    for copy in waits_q:
        copy.wait()
    zero = jnp.zeros((GROUP, HD), BF)

    def diagonal(block):
        return jnp.concatenate(
            [
                jnp.concatenate([block[:, :HD], zero], 1),
                jnp.concatenate([zero, block[:, HD:]], 1),
            ],
            0,
        )

    row = lax.broadcasted_iota(jnp.int32, (per, 2 * GROUP), 0).astype(F32)
    for file in (0, 1):
        for u in range(groups):
            if u == 0:
                count = tail_ref[file, groups - 1 : groups, :].astype(F32)
            elif file:
                count = tail_ref[2, u - 1 : u, :].astype(F32)
            else:
                count = count_ref[u - 1].astype(F32)
            unit = file * groups + u
            at = slice(unit * per, (unit + 1) * per)
            tok = slice(u * GROUP, (u + 1) * GROUP)
            keys, values = kv_ref[at, :PAIR], kv_ref[at, PAIR:]
            queries, grads = diagonal(q_ref[file, tok, :]), diagonal(g_ref[file, tok, :])
            scores = mm(keys, queries, NT)
            prob_grad = mm(values, grads, NT)
            scores = jnp.where(row < count * RLEN, scores, NEG)
            peak = jnp.max(scores, axis=0, keepdims=True)
            weight = jnp.exp2((scores - peak) * (SCALE * LOG2E))
            total = jnp.sum(weight, axis=0, keepdims=True)
            inverse = jnp.where(count > 0, 1.0 / total, 0.0)
            probs = weight * inverse
            delta = jnp.sum(probs * prob_grad, axis=0, keepdims=True)
            score_grad = (probs * (prob_grad - delta)).astype(BF)
            low = probs.astype(BF)
            out = mm(low, values, TN).astype(BF)
            dq = (mm(score_grad, keys, TN) * SCALE).astype(BF)
            for index, value in enumerate((out, dq)):
                out_ref[file, index, tok, :HD] = value[:GROUP, :HD]
                out_ref[file, index, tok, HD:] = value[GROUP:, HD:]
            dkv_ref[at, :PAIR] = (mm(score_grad, queries, NN) * SCALE).astype(BF)
            dkv_ref[at, PAIR:] = mm(low, grads, NN).astype(BF)
    stores = []

    def store(source, target):
        copy = pltpu.make_async_copy(source, target, out_sem.at[len(stores)])
        copy.start()
        stores.append(copy)

    store(out_ref.at[0], own_out.at[:, :, there])
    store(out_ref.at[1], peer_out.at[:, :, there])
    wait_turn.wait()
    if turns:
        turned_ref[...] = mm(pick_ref[...], nb_ref[...], NT).astype(BF)
        store(turned_ref, turned_out)
    half = enc // 2
    bit = (shard // 2) % 2
    for index, (target, which) in enumerate(((send_out, 1 - bit), (keep_out, bit))):
        at = pl.ds(pl.multiple_of(which * half, 16), half)
        dw_ref[index] = mm(turned_ref[at, :], dkv_ref[...], NN).astype(BF)
        store(dw_ref.at[index], target.at[slot])
    for copy in stores:
        copy.wait()


def cross(chunk, info, counts, turn, nbs, weights, cq, do, peer, crossed, kept):
    tokens, half = peer.shape[1] - 16, peer.shape[2]
    groups, per, enc = nbs[1].shape
    size = 2 * groups * per
    slot = chunk % 2
    turns = chunk == 0
    held = [*crossed, *kept]
    smem = pl.BlockSpec(memory_space=pltpu.SMEM)
    operands = [info, counts, turn, *nbs, *weights, cq, do, peer]
    shapes = [jax.ShapeDtypeStruct((2, tokens, half), BF)] * 2
    shapes += [jax.ShapeDtypeStruct((2, enc // 2, 2 * PAIR), BF)] * 2
    aliases = {len(operands) + i: (i if crossed else 2 + i) for i in range(len(held))}
    if turns:
        shapes.append(jax.ShapeDtypeStruct((enc, size), BF))
    return pl.pallas_call(
        functools.partial(cross_kernel, chunk, slot, int(turns), len(weights)),
        in_specs=[smem, smem] + [ANY] * (len(operands) - 2 + len(held)),
        out_specs=[ANY] * len(shapes),
        out_shape=shapes,
        scratch_shapes=[
            pltpu.VMEM((enc, 2 * PAIR), BF),
            pltpu.VMEM((size, enc), BF),
            pltpu.VMEM((enc, size), BF),
            pltpu.VMEM((size, 2 * PAIR), BF),
            pltpu.VMEM((size, 2 * PAIR), BF),
            pltpu.VMEM((2, tokens, PAIR), BF),
            pltpu.VMEM((2, tokens, PAIR), BF),
            pltpu.VMEM((3, 16, 2 * GROUP), BF),
            pltpu.VMEM((2, 2, tokens, PAIR), BF),
            pltpu.VMEM((2, enc // 2, 2 * PAIR), BF),
            pltpu.VMEM((enc, enc) if turns else (16, 128), BF),
            pltpu.SemaphoreType.DMA((2 * groups + 12,)),
            pltpu.SemaphoreType.DMA((5,)),
        ],
        input_output_aliases=aliases,
        compiler_params=pltpu.CompilerParams(vmem_limit_bytes=VMEM),
        cost_estimate=cost(9),
    )(*operands, *held)


def self_kernel(
    heads, info_ref, q_ref, do_ref, kp_ref, ko_ref, vp_ref, vo_ref, *refs
):
    own_ref, back_ref, out_ref, dq_ref, cross_ref, dk_ref, dv_ref, stat_ref = refs
    first_half = pl.program_id(0) < pl.num_programs(0) // 2
    crossed = jnp.where(first_half, own_ref[0], back_ref[0])
    cross_ref[...] = jnp.where(first_half, own_ref[1], back_ref[1])
    later = info_ref[1] > 0
    tokens = q_ref.shape[0]
    half = tokens // 2
    key_at = lax.broadcasted_iota(jnp.int32, (half, half), 0)
    query_at = lax.broadcasted_iota(jnp.int32, (half, half), 1)
    above = jnp.logical_and(key_at > query_at, later)
    below = key_at <= query_at
    zero = jnp.zeros((half, half), BF)
    lo, hi = slice(0, half), slice(half, None)
    for head in range(heads):
        at = slice(head * HD, (head + 1) * HD)
        queries, grads = q_ref[:, at], do_ref[:, at]
        kp, ko, vp, vo = kp_ref[:, at], ko_ref[:, at], vp_ref[:, at], vo_ref[:, at]
        sp, so = mm(kp, queries, NT), mm(ko, queries, NT)
        gp, go = mm(vp, grads, NT), mm(vo, grads, NT)
        rows = []
        for a in (0, 1):
            if a == 0:
                blocks = (sp[lo, lo], sp[hi, lo], so[lo, lo])
                pgrads = (gp[lo, lo], gp[hi, lo], go[lo, lo])
                middle = jnp.where(later, blocks[1], NEG)
            else:
                blocks = (sp[hi, hi], so[lo, hi], so[hi, hi])
                pgrads = (gp[hi, hi], go[lo, hi], go[hi, hi])
                middle = blocks[1]
            scores = (jnp.where(above, blocks[0], NEG), middle, jnp.where(below, blocks[2], NEG))
            peak = jnp.max(
                jnp.maximum(jnp.maximum(scores[0], scores[1]), scores[2]), axis=0, keepdims=True
            )
            weight = [jnp.exp2((s - peak) * (SCALE * LOG2E)) for s in scores]
            total = jnp.sum(weight[0] + weight[1] + weight[2], axis=0, keepdims=True)
            inverse = 1.0 / total
            probs = [w * inverse for w in weight]
            delta = jnp.sum(
                probs[0] * pgrads[0] + probs[1] * pgrads[1] + probs[2] * pgrads[2],
                axis=0,
                keepdims=True,
            )
            score_grad = [(p * (g - delta)).astype(BF) for p, g in zip(probs, pgrads)]
            rows.append(([p.astype(BF) for p in probs], score_grad))
            lanes = slice(a * half, (a + 1) * half)
            stat_ref[head, 0:1, lanes] = peak * (SCALE * LOG2E) + jnp.log2(total)
            stat_ref[head, 1:2, lanes] = delta

        def spread(which):
            first, second = rows[0][which], rows[1][which]
            before = jnp.concatenate(
                [
                    jnp.concatenate([first[0], zero], 1),
                    jnp.concatenate([first[1], second[0]], 1),
                ],
                0,
            )
            own = jnp.concatenate(
                [
                    jnp.concatenate([first[2], second[1]], 1),
                    jnp.concatenate([zero, second[2]], 1),
                ],
                0,
            )
            return before, own

        (pp, po), (dp, do) = spread(0), spread(1)
        out = mm(pp, vp, TN) + mm(po, vo, TN) + crossed[:, at].astype(F32)
        out_ref[:, at] = out.astype(BF)
        dq_ref[:, at] = ((mm(dp, kp, TN) + mm(do, ko, TN)) * SCALE).astype(BF)
        dk_ref[:, at] = mm(do, queries, NN) * SCALE
        dv_ref[:, at] = mm(po, grads, NN)


def self_part(info, q, do, before, k, v, own, back):
    heads = 2
    tokens, width = q.shape
    steps = width // (heads * HD)
    half = steps // 2
    shape = (tokens, heads * HD)

    def place(p, info):
        return (p + (info[0] & 1) * half) % steps

    spec = pl.BlockSpec(shape, lambda p, info: (0, place(p, info)))
    vp_spec = pl.BlockSpec(shape, lambda p, info: (0, steps + place(p, info)))
    own_spec = pl.BlockSpec((2, *shape), lambda p, info: (0, 0, jnp.minimum(p, half - 1)))
    back_spec = pl.BlockSpec((2, *shape), lambda p, info: (0, 0, jnp.maximum(p - half, 0)))
    stat_spec = pl.BlockSpec((heads, 2, tokens), lambda p, info: (place(p, info), 0, 0))
    full = jax.ShapeDtypeStruct(q.shape, BF)
    wide = jax.ShapeDtypeStruct(q.shape, F32)
    stats = jax.ShapeDtypeStruct((width // HD, 2, tokens), F32)
    return pl.pallas_call(
        functools.partial(self_kernel, heads),
        grid_spec=pltpu.PrefetchScalarGridSpec(
            num_scalar_prefetch=1,
            grid=(steps,),
            in_specs=[spec, spec, spec, spec, vp_spec, spec, own_spec, back_spec],
            out_specs=[spec] * 5 + [stat_spec],
        ),
        out_shape=[full] * 3 + [wide] * 2 + [stats],
        compiler_params=pltpu.CompilerParams(vmem_limit_bytes=VMEM),
        cost_estimate=cost(14),
    )(info, q, do, before, k, before, v, own, back)


def next_kernel(
    heads, q_ref, do_ref, k_ref, v_ref, stat_ref, dkp_ref, dvp_ref, *refs
):
    dk_ref, dv_ref = refs[-2:]
    tokens = q_ref.shape[0]
    half = tokens // 2
    key_at = lax.broadcasted_iota(jnp.int32, (half, half), 0)
    query_at = lax.broadcasted_iota(jnp.int32, (half, half), 1)
    above = key_at > query_at
    zero = jnp.zeros((half, half), BF)
    lo, hi = slice(0, half), slice(half, None)
    for head in range(heads):
        at = slice(head * HD, (head + 1) * HD)
        queries, grads = q_ref[:, at], do_ref[:, at]
        scores = mm(k_ref[:, at], queries, NT)
        prob_grad = mm(v_ref[:, at], grads, NT)
        level, delta = stat_ref[head, 0:1, :], stat_ref[head, 1:2, :]

        def block(rows, lanes, mask):
            exponent = scores[rows, lanes] * (SCALE * LOG2E) - level[:, lanes]
            if mask:
                exponent = jnp.where(above, exponent, NEG)
            probs = jnp.exp2(exponent)
            return probs.astype(BF), (probs * (prob_grad[rows, lanes] - delta[:, lanes])).astype(BF)

        first, middle, last = block(lo, lo, True), block(hi, lo, False), block(hi, hi, True)
        low, score_grad = [
            jnp.concatenate(
                [
                    jnp.concatenate([first[i], zero], 1),
                    jnp.concatenate([middle[i], last[i]], 1),
                ],
                0,
            )
            for i in (0, 1)
        ]
        dk_ref[:, at] = (dkp_ref[:, at] + mm(score_grad, queries, NN) * SCALE).astype(BF)
        dv_ref[:, at] = (dvp_ref[:, at] + mm(low, grads, NN)).astype(BF)


def next_part(part, late, k, v, stats, dk, dv, held):
    heads = 2
    tokens, width = k.shape
    steps = width // (heads * HD) // SPLIT
    shape = (tokens, heads * HD)
    spec = pl.BlockSpec(shape, lambda p: (0, part * steps + p))
    q_spec = pl.BlockSpec(shape, lambda p: (0, p))
    do_spec = pl.BlockSpec(shape, lambda p: (0, steps + p))
    stat_spec = pl.BlockSpec((heads, 2, tokens), lambda p: (part * steps + p, 0, 0))
    full = jax.ShapeDtypeStruct(k.shape, BF)
    return pl.pallas_call(
        functools.partial(next_kernel, heads),
        grid=(steps,),
        in_specs=[q_spec, do_spec, spec, spec, stat_spec, spec, spec] + [ANY] * len(held),
        out_specs=[spec] * 2,
        out_shape=[full] * 2,
        input_output_aliases={7 + i: i for i in range(len(held))},
        compiler_params=pltpu.CompilerParams(vmem_limit_bytes=VMEM),
        cost_estimate=cost(4),
    )(late, late, k, v, stats, dk, dv, *held)


def halving_order(fsdp, seq):
    bits = [("fsdp", 1 << i) for i in range(1, fsdp.bit_length() - 1)]
    seq_bits = [("seq", 1 << i) for i in range(seq.bit_length() - 1)]
    return bits + seq_bits[1:] + seq_bits[:1]


def row_order(fsdp, seq, rows):
    index = np.arange(rows).reshape(seq * fsdp, -1)
    block = np.arange(seq * fsdp)
    keys = []
    for axis, bit in halving_order(fsdp, seq) + [("fsdp", 1)]:
        value = block % fsdp if axis == "fsdp" else block // fsdp
        keys.append((value // bit) % 2)
    order = np.lexsort(keys[::-1])
    return index[order].reshape(-1)


def take_half(value, upper):
    half = value.shape[0] // 2
    return lax.dynamic_slice_in_dim(value, upper * half, half, 0)


def halve_kernel(parts, axis, bit, info_ref, *refs):
    keep_ref, got_ref, mine_ref, other_ref = refs
    half, width = mine_ref.shape
    width //= parts
    upper = (info_ref[0 if axis == "fsdp" else 1] // bit) % 2
    for ref, which in ((mine_ref, upper), (other_ref, 1 - upper)):
        at = pl.ds(pl.multiple_of(which * half, 16), half)
        for part in range(parts):
            total = keep_ref[part, at, :].astype(F32) + got_ref[part, at, :].astype(F32)
            ref[:, part * width : (part + 1) * width] = total.astype(BF)


def halve(info, keep, received, stage):
    axis, bit = stage
    if keep.ndim == 2:
        keep, received = keep[None], received[None]
    parts, rows, width = keep.shape
    shape = (rows // 2, parts * width)
    if shape[0] % 16:
        upper = (info[0 if axis == "fsdp" else 1] // bit) % 2
        total = keep.astype(F32) + received.astype(F32)
        total = total.transpose(1, 0, 2).reshape(rows, parts * width)
        return take_half(total, upper).astype(BF), take_half(total, 1 - upper).astype(BF)
    return pl.pallas_call(
        functools.partial(halve_kernel, parts, axis, bit),
        in_specs=[pl.BlockSpec(memory_space=pltpu.SMEM)]
        + [pl.BlockSpec(memory_space=pltpu.VMEM)] * 2,
        out_shape=[jax.ShapeDtypeStruct(shape, BF)] * 2,
        cost_estimate=cost(1),
    )(info, keep, received)


def on_device(
    self_query, self_key, self_value, cross_query, neighbours, neighbour_count, kv_weight, out_grad
):
    fsdp, seq = lax.axis_size("fsdp"), lax.axis_size("seq")
    shard, slab = lax.axis_index("fsdp"), lax.axis_index("seq")
    q, k, v, cq, do = (x[0] for x in (self_query, self_key, self_value, cross_query, out_grad))
    nb, counts = neighbours[0], neighbour_count[0]
    tokens, width = q.shape
    groups, per, enc = nb.shape
    info = jnp.stack([shard, slab]).astype(jnp.int32)

    last = pack(nb, counts)
    nb_last = shift(last, "seq", 1)

    mine, first, other, pair = cut(after(info, last), counts, kv_weight, cq, do)
    near = swap(other, "fsdp", 1)
    both = stack(mine, near)
    weights = [[mine[0], near]]
    for piece in range(2, fsdp, 2):
        weights[0] += [swap(mine[0], "fsdp", piece), swap(first, "fsdp", piece + 1)]
    for chunk in range(1, CHUNKS):
        weights.append([mine[chunk], near])
        for piece in range(2, fsdp, 2):
            weights[chunk].append(swap(both[chunk - 1], "fsdp", piece))
    nb_peer = swap(after(nb, near), "fsdp", 1)
    peer = swap(pair, "fsdp", 1)
    keyed, = join(k, v, 1)
    nb_last = after(nb_last, both[0], keyed, weights[0][-1], weights[0][-2])
    peer_last = swap(nb_last, "fsdp", 1)
    nbs = [nb_last, nb, peer_last, nb_peer]

    before = shift(after(keyed, nb_last), "seq", 1)

    stages = halving_order(fsdp, seq)
    split_at = fsdp.bit_length() - 2

    turn = jnp.asarray(np.eye(enc)[row_order(fsdp, seq, enc)], BF)
    crossed, pairs = [], []
    for chunk in range(0, CHUNKS, 2):
        kept = []
        for c in (chunk, chunk + 1):
            results = cross(c, info, counts, turn, nbs, weights[c], cq, do, peer, crossed, kept)
            crossed, kept = results[:2], results[2:4]
            if not c:
                turn = results[4]
        keep, send = kept
        received = swap(send, *stages[0])
        for stage in range(1, split_at):
            keep, send = halve(info, keep, received, stages[stage])
            received = swap(send, *stages[stage])
        pairs.append((keep, received))
    own, away = crossed
    back = swap(away, "fsdp", 1)

    asked = join(q, do, SPLIT)
    late = [shift(after(x, pairs[0][0]), "seq", -1) for x in asked]

    halves = [halve(info, *pairs[0], stages[split_at])]
    block_out, query_grad, cross_grad, dk, dv, stats = self_part(
        after(info, halves[0][1]), q, do, before, k, v, own, back
    )
    halves.append(halve(after(info, stats), *pairs[1], stages[split_at]))
    stats_after = shift(stats, "seq", -1)

    done = []
    for keep, send in halves:
        received = swap(send, *stages[split_at])
        for stage in range(split_at + 1, len(stages)):
            keep, send = halve(after(info, stats), keep, received, stages[stage])
            received = swap(send, *stages[stage])
        total = keep.astype(F32) + received.astype(F32)
        core = shard % 2
        away = swap(take_half(total, 1 - core).astype(BF), "fsdp", 1)
        done.append((take_half(total, core), away.astype(F32)))
    columns = [
        jnp.concatenate(
            [
                group[side][:, (2 * c + part) * PAIR : (2 * c + part + 1) * PAIR]
                for group in done
                for c in range(CHUNKS // SPLIT)
            ],
            -1,
        )
        for part in (0, 1)
        for side in (0, 1)
    ]
    key_mine, key_away, value_mine, value_away = columns
    low = shard % 2 == 0
    weight_grad = jnp.concatenate(
        [
            jnp.where(low, key_mine, key_away),
            jnp.where(low, key_away, key_mine),
            jnp.where(low, value_mine, value_away),
            jnp.where(low, value_away, value_mine),
        ],
        -1,
    )

    held = []
    for part in range(SPLIT):
        held = next_part(part, late[part], k, v, stats_after, dk, dv, held)
    key_grad, value_grad = held
    return (
        block_out[None],
        query_grad[None],
        key_grad[None],
        value_grad[None],
        cross_grad[None],
        weight_grad,
    )


def solution(mesh):
    in_specs = (
        P("fsdp", "seq", None),
        P("fsdp", "seq", None),
        P("fsdp", "seq", None),
        P("fsdp", "seq", None),
        P("fsdp", "seq", None, None),
        P("fsdp", "seq"),
        P("fsdp", None),
        P("fsdp", "seq", None),
    )
    out_specs = (
        P("fsdp", "seq", None),
        P("fsdp", "seq", None),
        P("fsdp", "seq", None),
        P("fsdp", "seq", None),
        P("fsdp", "seq", None),
        P(("seq", "fsdp"), None),
    )
    return jax.shard_map(
        on_device, mesh=mesh, in_specs=in_specs, out_specs=out_specs, check_vma=False
    )
```

```python
import functools

import numpy as np
import jax
import jax.numpy as jnp
from jax import lax
from jax.experimental import pallas as pl
from jax.experimental.pallas import tpu as pltpu
from jax.sharding import PartitionSpec as P

HEADS = 16
HD = 128
GROUP = 64
RLEN = 128
PAIR = 2 * HD
CHUNKS = HEADS // 4
TOGETHER = 2
VMEM = 60 * 2**20
SCALE = HD ** (-0.5)
LOG2E = 1.4426950408889634
NEG = -1e30
BF = jnp.bfloat16
F32 = jnp.float32
ANY = pl.BlockSpec(memory_space=pl.ANY)

NT = (((1,), (1,)), ((), ()))
TN = (((0,), (0,)), ((), ()))
NN = (((1,), (0,)), ((), ()))


def cost(micros):
    return pl.CostEstimate(flops=int(micros * 1e9), bytes_accessed=1000, transcendentals=0)


def mm(a, b, dims):
    return lax.dot_general(a, b, dims, preferred_element_type=F32)


def shift(value, axis, steps):
    count = lax.axis_size(axis)
    first, last = max(0, -steps), min(count, count - steps)
    return lax.ppermute(value, axis, [(i, i + steps) for i in range(first, last)])


def after(value, *others):
    return lax.optimization_barrier((value, *others))[0]


def swap(value, axis, bit):
    return lax.ppermute(value, axis, [(i, i ^ bit) for i in range(lax.axis_size(axis))])


def count_rows(count_ref, width):
    row = lax.broadcasted_iota(jnp.int32, (16, width), 0)
    tail = jnp.zeros((16, width), F32)
    for u in range(count_ref.shape[0]):
        tail = jnp.where(row == u, count_ref[u].astype(F32), tail)
    return tail.astype(BF)


def pack_kernel(count_ref, nb_ref, out_ref):
    per, enc = nb_ref.shape[1:]
    out_ref[:per, :] = nb_ref[0]
    out_ref[per:, :] = count_rows(count_ref, enc)


def pack(nb, counts):
    groups, per, enc = nb.shape
    return pl.pallas_call(
        pack_kernel,
        grid=(1,),
        in_specs=[
            pl.BlockSpec(memory_space=pltpu.SMEM),
            pl.BlockSpec((1, per, enc), lambda p: (groups - 1, 0, 0)),
        ],
        out_specs=pl.BlockSpec((per + 16, enc), lambda p: (0, 0)),
        out_shape=jax.ShapeDtypeStruct((per + 16, enc), BF),
        compiler_params=pltpu.CompilerParams(vmem_limit_bytes=VMEM),
        cost_estimate=cost(2),
    )(counts, nb)


def cut_kernel(info_ref, count_ref, *refs):
    sources, parts, other_ref, pair_ref = refs[:6], refs[6:-2], refs[-2], refs[-1]
    for which in (0, 1):
        keys, values = sources[2 * which : 2 * which + 2]
        for chunk in range(CHUNKS):
            at = slice(chunk * PAIR, (chunk + 1) * PAIR)
            ref = other_ref if which else parts[chunk // TOGETHER]
            where = chunk if which else chunk % TOGETHER
            ref[where, :, :PAIR] = keys[:, at]
            ref[where, :, PAIR:] = values[:, at]
    tokens, width = sources[4].shape
    for index in (0, 1):
        pair_ref[index, :tokens, :] = sources[4 + index][...]
        pair_ref[index, tokens:, :] = count_rows(count_ref, width)


def cut(info, counts, weight, cq, do):
    rows = weight.shape[0]
    tokens, width = cq.shape
    count = CHUNKS // TOGETHER
    part = jax.ShapeDtypeStruct((TOGETHER, rows, 2 * PAIR), BF)
    parts = jax.ShapeDtypeStruct((CHUNKS, rows, 2 * PAIR), BF)
    half = jax.ShapeDtypeStruct((2, tokens + 16, width // 2), BF)

    def columns(height, other, value):
        return pl.BlockSpec(
            (height, width // 2), lambda p, info: (0, 2 * value + ((info[0] & 1) ^ other))
        )

    *mine, other, pair = pl.pallas_call(
        cut_kernel,
        grid_spec=pltpu.PrefetchScalarGridSpec(
            num_scalar_prefetch=1,
            grid=(1,),
            in_specs=[pl.BlockSpec(memory_space=pltpu.SMEM)]
            + [columns(rows, other, value) for other in (0, 1) for value in (0, 1)]
            + [columns(tokens, 1, 0)] * 2,
            out_specs=[
                pl.BlockSpec(x.shape, lambda p, info: (0, 0, 0))
                for x in [part] * count + [parts, half]
            ],
        ),
        out_shape=[part] * count + [parts, half],
        compiler_params=pltpu.CompilerParams(vmem_limit_bytes=VMEM),
        cost_estimate=cost(3),
    )(info, counts, weight, weight, weight, weight, cq, do)
    return mine, other, pair


def stack_kernel(*refs):
    count = CHUNKS // TOGETHER
    mine, near_ref, outs = refs[:count], refs[count], refs[count + 1 :]
    rows = near_ref.shape[1]
    for group, (ref, out) in enumerate(zip(mine, outs)):
        out[:, :rows, :] = ref[...]
        out[:, rows:, :] = near_ref[group * TOGETHER : (group + 1) * TOGETHER]


def stack(mine, near):
    together, rows, width = mine[0].shape
    return pl.pallas_call(
        stack_kernel,
        out_shape=[jax.ShapeDtypeStruct((together, 2 * rows, width), BF)] * len(mine),
        compiler_params=pltpu.CompilerParams(vmem_limit_bytes=VMEM),
        cost_estimate=cost(2),
    )(*mine, near)


def cross_kernel(group, turns, pieces, held, info_ref, count_ref, *refs):
    (turn_ref, nb_last, nb_own, peer_last, nb_peer), refs = refs[:5], refs[5:]
    weights, refs = refs[:pieces], refs[pieces:]
    (cq_ref, do_ref, peer_ref), refs = refs[:3], refs[3 + held :]
    token_outs, (keep_out, send_out), refs = refs[:4], refs[4:6], refs[6:]
    turned_out, refs = (refs[0], refs[1:]) if turns else (None, refs)
    (w_ref, nb_ref, turned_ref, kv_ref, dkv_ref, q_ref, g_ref, tail_ref), refs = refs[:8], refs[8:]
    out_ref, dw_ref, pick_ref, sem, out_sem = refs
    shard = info_ref[0]
    enc = nb_ref.shape[1]
    tokens = q_ref.shape[1]
    groups = tokens // GROUP
    per = 2 * RLEN
    size = groups * per
    rows = weights[0].shape[1]
    wide = TOGETHER * PAIR
    loads, stores = [], []

    def load(source, target):
        copy = pltpu.make_async_copy(source, target, sem.at[len(loads)])
        copy.start()
        loads.append(copy)
        return copy

    def store(source, target):
        copy = pltpu.make_async_copy(source, target, out_sem.at[len(stores)])
        copy.start()
        stores.append(copy)

    def load_weight(index):
        sources = [weights[0].at[index], weights[1].at[group * TOGETHER + index]]
        for ref in weights[2:]:
            sources += [ref.at[index, :rows, :], ref.at[index, rows:, :]]
        waits = []
        for piece, source in enumerate(sources):
            at = pl.ds(pl.multiple_of((shard ^ piece) * rows, 16), rows)
            waits.append(load(source, w_ref.at[index, at, :]))
        return waits

    waits_w = [load_weight(0)]
    waits_nb = [
        load(nb_last.at[:per, :], nb_ref.at[:per, :]),
        *[load(nb_own.at[u - 1], nb_ref.at[u * per : (u + 1) * per, :]) for u in range(1, groups)],
        load(peer_last.at[:per, :], nb_ref.at[size : size + per, :]),
        *[
            load(nb_peer.at[u - 1], nb_ref.at[size + u * per : size + (u + 1) * per, :])
            for u in range(1, groups)
        ],
    ]
    lanes = pl.ds(pl.multiple_of(((shard & 1) * CHUNKS + group * TOGETHER) * PAIR, PAIR), wide)
    there = slice(group * wide, (group + 1) * wide)
    waits_q = [
        load(cq_ref.at[:, lanes], q_ref.at[0]),
        load(do_ref.at[:, lanes], g_ref.at[0]),
        load(peer_ref.at[0, :tokens, there], q_ref.at[1]),
        load(peer_ref.at[1, :tokens, there], g_ref.at[1]),
        load(nb_last.at[per:, : 2 * GROUP], tail_ref.at[0]),
        load(peer_last.at[per:, : 2 * GROUP], tail_ref.at[1]),
        load(peer_ref.at[0, tokens:, : 2 * GROUP], tail_ref.at[2]),
    ]
    wait_turn = load(turn_ref, pick_ref if turns else turned_ref)
    for index in range(1, TOGETHER):
        waits_w.append(load_weight(index))

    def project(index):
        for copy in waits_w[index]:
            copy.wait()
        for file in (0, 1):
            for start, stop in ((0, 1), (1, groups)):
                if index == 0:
                    for copy in waits_nb[file * groups + start : file * groups + stop]:
                        copy.wait()
                at = slice(file * size + start * per, file * size + stop * per)
                kv_ref[index, at, :] = mm(nb_ref[at, :], w_ref[index], NN).astype(BF)

    zero = jnp.zeros((GROUP, HD), BF)

    def diagonal(block):
        return jnp.concatenate(
            [
                jnp.concatenate([block[:, :HD], zero], 1),
                jnp.concatenate([zero, block[:, HD:]], 1),
            ],
            0,
        )

    row = lax.broadcasted_iota(jnp.int32, (per, 2 * GROUP), 0).astype(F32)

    def attend(index, file, u):
        if u == 0:
            count = tail_ref[file, groups - 1 : groups, :].astype(F32)
        elif file:
            count = tail_ref[2, u - 1 : u, :].astype(F32)
        else:
            count = count_ref[u - 1].astype(F32)
        unit = file * groups + u
        at = slice(unit * per, (unit + 1) * per)
        tok = slice(u * GROUP, (u + 1) * GROUP)
        cols = slice(index * PAIR, (index + 1) * PAIR)
        keys, values = kv_ref[index, at, :PAIR], kv_ref[index, at, PAIR:]
        queries, grads = diagonal(q_ref[file, tok, cols]), diagonal(g_ref[file, tok, cols])
        scores = mm(keys, queries, NT)
        prob_grad = mm(values, grads, NT)
        scores = jnp.where(row < count * RLEN, scores, NEG)
        peak = jnp.max(scores, axis=0, keepdims=True)
        weight = jnp.exp2((scores - peak) * (SCALE * LOG2E))
        total = jnp.sum(weight, axis=0, keepdims=True)
        inverse = jnp.where(count > 0, 1.0 / total, 0.0)
        probs = weight * inverse
        delta = jnp.sum(probs * prob_grad, axis=0, keepdims=True)
        score_grad = (probs * (prob_grad - delta)).astype(BF)
        low = probs.astype(BF)
        out = mm(low, values, TN).astype(BF)
        dq = (mm(score_grad, keys, TN) * SCALE).astype(BF)
        for which, value in enumerate((out, dq)):
            out_ref[file, which, tok, index * PAIR : index * PAIR + HD] = value[:GROUP, :HD]
            out_ref[file, which, tok, index * PAIR + HD : (index + 1) * PAIR] = value[GROUP:, HD:]
        dkv_ref[index, at, :PAIR] = (mm(score_grad, queries, NN) * SCALE).astype(BF)
        dkv_ref[index, at, PAIR:] = mm(low, grads, NN).astype(BF)

    half = enc // 2
    bit = (shard // 2) % 2

    def weigh(index, targets):
        for slot, target, which in targets:
            at = pl.ds(pl.multiple_of(which * half, 16), half)
            dw_ref[slot, index] = mm(turned_ref[at, :], dkv_ref[index], NN).astype(BF)
            store(dw_ref.at[slot, index], target.at[index])

    both = ((0, send_out, 1 - bit), (1, keep_out, bit))
    project(0)
    for copy in waits_q:
        copy.wait()
    for index in range(TOGETHER):
        for file in (0, 1):
            for u in range(groups):
                attend(index, file, u)
        if index + 1 < TOGETHER:
            project(index + 1)
        if index == 0:
            wait_turn.wait()
            if turns:
                turned_ref[...] = mm(pick_ref[...], nb_ref[...], NT).astype(BF)
                store(turned_ref, turned_out)
        if index + 1 == TOGETHER:
            for which, target in enumerate(token_outs):
                store(out_ref.at[which // 2, which % 2], target.at[:, there])
        weigh(index, both)
    for copy in stores:
        copy.wait()


def cross(group, info, counts, turn, nbs, weights, cq, do, peer, held):
    tokens, half = peer.shape[1] - 16, peer.shape[2]
    groups, per, enc = nbs[1].shape
    size = 2 * groups * per
    turns = group == 0
    smem = pl.BlockSpec(memory_space=pltpu.SMEM)
    operands = [info, counts, turn, *nbs, *weights, cq, do, peer]
    shapes = [jax.ShapeDtypeStruct((tokens, half), BF)] * 4
    shapes += [jax.ShapeDtypeStruct((TOGETHER, enc // 2, 2 * PAIR), BF)] * 2
    if turns:
        shapes.append(jax.ShapeDtypeStruct((enc, size), BF))
    return pl.pallas_call(
        functools.partial(cross_kernel, group, turns, len(weights), len(held)),
        in_specs=[smem, smem] + [ANY] * (len(operands) - 2 + len(held)),
        out_specs=[ANY] * len(shapes),
        out_shape=shapes,
        scratch_shapes=[
            pltpu.VMEM((TOGETHER, enc, 2 * PAIR), BF),
            pltpu.VMEM((size, enc), BF),
            pltpu.VMEM((enc, size), BF),
            pltpu.VMEM((TOGETHER, size, 2 * PAIR), BF),
            pltpu.VMEM((TOGETHER, size, 2 * PAIR), BF),
            pltpu.VMEM((2, tokens, TOGETHER * PAIR), BF),
            pltpu.VMEM((2, tokens, TOGETHER * PAIR), BF),
            pltpu.VMEM((3, 16, 2 * GROUP), BF),
            pltpu.VMEM((2, 2, tokens, TOGETHER * PAIR), BF),
            pltpu.VMEM((2, TOGETHER, enc // 2, 2 * PAIR), BF),
            pltpu.VMEM((enc, enc) if turns else (16, 128), BF),
            pltpu.SemaphoreType.DMA((2 * groups + 8 + TOGETHER * 2 * len(weights),)),
            pltpu.SemaphoreType.DMA((5 + 2 * TOGETHER,)),
        ],
        input_output_aliases={len(operands) + i: i for i in range(len(held))},
        compiler_params=pltpu.CompilerParams(vmem_limit_bytes=VMEM),
        cost_estimate=cost(9),
    )(*operands, *held)


def self_kernel(
    heads, info_ref, q_ref, do_ref, ko_ref, vo_ref, one_ref, two_ref, three_ref, *refs
):
    own_ref, own_grad, back_ref, back_grad, *refs = refs
    out_ref, dq_ref, cross_ref, dk_ref, dv_ref, stat_ref = refs
    first_half = pl.program_id(0) < pl.num_programs(0) // 2
    crossed = jnp.where(first_half, own_ref[...], back_ref[...])
    cross_ref[...] = jnp.where(first_half, own_grad[...], back_grad[...])
    odd = info_ref[1] % 2 == 1
    keys_before = jnp.where(odd, one_ref[...], two_ref[...])
    values_before = jnp.where(odd, two_ref[...], three_ref[...])
    later = info_ref[1] > 0
    tokens = q_ref.shape[0]
    half = tokens // 2
    key_at = lax.broadcasted_iota(jnp.int32, (half, half), 0)
    query_at = lax.broadcasted_iota(jnp.int32, (half, half), 1)
    above = jnp.logical_and(key_at > query_at, later)
    below = key_at <= query_at
    zero = jnp.zeros((half, half), BF)
    lo, hi = slice(0, half), slice(half, None)
    for head in range(heads):
        at = slice(head * HD, (head + 1) * HD)
        queries, grads = q_ref[:, at], do_ref[:, at]
        kp, vp = keys_before[:, at], values_before[:, at]
        ko, vo = ko_ref[:, at], vo_ref[:, at]
        sp, so = mm(kp, queries, NT), mm(ko, queries, NT)
        gp, go = mm(vp, grads, NT), mm(vo, grads, NT)
        rows = []
        for a in (0, 1):
            if a == 0:
                blocks = (sp[lo, lo], sp[hi, lo], so[lo, lo])
                pgrads = (gp[lo, lo], gp[hi, lo], go[lo, lo])
                middle = jnp.where(later, blocks[1], NEG)
            else:
                blocks = (sp[hi, hi], so[lo, hi], so[hi, hi])
                pgrads = (gp[hi, hi], go[lo, hi], go[hi, hi])
                middle = blocks[1]
            scores = (jnp.where(above, blocks[0], NEG), middle, jnp.where(below, blocks[2], NEG))
            peak = jnp.max(
                jnp.maximum(jnp.maximum(scores[0], scores[1]), scores[2]), axis=0, keepdims=True
            )
            weight = [jnp.exp2((s - peak) * (SCALE * LOG2E)) for s in scores]
            total = jnp.sum(weight[0] + weight[1] + weight[2], axis=0, keepdims=True)
            inverse = 1.0 / total
            probs = [w * inverse for w in weight]
            delta = jnp.sum(
                probs[0] * pgrads[0] + probs[1] * pgrads[1] + probs[2] * pgrads[2],
                axis=0,
                keepdims=True,
            )
            score_grad = [(p * (g - delta)).astype(BF) for p, g in zip(probs, pgrads)]
            rows.append(([p.astype(BF) for p in probs], score_grad))
            lanes = slice(a * half, (a + 1) * half)
            stat_ref[head, 0:1, lanes] = peak * (SCALE * LOG2E) + jnp.log2(total)
            stat_ref[head, 1:2, lanes] = delta

        def spread(which):
            first, second = rows[0][which], rows[1][which]
            before = jnp.concatenate(
                [
                    jnp.concatenate([first[0], zero], 1),
                    jnp.concatenate([first[1], second[0]], 1),
                ],
                0,
            )
            own = jnp.concatenate(
                [
                    jnp.concatenate([first[2], second[1]], 1),
                    jnp.concatenate([zero, second[2]], 1),
                ],
                0,
            )
            return before, own

        (pp, po), (dp, do) = spread(0), spread(1)
        out = mm(pp, vp, TN) + mm(po, vo, TN) + crossed[:, at].astype(F32)
        out_ref[:, at] = out.astype(BF)
        dq_ref[:, at] = ((mm(dp, kp, TN) + mm(do, ko, TN)) * SCALE).astype(BF)
        dk_ref[:, at] = mm(do, queries, NN) * SCALE
        dv_ref[:, at] = mm(po, grads, NN)


def self_part(info, q, do, k, v, one, two, three, own, back):
    heads = 2
    tokens, width = q.shape
    steps = width // (heads * HD)
    half = steps // 2
    shape = (tokens, heads * HD)

    def place(p, info):
        return (p + (info[0] & 1) * half) % steps

    spec = pl.BlockSpec(shape, lambda p, info: (0, place(p, info)))
    own_spec = pl.BlockSpec(shape, lambda p, info: (0, jnp.minimum(p, half - 1)))
    back_spec = pl.BlockSpec(shape, lambda p, info: (0, jnp.maximum(p - half, 0)))
    stat_spec = pl.BlockSpec((heads, 2, tokens), lambda p, info: (place(p, info), 0, 0))
    full = jax.ShapeDtypeStruct(q.shape, BF)
    wide = jax.ShapeDtypeStruct(q.shape, F32)
    stats = jax.ShapeDtypeStruct((width // HD, 2, tokens), F32)
    return pl.pallas_call(
        functools.partial(self_kernel, heads),
        grid_spec=pltpu.PrefetchScalarGridSpec(
            num_scalar_prefetch=1,
            grid=(steps,),
            in_specs=[spec] * 7 + [own_spec] * 2 + [back_spec] * 2,
            out_specs=[spec] * 5 + [stat_spec],
        ),
        out_shape=[full] * 3 + [wide] * 2 + [stats],
        compiler_params=pltpu.CompilerParams(vmem_limit_bytes=VMEM),
        cost_estimate=cost(14),
    )(info, q, do, k, v, one, two, three, *own, *back)


def next_kernel(
    heads, info_ref, one_ref, three_ref, do_ref, k_ref, v_ref, stat_ref, dkp_ref, dvp_ref,
    dk_ref, dv_ref,
):
    all_queries = jnp.where(info_ref[1] % 2 == 1, three_ref[...], one_ref[...])
    tokens = do_ref.shape[0]
    half = tokens // 2
    key_at = lax.broadcasted_iota(jnp.int32, (half, half), 0)
    query_at = lax.broadcasted_iota(jnp.int32, (half, half), 1)
    above = key_at > query_at
    zero = jnp.zeros((half, half), BF)
    lo, hi = slice(0, half), slice(half, None)
    for head in range(heads):
        at = slice(head * HD, (head + 1) * HD)
        queries, grads = all_queries[:, at], do_ref[:, at]
        scores = mm(k_ref[:, at], queries, NT)
        prob_grad = mm(v_ref[:, at], grads, NT)
        level, delta = stat_ref[head, 0:1, :], stat_ref[head, 1:2, :]

        def block(rows, lanes, mask):
            exponent = scores[rows, lanes] * (SCALE * LOG2E) - level[:, lanes]
            if mask:
                exponent = jnp.where(above, exponent, NEG)
            probs = jnp.exp2(exponent)
            return probs.astype(BF), (probs * (prob_grad[rows, lanes] - delta[:, lanes])).astype(BF)

        first, middle, last = block(lo, lo, True), block(hi, lo, False), block(hi, hi, True)
        low, score_grad = [
            jnp.concatenate(
                [
                    jnp.concatenate([first[i], zero], 1),
                    jnp.concatenate([middle[i], last[i]], 1),
                ],
                0,
            )
            for i in (0, 1)
        ]
        dk_ref[:, at] = (dkp_ref[:, at] + mm(score_grad, queries, NN) * SCALE).astype(BF)
        dv_ref[:, at] = (dvp_ref[:, at] + mm(low, grads, NN)).astype(BF)


def next_part(info, one, three, do, k, v, stats, dk, dv):
    heads = 2
    tokens, width = k.shape
    spec = pl.BlockSpec((tokens, heads * HD), lambda p: (0, p))
    stat_spec = pl.BlockSpec((heads, 2, tokens), lambda p: (p, 0, 0))
    full = jax.ShapeDtypeStruct(k.shape, BF)
    return pl.pallas_call(
        functools.partial(next_kernel, heads),
        grid=(width // (heads * HD),),
        in_specs=[pl.BlockSpec(memory_space=pltpu.SMEM)]
        + [spec] * 5
        + [stat_spec]
        + [spec] * 2,
        out_specs=[spec] * 2,
        out_shape=[full] * 2,
        compiler_params=pltpu.CompilerParams(vmem_limit_bytes=VMEM),
        cost_estimate=cost(8),
    )(info, one, three, do, k, v, stats, dk, dv)


def halving_order(fsdp, seq):
    bits = [("fsdp", 1 << i) for i in range(1, fsdp.bit_length() - 1)]
    seq_bits = [("seq", 1 << i) for i in range(seq.bit_length() - 1)]
    return bits + seq_bits[1:] + seq_bits[:1]


def row_order(fsdp, seq, rows):
    index = np.arange(rows).reshape(seq * fsdp, -1)
    block = np.arange(seq * fsdp)
    keys = []
    for axis, bit in halving_order(fsdp, seq) + [("fsdp", 1)]:
        value = block % fsdp if axis == "fsdp" else block // fsdp
        keys.append((value // bit) % 2)
    order = np.lexsort(keys[::-1])
    return index[order].reshape(-1)


def take_half(value, upper):
    half = value.shape[0] // 2
    return lax.dynamic_slice_in_dim(value, upper * half, half, 0)


def halve_kernel(spans, axis, bit, info_ref, *refs):
    sources, (mine_ref, other_ref) = refs[:-2], refs[-2:]
    count = len(sources) // 2
    half = mine_ref.shape[0]
    upper = (info_ref[0 if axis == "fsdp" else 1] // bit) % 2
    for ref, which in ((mine_ref, upper), (other_ref, 1 - upper)):
        at = pl.ds(pl.multiple_of(which * half, 16), half)
        start = 0
        for keep, got, parts in zip(sources[:count], sources[count:], spans):
            width = keep.shape[-1]
            for part in range(parts):
                where = (part, at) if len(keep.shape) == 3 else (at,)
                total = keep[where].astype(F32) + got[where].astype(F32)
                ref[:, start : start + width] = total.astype(BF)
                start += width


def halve(info, keeps, received, stage):
    axis, bit = stage
    spans = [x.shape[0] if x.ndim == 3 else 1 for x in keeps]
    rows = keeps[0].shape[-2]
    width = sum(parts * x.shape[-1] for parts, x in zip(spans, keeps))
    if rows // 2 % 16:
        upper = (info[0 if axis == "fsdp" else 1] // bit) % 2
        sums = [
            (x.astype(F32) + y.astype(F32)).reshape(-1, rows, x.shape[-1])
            for x, y in zip(keeps, received)
        ]
        total = jnp.concatenate([part for x in sums for part in x], -1)
        return take_half(total, upper).astype(BF), take_half(total, 1 - upper).astype(BF)
    return pl.pallas_call(
        functools.partial(halve_kernel, spans, axis, bit),
        in_specs=[pl.BlockSpec(memory_space=pltpu.SMEM)]
        + [pl.BlockSpec(memory_space=pltpu.VMEM)] * (2 * len(keeps)),
        out_shape=[jax.ShapeDtypeStruct((rows // 2, width), BF)] * 2,
        compiler_params=pltpu.CompilerParams(vmem_limit_bytes=VMEM),
        cost_estimate=cost(1),
    )(info, *keeps, *received)


def on_device(
    self_query, self_key, self_value, cross_query, neighbours, neighbour_count, kv_weight, out_grad
):
    fsdp, seq = lax.axis_size("fsdp"), lax.axis_size("seq")
    shard, slab = lax.axis_index("fsdp"), lax.axis_index("seq")
    q, k, v, cq, do = (x[0] for x in (self_query, self_key, self_value, cross_query, out_grad))
    nb, counts = neighbours[0], neighbour_count[0]
    tokens, width = q.shape
    groups, per, enc = nb.shape
    info = jnp.stack([shard, slab]).astype(jnp.int32)

    last = pack(nb, counts)
    nb_last = shift(last, "seq", 1)

    nb_peer = swap(nb, "fsdp", 1)
    mine, other, pair = cut(after(info, last, nb_peer), counts, kv_weight, cq, do)
    near = swap(other, "fsdp", 1)
    weights = [
        [here, near, *[swap(x, "fsdp", piece) for piece in range(2, fsdp, 2)]]
        for here, x in zip(mine, stack(mine, near))
    ]
    peer = swap(pair, "fsdp", 1)

    even = slab % 2 == 0

    def pick(when_even, when_odd, *others):
        return jnp.where(after(even, nb_last, *others), when_even, when_odd)

    def hop(value):
        odds = [(i, i + 2) for i in range(1, seq - 2, 2)]
        return lax.ppermute(value, "seq", odds + [(i, i - 2) for i in range(2, seq, 2)])

    far_one = hop(pick(q, k))
    one = swap(pick(k, q), "seq", 1)

    nb_last = after(nb_last, peer)
    peer_last = swap(nb_last, "fsdp", 1)
    nbs = [nb_last, nb, peer_last, nb_peer]

    stages = halving_order(fsdp, seq)
    split_at = fsdp.bit_length() - 2

    turn = jnp.asarray(np.eye(enc)[row_order(fsdp, seq, enc)], BF)
    held, pairs = [], []
    for group in range(CHUNKS // TOGETHER):
        results = cross(group, info, counts, turn, nbs, weights[group], cq, do, peer, held)
        held, (keep, send) = results[:4], results[4:6]
        if not group:
            turn = results[6]
            two = swap(pick(v, far_one, turn), "seq", 1)
            far_two = hop(pick(do, v, turn))
        received = swap(send, *stages[0])
        for stage in range(1, split_at):
            keep, send = halve(info, [keep], [received], stages[stage])
            received = swap(send, *stages[stage])
        pairs.append((keep, received))
    own = held[:2]
    back = [swap(x, "fsdp", 1) for x in after(held[2:], pairs[0][1], one, two, far_two)]
    third = pick(far_one, far_two, pairs[-1][0])
    three = swap(third, "seq", 1)

    halves = [halve(info, [pairs[0][0]], [pairs[0][1]], stages[split_at])]
    got = [swap(halves[0][1], *stages[split_at])]
    halves.append(
        halve(after(info, halves[0][1], *back), [pairs[1][0]], [pairs[1][1]], stages[split_at])
    )
    got.append(swap(halves[1][1], *stages[split_at]))
    four = swap(pick(far_two, do, halves[1][1], third), "seq", 1)
    keeps = [keep for keep, _ in halves]
    keep, send = halve(after(info, three), keeps, got, stages[split_at + 1])
    keeps, got = [keep], [swap(send, *stages[split_at + 1])]
    block_out, query_grad, cross_grad, dk, dv, stats = self_part(
        after(info, send), q, do, k, v, one, two, three, own, back
    )
    stats_after = shift(stats, "seq", -1)
    key_grad, value_grad = next_part(info, one, three, four, k, v, stats_after, dk, dv)

    for stage in range(split_at + 2, len(stages)):
        keep, send = halve(after(info, stats), keeps, got, stages[stage])
        keeps, got = [keep], [swap(send, *stages[stage])]
    total = keeps[0].astype(F32) + got[0].astype(F32)
    core = shard % 2
    away = swap(take_half(total, 1 - core).astype(BF), "fsdp", 1).astype(F32)
    nearby = take_half(total, core)
    key_mine, key_away, value_mine, value_away = [
        jnp.concatenate(
            [x[:, (2 * c + part) * PAIR : (2 * c + part + 1) * PAIR] for c in range(CHUNKS)], -1
        )
        for part in (0, 1)
        for x in (nearby, away)
    ]
    low = shard % 2 == 0
    weight_grad = jnp.concatenate(
        [
            jnp.where(low, key_mine, key_away),
            jnp.where(low, key_away, key_mine),
            jnp.where(low, value_mine, value_away),
            jnp.where(low, value_away, value_mine),
        ],
        -1,
    )

    return (
        block_out[None],
        query_grad[None],
        key_grad[None],
        value_grad[None],
        cross_grad[None],
        weight_grad,
    )


def solution(mesh):
    in_specs = (
        P("fsdp", "seq", None),
        P("fsdp", "seq", None),
        P("fsdp", "seq", None),
        P("fsdp", "seq", None),
        P("fsdp", "seq", None, None),
        P("fsdp", "seq"),
        P("fsdp", None),
        P("fsdp", "seq", None),
    )
    out_specs = (
        P("fsdp", "seq", None),
        P("fsdp", "seq", None),
        P("fsdp", "seq", None),
        P("fsdp", "seq", None),
        P("fsdp", "seq", None),
        P(("seq", "fsdp"), None),
    )
    return jax.shard_map(
        on_device, mesh=mesh, in_specs=in_specs, out_specs=out_specs, check_vma=False
    )
```

```python
import functools

import numpy as np
import jax
import jax.numpy as jnp
from jax import lax
from jax.experimental import pallas as pl
from jax.experimental.pallas import tpu as pltpu
from jax.sharding import PartitionSpec as P

HEADS = 16
HD = 128
GROUP = 64
RLEN = 128
PAIR = 2 * HD
CHUNKS = HEADS // 4
TOGETHER = 2
VMEM = 60 * 2**20
SCALE = HD ** (-0.5)
LOG2E = 1.4426950408889634
NEG = -1e30
BF = jnp.bfloat16
F32 = jnp.float32
ANY = pl.BlockSpec(memory_space=pl.ANY)

NT = (((1,), (1,)), ((), ()))
TN = (((0,), (0,)), ((), ()))
NN = (((1,), (0,)), ((), ()))


def cost(micros):
    return pl.CostEstimate(flops=int(micros * 1e9), bytes_accessed=1000, transcendentals=0)


def mm(a, b, dims):
    return lax.dot_general(a, b, dims, preferred_element_type=F32)


def shift(value, axis, steps):
    count = lax.axis_size(axis)
    first, last = max(0, -steps), min(count, count - steps)
    return lax.ppermute(value, axis, [(i, i + steps) for i in range(first, last)])


def after(value, *others):
    return lax.optimization_barrier((value, *others))[0]


def swap(value, axis, bit):
    return lax.ppermute(value, axis, [(i, i ^ bit) for i in range(lax.axis_size(axis))])


def count_rows(count_ref, width):
    row = lax.broadcasted_iota(jnp.int32, (16, width), 0)
    tail = jnp.zeros((16, width), F32)
    for u in range(count_ref.shape[0]):
        tail = jnp.where(row == u, count_ref[u].astype(F32), tail)
    return tail.astype(BF)


def pack_kernel(count_ref, nb_ref, out_ref):
    per, enc = nb_ref.shape[1:]
    out_ref[:per, :] = nb_ref[0]
    out_ref[per:, :] = count_rows(count_ref, enc)


def pack(nb, counts):
    groups, per, enc = nb.shape
    return pl.pallas_call(
        pack_kernel,
        grid=(1,),
        in_specs=[
            pl.BlockSpec(memory_space=pltpu.SMEM),
            pl.BlockSpec((1, per, enc), lambda p: (groups - 1, 0, 0)),
        ],
        out_specs=pl.BlockSpec((per + 16, enc), lambda p: (0, 0)),
        out_shape=jax.ShapeDtypeStruct((per + 16, enc), BF),
        compiler_params=pltpu.CompilerParams(vmem_limit_bytes=VMEM),
        cost_estimate=cost(2),
    )(counts, nb)


def cut_kernel(info_ref, count_ref, *refs):
    sources, parts, other_ref, pair_ref = refs[:6], refs[6:-2], refs[-2], refs[-1]
    for which in (0, 1):
        keys, values = sources[2 * which : 2 * which + 2]
        for chunk in range(CHUNKS):
            at = slice(chunk * PAIR, (chunk + 1) * PAIR)
            ref = other_ref if which else parts[chunk // TOGETHER]
            where = chunk if which else chunk % TOGETHER
            ref[where, :, :PAIR] = keys[:, at]
            ref[where, :, PAIR:] = values[:, at]
    tokens, width = sources[4].shape
    for index in (0, 1):
        pair_ref[index, :tokens, :] = sources[4 + index][...]
        pair_ref[index, tokens:, :] = count_rows(count_ref, width)


def cut(info, counts, weight, cq, do):
    rows = weight.shape[0]
    tokens, width = cq.shape
    count = CHUNKS // TOGETHER
    part = jax.ShapeDtypeStruct((TOGETHER, rows, 2 * PAIR), BF)
    parts = jax.ShapeDtypeStruct((CHUNKS, rows, 2 * PAIR), BF)
    half = jax.ShapeDtypeStruct((2, tokens + 16, width // 2), BF)

    def columns(height, other, value):
        return pl.BlockSpec(
            (height, width // 2), lambda p, info: (0, 2 * value + ((info[0] & 1) ^ other))
        )

    *mine, other, pair = pl.pallas_call(
        cut_kernel,
        grid_spec=pltpu.PrefetchScalarGridSpec(
            num_scalar_prefetch=1,
            grid=(1,),
            in_specs=[pl.BlockSpec(memory_space=pltpu.SMEM)]
            + [columns(rows, other, value) for other in (0, 1) for value in (0, 1)]
            + [columns(tokens, 1, 0)] * 2,
            out_specs=[
                pl.BlockSpec(x.shape, lambda p, info: (0, 0, 0))
                for x in [part] * count + [parts, half]
            ],
        ),
        out_shape=[part] * count + [parts, half],
        compiler_params=pltpu.CompilerParams(vmem_limit_bytes=VMEM),
        cost_estimate=cost(3),
    )(info, counts, weight, weight, weight, weight, cq, do)
    return mine, other, pair


def stack_kernel(*refs):
    count = CHUNKS // TOGETHER
    mine, near_ref, outs = refs[:count], refs[count], refs[count + 1 :]
    rows = near_ref.shape[1]
    for group, (ref, out) in enumerate(zip(mine, outs)):
        out[:, :rows, :] = ref[...]
        out[:, rows:, :] = near_ref[group * TOGETHER : (group + 1) * TOGETHER]


def stack(mine, near):
    together, rows, width = mine[0].shape
    return pl.pallas_call(
        stack_kernel,
        out_shape=[jax.ShapeDtypeStruct((together, 2 * rows, width), BF)] * len(mine),
        compiler_params=pltpu.CompilerParams(vmem_limit_bytes=VMEM),
        cost_estimate=cost(2),
    )(*mine, near)


def cross_kernel(group, turns, pieces, held, info_ref, count_ref, *refs):
    (turn_ref, nb_last, nb_own, peer_last, nb_peer), refs = refs[:5], refs[5:]
    weights, refs = refs[:pieces], refs[pieces:]
    (cq_ref, do_ref, peer_ref), refs = refs[:3], refs[3 + held :]
    token_outs, (keep_out, send_out), refs = refs[:4], refs[4:6], refs[6:]
    turned_out, refs = (refs[0], refs[1:]) if turns else (None, refs)
    (w_ref, nb_ref, turned_ref, kv_ref, dkv_ref, q_ref, g_ref, tail_ref), refs = refs[:8], refs[8:]
    out_ref, dw_ref, pick_ref, sem, out_sem = refs
    shard = info_ref[0]
    enc = nb_ref.shape[1]
    tokens = q_ref.shape[1]
    groups = tokens // GROUP
    per = 2 * RLEN
    size = groups * per
    rows = weights[0].shape[1]
    wide = TOGETHER * PAIR
    loads, stores = [], []

    def load(source, target):
        copy = pltpu.make_async_copy(source, target, sem.at[len(loads)])
        copy.start()
        loads.append(copy)
        return copy

    def store(source, target):
        copy = pltpu.make_async_copy(source, target, out_sem.at[len(stores)])
        copy.start()
        stores.append(copy)

    def load_weight(index):
        sources = [weights[0].at[index], weights[1].at[group * TOGETHER + index]]
        for ref in weights[2:]:
            sources += [ref.at[index, :rows, :], ref.at[index, rows:, :]]
        waits = []
        for piece, source in enumerate(sources):
            at = pl.ds(pl.multiple_of((shard ^ piece) * rows, 16), rows)
            waits.append(load(source, w_ref.at[index, at, :]))
        return waits

    waits_w = [load_weight(0)]
    waits_nb = [
        load(nb_last.at[:per, :], nb_ref.at[:per, :]),
        *[load(nb_own.at[u - 1], nb_ref.at[u * per : (u + 1) * per, :]) for u in range(1, groups)],
        load(peer_last.at[:per, :], nb_ref.at[size : size + per, :]),
        *[
            load(nb_peer.at[u - 1], nb_ref.at[size + u * per : size + (u + 1) * per, :])
            for u in range(1, groups)
        ],
    ]
    lanes = pl.ds(pl.multiple_of(((shard & 1) * CHUNKS + group * TOGETHER) * PAIR, PAIR), wide)
    there = slice(group * wide, (group + 1) * wide)
    waits_q = [
        load(cq_ref.at[:, lanes], q_ref.at[0]),
        load(do_ref.at[:, lanes], g_ref.at[0]),
        load(peer_ref.at[0, :tokens, there], q_ref.at[1]),
        load(peer_ref.at[1, :tokens, there], g_ref.at[1]),
        load(nb_last.at[per:, : 2 * GROUP], tail_ref.at[0]),
        load(peer_last.at[per:, : 2 * GROUP], tail_ref.at[1]),
        load(peer_ref.at[0, tokens:, : 2 * GROUP], tail_ref.at[2]),
    ]
    wait_turn = load(turn_ref, pick_ref if turns else turned_ref)
    for index in range(1, TOGETHER):
        waits_w.append(load_weight(index))

    def project(index):
        for copy in waits_w[index]:
            copy.wait()
        for file in (0, 1):
            for start, stop in ((0, 1), (1, groups)):
                if index == 0:
                    for copy in waits_nb[file * groups + start : file * groups + stop]:
                        copy.wait()
                at = slice(file * size + start * per, file * size + stop * per)
                kv_ref[index, at, :] = mm(nb_ref[at, :], w_ref[index], NN).astype(BF)

    zero = jnp.zeros((GROUP, HD), BF)

    def diagonal(block):
        return jnp.concatenate(
            [
                jnp.concatenate([block[:, :HD], zero], 1),
                jnp.concatenate([zero, block[:, HD:]], 1),
            ],
            0,
        )

    row = lax.broadcasted_iota(jnp.int32, (per, 2 * GROUP), 0).astype(F32)

    def first(index, file, u):
        unit = file * groups + u
        at = slice(unit * per, (unit + 1) * per)
        tok = slice(u * GROUP, (u + 1) * GROUP)
        cols = slice(index * PAIR, (index + 1) * PAIR)
        keys, values = kv_ref[index, at, :PAIR], kv_ref[index, at, PAIR:]
        queries, grads = diagonal(q_ref[file, tok, cols]), diagonal(g_ref[file, tok, cols])
        return keys, values, queries, grads, mm(keys, queries, NT), mm(values, grads, NT)

    def second(index, file, u, state):
        keys, values, queries, grads, scores, prob_grad = state
        if u == 0:
            count = tail_ref[file, groups - 1 : groups, :].astype(F32)
        elif file:
            count = tail_ref[2, u - 1 : u, :].astype(F32)
        else:
            count = count_ref[u - 1].astype(F32)
        scores = jnp.where(row < count * RLEN, scores, NEG)
        peak = jnp.max(scores, axis=0, keepdims=True)
        weight = jnp.exp2((scores - peak) * (SCALE * LOG2E))
        total = jnp.sum(weight, axis=0, keepdims=True)
        inverse = jnp.where(count > 0, 1.0 / total, 0.0)
        probs = weight * inverse
        delta = jnp.sum(probs * prob_grad, axis=0, keepdims=True)
        score_grad = (probs * (prob_grad - delta)).astype(BF)
        return keys, values, queries, grads, probs.astype(BF), score_grad

    def third(index, file, u, state):
        keys, values, queries, grads, low, score_grad = state
        unit = file * groups + u
        at = slice(unit * per, (unit + 1) * per)
        tok = slice(u * GROUP, (u + 1) * GROUP)
        out = mm(low, values, TN).astype(BF)
        dq = (mm(score_grad, keys, TN) * SCALE).astype(BF)
        for which, value in enumerate((out, dq)):
            out_ref[file, which, tok, index * PAIR : index * PAIR + HD] = value[:GROUP, :HD]
            out_ref[file, which, tok, index * PAIR + HD : (index + 1) * PAIR] = value[GROUP:, HD:]
        dkv_ref[index, at, :PAIR] = (mm(score_grad, queries, NN) * SCALE).astype(BF)
        dkv_ref[index, at, PAIR:] = mm(low, grads, NN).astype(BF)

    half = enc // 2
    bit = (shard // 2) % 2

    def weigh(index, targets):
        for slot, target, which in targets:
            at = pl.ds(pl.multiple_of(which * half, 16), half)
            dw_ref[slot, index] = mm(turned_ref[at, :], dkv_ref[index], NN).astype(BF)
            store(dw_ref.at[slot, index], target.at[index])

    both = ((0, send_out, 1 - bit), (1, keep_out, bit))
    project(0)
    for copy in waits_q:
        copy.wait()
    for index in range(TOGETHER):
        units = [(index, file, u) for file in (0, 1) for u in range(groups)]
        ready, late = first(*units[0]), None
        for number, unit in enumerate(units):
            upcoming = first(*units[number + 1]) if number + 1 < len(units) else None
            done = second(*unit, ready)
            if late:
                third(*late)
            ready, late = upcoming, (*unit, done)
        third(*late)
        if index + 1 < TOGETHER:
            project(index + 1)
        if index == 0:
            wait_turn.wait()
            if turns:
                turned_ref[...] = mm(pick_ref[...], nb_ref[...], NT).astype(BF)
                store(turned_ref, turned_out)
        if index + 1 == TOGETHER:
            for which, target in enumerate(token_outs):
                store(out_ref.at[which // 2, which % 2], target.at[:, there])
        weigh(index, both)
    for copy in stores:
        copy.wait()


def cross(group, info, counts, turn, nbs, weights, cq, do, peer, held):
    tokens, half = peer.shape[1] - 16, peer.shape[2]
    groups, per, enc = nbs[1].shape
    size = 2 * groups * per
    turns = group == 0
    smem = pl.BlockSpec(memory_space=pltpu.SMEM)
    operands = [info, counts, turn, *nbs, *weights, cq, do, peer]
    shapes = [jax.ShapeDtypeStruct((tokens, half), BF)] * 4
    shapes += [jax.ShapeDtypeStruct((TOGETHER, enc // 2, 2 * PAIR), BF)] * 2
    if turns:
        shapes.append(jax.ShapeDtypeStruct((enc, size), BF))
    return pl.pallas_call(
        functools.partial(cross_kernel, group, turns, len(weights), len(held)),
        in_specs=[smem, smem] + [ANY] * (len(operands) - 2 + len(held)),
        out_specs=[ANY] * len(shapes),
        out_shape=shapes,
        scratch_shapes=[
            pltpu.VMEM((TOGETHER, enc, 2 * PAIR), BF),
            pltpu.VMEM((size, enc), BF),
            pltpu.VMEM((enc, size), BF),
            pltpu.VMEM((TOGETHER, size, 2 * PAIR), BF),
            pltpu.VMEM((TOGETHER, size, 2 * PAIR), BF),
            pltpu.VMEM((2, tokens, TOGETHER * PAIR), BF),
            pltpu.VMEM((2, tokens, TOGETHER * PAIR), BF),
            pltpu.VMEM((3, 16, 2 * GROUP), BF),
            pltpu.VMEM((2, 2, tokens, TOGETHER * PAIR), BF),
            pltpu.VMEM((2, TOGETHER, enc // 2, 2 * PAIR), BF),
            pltpu.VMEM((enc, enc) if turns else (16, 128), BF),
            pltpu.SemaphoreType.DMA((2 * groups + 8 + TOGETHER * 2 * len(weights),)),
            pltpu.SemaphoreType.DMA((5 + 2 * TOGETHER,)),
        ],
        input_output_aliases={len(operands) + i: i for i in range(len(held))},
        compiler_params=pltpu.CompilerParams(vmem_limit_bytes=VMEM),
        cost_estimate=cost(9),
    )(*operands, *held)


def self_kernel(
    heads, info_ref, q_ref, do_ref, ko_ref, vo_ref, one_ref, two_ref, three_ref, *refs
):
    own_ref, own_grad, back_ref, back_grad, *refs = refs
    out_ref, dq_ref, cross_ref, dk_ref, dv_ref, stat_ref = refs
    first_half = pl.program_id(0) < pl.num_programs(0) // 2
    crossed = jnp.where(first_half, own_ref[...], back_ref[...])
    cross_ref[...] = jnp.where(first_half, own_grad[...], back_grad[...])
    odd = info_ref[1] % 2 == 1
    keys_before = jnp.where(odd, one_ref[...], two_ref[...])
    values_before = jnp.where(odd, two_ref[...], three_ref[...])
    later = info_ref[1] > 0
    tokens = q_ref.shape[0]
    half = tokens // 2
    key_at = lax.broadcasted_iota(jnp.int32, (half, half), 0)
    query_at = lax.broadcasted_iota(jnp.int32, (half, half), 1)
    above = jnp.logical_and(key_at > query_at, later)
    below = key_at <= query_at
    zero = jnp.zeros((half, half), BF)
    lo, hi = slice(0, half), slice(half, None)

    def first(head):
        at = slice(head * HD, (head + 1) * HD)
        queries, grads = q_ref[:, at], do_ref[:, at]
        kp, vp = keys_before[:, at], values_before[:, at]
        ko, vo = ko_ref[:, at], vo_ref[:, at]
        return (
            (queries, grads, kp, vp, ko, vo),
            (mm(kp, queries, NT), mm(ko, queries, NT)),
            (mm(vp, grads, NT), mm(vo, grads, NT)),
        )

    def second(head, state):
        inputs, (sp, so), (gp, go) = state
        rows = []
        for a in (0, 1):
            if a == 0:
                blocks = (sp[lo, lo], sp[hi, lo], so[lo, lo])
                pgrads = (gp[lo, lo], gp[hi, lo], go[lo, lo])
                middle = jnp.where(later, blocks[1], NEG)
            else:
                blocks = (sp[hi, hi], so[lo, hi], so[hi, hi])
                pgrads = (gp[hi, hi], go[lo, hi], go[hi, hi])
                middle = blocks[1]
            scores = (jnp.where(above, blocks[0], NEG), middle, jnp.where(below, blocks[2], NEG))
            peak = jnp.max(
                jnp.maximum(jnp.maximum(scores[0], scores[1]), scores[2]), axis=0, keepdims=True
            )
            weight = [jnp.exp2((s - peak) * (SCALE * LOG2E)) for s in scores]
            total = jnp.sum(weight[0] + weight[1] + weight[2], axis=0, keepdims=True)
            inverse = 1.0 / total
            probs = [w * inverse for w in weight]
            delta = jnp.sum(
                probs[0] * pgrads[0] + probs[1] * pgrads[1] + probs[2] * pgrads[2],
                axis=0,
                keepdims=True,
            )
            score_grad = [(p * (g - delta)).astype(BF) for p, g in zip(probs, pgrads)]
            rows.append(([p.astype(BF) for p in probs], score_grad))
            lanes = slice(a * half, (a + 1) * half)
            stat_ref[head, 0:1, lanes] = peak * (SCALE * LOG2E) + jnp.log2(total)
            stat_ref[head, 1:2, lanes] = delta

        def spread(which):
            one, two = rows[0][which], rows[1][which]
            before = jnp.concatenate(
                [jnp.concatenate([one[0], zero], 1), jnp.concatenate([one[1], two[0]], 1)], 0
            )
            own = jnp.concatenate(
                [jnp.concatenate([one[2], two[1]], 1), jnp.concatenate([zero, two[2]], 1)], 0
            )
            return before, own

        return inputs, spread(0), spread(1)

    def third(head, state):
        at = slice(head * HD, (head + 1) * HD)
        (queries, grads, kp, vp, ko, vo), (pp, po), (dp, do) = state
        out = mm(pp, vp, TN) + mm(po, vo, TN) + crossed[:, at].astype(F32)
        out_ref[:, at] = out.astype(BF)
        dq_ref[:, at] = ((mm(dp, kp, TN) + mm(do, ko, TN)) * SCALE).astype(BF)
        dk_ref[:, at] = mm(do, queries, NN) * SCALE
        dv_ref[:, at] = mm(po, grads, NN)

    ready = first(0)
    for head in range(heads):
        upcoming = first(head + 1) if head + 1 < heads else None
        third(head, second(head, ready))
        ready = upcoming


def self_part(info, q, do, k, v, one, two, three, own, back):
    heads = 4
    tokens, width = q.shape
    steps = width // (heads * HD)
    half = steps // 2
    shape = (tokens, heads * HD)

    def place(p, info):
        return (p + (info[0] & 1) * half) % steps

    spec = pl.BlockSpec(shape, lambda p, info: (0, place(p, info)))
    own_spec = pl.BlockSpec(shape, lambda p, info: (0, jnp.minimum(p, half - 1)))
    back_spec = pl.BlockSpec(shape, lambda p, info: (0, jnp.maximum(p - half, 0)))
    stat_spec = pl.BlockSpec((heads, 2, tokens), lambda p, info: (place(p, info), 0, 0))
    full = jax.ShapeDtypeStruct(q.shape, BF)
    wide = jax.ShapeDtypeStruct(q.shape, F32)
    stats = jax.ShapeDtypeStruct((width // HD, 2, tokens), F32)
    return pl.pallas_call(
        functools.partial(self_kernel, heads),
        grid_spec=pltpu.PrefetchScalarGridSpec(
            num_scalar_prefetch=1,
            grid=(steps,),
            in_specs=[spec] * 7 + [own_spec] * 2 + [back_spec] * 2,
            out_specs=[spec] * 5 + [stat_spec],
        ),
        out_shape=[full] * 3 + [wide] * 2 + [stats],
        compiler_params=pltpu.CompilerParams(vmem_limit_bytes=VMEM),
        cost_estimate=cost(14),
    )(info, q, do, k, v, one, two, three, *own, *back)


def next_kernel(
    heads, info_ref, one_ref, three_ref, do_ref, k_ref, v_ref, stat_ref, dkp_ref, dvp_ref,
    dk_ref, dv_ref,
):
    all_queries = jnp.where(info_ref[1] % 2 == 1, three_ref[...], one_ref[...])
    tokens = do_ref.shape[0]
    half = tokens // 2
    key_at = lax.broadcasted_iota(jnp.int32, (half, half), 0)
    query_at = lax.broadcasted_iota(jnp.int32, (half, half), 1)
    above = key_at > query_at
    zero = jnp.zeros((half, half), BF)
    lo, hi = slice(0, half), slice(half, None)

    def first(head):
        at = slice(head * HD, (head + 1) * HD)
        queries, grads = all_queries[:, at], do_ref[:, at]
        return queries, grads, mm(k_ref[:, at], queries, NT), mm(v_ref[:, at], grads, NT)

    def second(head, state):
        at = slice(head * HD, (head + 1) * HD)
        queries, grads, scores, prob_grad = state
        level, delta = stat_ref[head, 0:1, :], stat_ref[head, 1:2, :]

        def block(rows, lanes, mask):
            exponent = scores[rows, lanes] * (SCALE * LOG2E) - level[:, lanes]
            if mask:
                exponent = jnp.where(above, exponent, NEG)
            probs = jnp.exp2(exponent)
            return probs.astype(BF), (probs * (prob_grad[rows, lanes] - delta[:, lanes])).astype(BF)

        one, middle, last = block(lo, lo, True), block(hi, lo, False), block(hi, hi, True)
        low, score_grad = [
            jnp.concatenate(
                [
                    jnp.concatenate([one[i], zero], 1),
                    jnp.concatenate([middle[i], last[i]], 1),
                ],
                0,
            )
            for i in (0, 1)
        ]
        dk_ref[:, at] = (dkp_ref[:, at] + mm(score_grad, queries, NN) * SCALE).astype(BF)
        dv_ref[:, at] = (dvp_ref[:, at] + mm(low, grads, NN)).astype(BF)

    ready = first(0)
    for head in range(heads):
        upcoming = first(head + 1) if head + 1 < heads else None
        second(head, ready)
        ready = upcoming


def next_part(info, one, three, do, k, v, stats, dk, dv):
    heads = 8
    tokens, width = k.shape
    spec = pl.BlockSpec((tokens, heads * HD), lambda p: (0, p))
    stat_spec = pl.BlockSpec((heads, 2, tokens), lambda p: (p, 0, 0))
    full = jax.ShapeDtypeStruct(k.shape, BF)
    return pl.pallas_call(
        functools.partial(next_kernel, heads),
        grid=(width // (heads * HD),),
        in_specs=[pl.BlockSpec(memory_space=pltpu.SMEM)]
        + [spec] * 5
        + [stat_spec]
        + [spec] * 2,
        out_specs=[spec] * 2,
        out_shape=[full] * 2,
        compiler_params=pltpu.CompilerParams(vmem_limit_bytes=VMEM),
        cost_estimate=cost(8),
    )(info, one, three, do, k, v, stats, dk, dv)


def halving_order(fsdp, seq):
    bits = [("fsdp", 1 << i) for i in range(1, fsdp.bit_length() - 1)]
    seq_bits = [("seq", 1 << i) for i in range(seq.bit_length() - 1)]
    return bits + seq_bits[1:] + seq_bits[:1]


def row_order(fsdp, seq, rows):
    index = np.arange(rows).reshape(seq * fsdp, -1)
    block = np.arange(seq * fsdp)
    keys = []
    for axis, bit in halving_order(fsdp, seq) + [("fsdp", 1)]:
        value = block % fsdp if axis == "fsdp" else block // fsdp
        keys.append((value // bit) % 2)
    order = np.lexsort(keys[::-1])
    return index[order].reshape(-1)


def take_half(value, upper):
    half = value.shape[0] // 2
    return lax.dynamic_slice_in_dim(value, upper * half, half, 0)


def halve_kernel(spans, axis, bit, info_ref, *refs):
    sources, (mine_ref, other_ref) = refs[:-2], refs[-2:]
    count = len(sources) // 2
    half = mine_ref.shape[0]
    upper = (info_ref[0 if axis == "fsdp" else 1] // bit) % 2
    for ref, which in ((mine_ref, upper), (other_ref, 1 - upper)):
        at = pl.ds(pl.multiple_of(which * half, 16), half)
        start = 0
        for keep, got, parts in zip(sources[:count], sources[count:], spans):
            width = keep.shape[-1]
            for part in range(parts):
                where = (part, at) if len(keep.shape) == 3 else (at,)
                total = keep[where].astype(F32) + got[where].astype(F32)
                ref[:, start : start + width] = total.astype(BF)
                start += width


def halve(info, keeps, received, stage):
    axis, bit = stage
    spans = [x.shape[0] if x.ndim == 3 else 1 for x in keeps]
    rows = keeps[0].shape[-2]
    width = sum(parts * x.shape[-1] for parts, x in zip(spans, keeps))
    if rows // 2 % 16:
        upper = (info[0 if axis == "fsdp" else 1] // bit) % 2
        sums = [
            (x.astype(F32) + y.astype(F32)).reshape(-1, rows, x.shape[-1])
            for x, y in zip(keeps, received)
        ]
        total = jnp.concatenate([part for x in sums for part in x], -1)
        return take_half(total, upper).astype(BF), take_half(total, 1 - upper).astype(BF)
    return pl.pallas_call(
        functools.partial(halve_kernel, spans, axis, bit),
        in_specs=[pl.BlockSpec(memory_space=pltpu.SMEM)]
        + [pl.BlockSpec(memory_space=pltpu.VMEM)] * (2 * len(keeps)),
        out_shape=[jax.ShapeDtypeStruct((rows // 2, width), BF)] * 2,
        compiler_params=pltpu.CompilerParams(vmem_limit_bytes=VMEM),
        cost_estimate=cost(1),
    )(info, *keeps, *received)


def on_device(
    self_query, self_key, self_value, cross_query, neighbours, neighbour_count, kv_weight, out_grad
):
    fsdp, seq = lax.axis_size("fsdp"), lax.axis_size("seq")
    shard, slab = lax.axis_index("fsdp"), lax.axis_index("seq")
    q, k, v, cq, do = (x[0] for x in (self_query, self_key, self_value, cross_query, out_grad))
    nb, counts = neighbours[0], neighbour_count[0]
    tokens, width = q.shape
    groups, per, enc = nb.shape
    info = jnp.stack([shard, slab]).astype(jnp.int32)

    last = pack(nb, counts)
    nb_last = shift(last, "seq", 1)

    nb_peer = swap(nb, "fsdp", 1)
    mine, other, pair = cut(after(info, last, nb_peer), counts, kv_weight, cq, do)
    near = swap(other, "fsdp", 1)
    weights = [
        [here, near, *[swap(x, "fsdp", piece) for piece in range(2, fsdp, 2)]]
        for here, x in zip(mine, stack(mine, near))
    ]
    peer = swap(pair, "fsdp", 1)

    even = slab % 2 == 0

    def pick(when_even, when_odd, *others):
        return jnp.where(after(even, nb_last, *others), when_even, when_odd)

    def hop(value):
        odds = [(i, i + 2) for i in range(1, seq - 2, 2)]
        return lax.ppermute(value, "seq", odds + [(i, i - 2) for i in range(2, seq, 2)])

    far_one = hop(pick(q, k))
    one = swap(pick(k, q), "seq", 1)
    far_two = hop(pick(do, v))

    nb_last = after(nb_last, peer)
    peer_last = swap(nb_last, "fsdp", 1)
    nbs = [nb_last, nb, peer_last, nb_peer]

    stages = halving_order(fsdp, seq)
    split_at = fsdp.bit_length() - 2

    turn = jnp.asarray(np.eye(enc)[row_order(fsdp, seq, enc)], BF)
    held, pairs = [], []
    for group in range(CHUNKS // TOGETHER):
        results = cross(group, info, counts, turn, nbs, weights[group], cq, do, peer, held)
        held, (keep, send) = results[:4], results[4:6]
        if not group:
            turn = results[6]
            two = swap(pick(v, far_one, turn), "seq", 1)
        received = swap(send, *stages[0])
        for stage in range(1, split_at):
            keep, send = halve(info, [keep], [received], stages[stage])
            received = swap(send, *stages[stage])
        pairs.append((keep, received))
    own = held[:2]
    back = [swap(x, "fsdp", 1) for x in after(held[2:], pairs[0][1], one, two)]
    third = pick(far_one, far_two, pairs[-1][0])
    three = swap(third, "seq", 1)

    halves = [halve(info, [pairs[0][0]], [pairs[0][1]], stages[split_at])]
    got = [swap(halves[0][1], *stages[split_at])]
    halves.append(
        halve(after(info, halves[0][1], *back), [pairs[1][0]], [pairs[1][1]], stages[split_at])
    )
    got.append(swap(halves[1][1], *stages[split_at]))
    four = swap(pick(far_two, do, halves[1][1], third), "seq", 1)
    keeps = [keep for keep, _ in halves]
    keep, send = halve(after(info, three), keeps, got, stages[split_at + 1])
    keeps, got = [keep], [swap(send, *stages[split_at + 1])]
    block_out, query_grad, cross_grad, dk, dv, stats = self_part(
        after(info, send), q, do, k, v, one, two, three, own, back
    )
    stats_after = shift(stats, "seq", -1)
    key_grad, value_grad = next_part(info, one, three, four, k, v, stats_after, dk, dv)

    for stage in range(split_at + 2, len(stages)):
        keep, send = halve(after(info, stats), keeps, got, stages[stage])
        keeps, got = [keep], [swap(send, *stages[stage])]
    total = keeps[0].astype(F32) + got[0].astype(F32)
    core = shard % 2
    away = swap(take_half(total, 1 - core).astype(BF), "fsdp", 1).astype(F32)
    nearby = take_half(total, core)
    key_mine, key_away, value_mine, value_away = [
        jnp.concatenate(
            [x[:, (2 * c + part) * PAIR : (2 * c + part + 1) * PAIR] for c in range(CHUNKS)], -1
        )
        for part in (0, 1)
        for x in (nearby, away)
    ]
    low = shard % 2 == 0
    weight_grad = jnp.concatenate(
        [
            jnp.where(low, key_mine, key_away),
            jnp.where(low, key_away, key_mine),
            jnp.where(low, value_mine, value_away),
            jnp.where(low, value_away, value_mine),
        ],
        -1,
    )

    return (
        block_out[None],
        query_grad[None],
        key_grad[None],
        value_grad[None],
        cross_grad[None],
        weight_grad,
    )


def solution(mesh):
    in_specs = (
        P("fsdp", "seq", None),
        P("fsdp", "seq", None),
        P("fsdp", "seq", None),
        P("fsdp", "seq", None),
        P("fsdp", "seq", None, None),
        P("fsdp", "seq"),
        P("fsdp", None),
        P("fsdp", "seq", None),
    )
    out_specs = (
        P("fsdp", "seq", None),
        P("fsdp", "seq", None),
        P("fsdp", "seq", None),
        P("fsdp", "seq", None),
        P("fsdp", "seq", None),
        P(("seq", "fsdp"), None),
    )
    return jax.shard_map(
        on_device, mesh=mesh, in_specs=in_specs, out_specs=out_specs, check_vma=False
    )
```

```python
import functools

import numpy as np
import jax
import jax.numpy as jnp
from jax import lax
from jax.experimental import pallas as pl
from jax.experimental.pallas import tpu as pltpu
from jax.sharding import PartitionSpec as P

HEADS = 16
HD = 128
GROUP = 64
RLEN = 128
PAIR = 2 * HD
CHUNKS = HEADS // 4
TOGETHER = 2
VMEM = 60 * 2**20
SCALE = HD ** (-0.5)
LOG2E = 1.4426950408889634
NEG = -1e30
BF = jnp.bfloat16
F32 = jnp.float32
ANY = pl.BlockSpec(memory_space=pl.ANY)

NT = (((1,), (1,)), ((), ()))
TN = (((0,), (0,)), ((), ()))
NN = (((1,), (0,)), ((), ()))


def cost(micros):
    return pl.CostEstimate(flops=int(micros * 1e9), bytes_accessed=1000, transcendentals=0)


def mm(a, b, dims):
    return lax.dot_general(a, b, dims, preferred_element_type=F32)


def shift(value, axis, steps):
    count = lax.axis_size(axis)
    first, last = max(0, -steps), min(count, count - steps)
    return lax.ppermute(value, axis, [(i, i + steps) for i in range(first, last)])


def after(value, *others):
    return lax.optimization_barrier((value, *others))[0]


def swap(value, axis, bit):
    return lax.ppermute(value, axis, [(i, i ^ bit) for i in range(lax.axis_size(axis))])


def count_rows(count_ref, width):
    row = lax.broadcasted_iota(jnp.int32, (16, width), 0)
    tail = jnp.zeros((16, width), F32)
    for u in range(count_ref.shape[0]):
        tail = jnp.where(row == u, count_ref[u].astype(F32), tail)
    return tail.astype(BF)


def pack_kernel(count_ref, nb_ref, out_ref):
    per, enc = nb_ref.shape[1:]
    out_ref[:per, :] = nb_ref[0]
    out_ref[per:, :] = count_rows(count_ref, enc)


def pack(nb, counts):
    groups, per, enc = nb.shape
    return pl.pallas_call(
        pack_kernel,
        grid=(1,),
        in_specs=[
            pl.BlockSpec(memory_space=pltpu.SMEM),
            pl.BlockSpec((1, per, enc), lambda p: (groups - 1, 0, 0)),
        ],
        out_specs=pl.BlockSpec((per + 16, enc), lambda p: (0, 0)),
        out_shape=jax.ShapeDtypeStruct((per + 16, enc), BF),
        compiler_params=pltpu.CompilerParams(vmem_limit_bytes=VMEM),
        cost_estimate=cost(2),
    )(counts, nb)


def cut_kernel(info_ref, count_ref, *refs):
    sources, parts, other_ref, pair_ref = refs[:6], refs[6:-2], refs[-2], refs[-1]
    for which in (0, 1):
        keys, values = sources[2 * which : 2 * which + 2]
        for chunk in range(CHUNKS):
            at = slice(chunk * PAIR, (chunk + 1) * PAIR)
            ref = other_ref if which else parts[chunk // TOGETHER]
            where = chunk if which else chunk % TOGETHER
            ref[where, :, :PAIR] = keys[:, at]
            ref[where, :, PAIR:] = values[:, at]
    tokens, width = sources[4].shape
    for index in (0, 1):
        pair_ref[index, :tokens, :] = sources[4 + index][...]
        pair_ref[index, tokens:, :] = count_rows(count_ref, width)


def cut(info, counts, weight, cq, do):
    rows = weight.shape[0]
    tokens, width = cq.shape
    count = CHUNKS // TOGETHER
    part = jax.ShapeDtypeStruct((TOGETHER, rows, 2 * PAIR), BF)
    parts = jax.ShapeDtypeStruct((CHUNKS, rows, 2 * PAIR), BF)
    half = jax.ShapeDtypeStruct((2, tokens + 16, width // 2), BF)

    def columns(height, other, value):
        return pl.BlockSpec(
            (height, width // 2), lambda p, info: (0, 2 * value + ((info[0] & 1) ^ other))
        )

    *mine, other, pair = pl.pallas_call(
        cut_kernel,
        grid_spec=pltpu.PrefetchScalarGridSpec(
            num_scalar_prefetch=1,
            grid=(1,),
            in_specs=[pl.BlockSpec(memory_space=pltpu.SMEM)]
            + [columns(rows, other, value) for other in (0, 1) for value in (0, 1)]
            + [columns(tokens, 1, 0)] * 2,
            out_specs=[
                pl.BlockSpec(x.shape, lambda p, info: (0, 0, 0))
                for x in [part] * count + [parts, half]
            ],
        ),
        out_shape=[part] * count + [parts, half],
        compiler_params=pltpu.CompilerParams(vmem_limit_bytes=VMEM),
        cost_estimate=cost(3),
    )(info, counts, weight, weight, weight, weight, cq, do)
    return mine, other, pair


def stack_kernel(*refs):
    count = CHUNKS // TOGETHER
    mine, near_ref, outs = refs[:count], refs[count], refs[count + 1 :]
    rows = near_ref.shape[1]
    for group, (ref, out) in enumerate(zip(mine, outs)):
        out[:, :rows, :] = ref[...]
        out[:, rows:, :] = near_ref[group * TOGETHER : (group + 1) * TOGETHER]


def stack(mine, near):
    together, rows, width = mine[0].shape
    return pl.pallas_call(
        stack_kernel,
        out_shape=[jax.ShapeDtypeStruct((together, 2 * rows, width), BF)] * len(mine),
        compiler_params=pltpu.CompilerParams(vmem_limit_bytes=VMEM),
        cost_estimate=cost(2),
    )(*mine, near)


def cross_kernel(group, turns, pieces, held, info_ref, count_ref, *refs):
    (turn_ref, nb_last, nb_own, peer_last, nb_peer), refs = refs[:5], refs[5:]
    weights, refs = refs[:pieces], refs[pieces:]
    (cq_ref, do_ref, peer_ref), refs = refs[:3], refs[3 + held :]
    token_outs, (keep_out, send_out), refs = refs[:4], refs[4:6], refs[6:]
    turned_out, refs = (refs[0], refs[1:]) if turns else (None, refs)
    (w_ref, nb_ref, turned_ref, kv_ref, dkv_ref, q_ref, g_ref, tail_ref), refs = refs[:8], refs[8:]
    out_ref, dw_ref, pick_ref, sem, out_sem = refs
    shard = info_ref[0]
    enc = nb_ref.shape[1]
    tokens = q_ref.shape[1]
    groups = tokens // GROUP
    per = 2 * RLEN
    size = groups * per
    rows = weights[0].shape[1]
    wide = TOGETHER * PAIR
    loads, stores = [], []

    def load(source, target):
        copy = pltpu.make_async_copy(source, target, sem.at[len(loads)])
        copy.start()
        loads.append(copy)
        return copy

    def store(source, target):
        copy = pltpu.make_async_copy(source, target, out_sem.at[len(stores)])
        copy.start()
        stores.append(copy)

    def load_weight(index):
        sources = [weights[0].at[index], weights[1].at[group * TOGETHER + index]]
        for ref in weights[2:]:
            sources += [ref.at[index, :rows, :], ref.at[index, rows:, :]]
        waits = []
        for piece, source in enumerate(sources):
            at = pl.ds(pl.multiple_of((shard ^ piece) * rows, 16), rows)
            waits.append(load(source, w_ref.at[index, at, :]))
        return waits

    waits_w = [load_weight(0)]
    waits_nb = [
        load(nb_last.at[:per, :], nb_ref.at[:per, :]),
        *[load(nb_own.at[u - 1], nb_ref.at[u * per : (u + 1) * per, :]) for u in range(1, groups)],
        load(peer_last.at[:per, :], nb_ref.at[size : size + per, :]),
        *[
            load(nb_peer.at[u - 1], nb_ref.at[size + u * per : size + (u + 1) * per, :])
            for u in range(1, groups)
        ],
    ]
    lanes = pl.ds(pl.multiple_of(((shard & 1) * CHUNKS + group * TOGETHER) * PAIR, PAIR), wide)
    there = slice(group * wide, (group + 1) * wide)
    waits_q = [
        load(cq_ref.at[:, lanes], q_ref.at[0]),
        load(do_ref.at[:, lanes], g_ref.at[0]),
        load(peer_ref.at[0, :tokens, there], q_ref.at[1]),
        load(peer_ref.at[1, :tokens, there], g_ref.at[1]),
        load(nb_last.at[per:, : 2 * GROUP], tail_ref.at[0]),
        load(peer_last.at[per:, : 2 * GROUP], tail_ref.at[1]),
        load(peer_ref.at[0, tokens:, : 2 * GROUP], tail_ref.at[2]),
    ]
    wait_turn = load(turn_ref, pick_ref if turns else turned_ref)
    for index in range(1, TOGETHER):
        waits_w.append(load_weight(index))

    def project(index):
        for copy in waits_w[index]:
            copy.wait()
        for file in (0, 1):
            for start, stop in ((0, 1), (1, groups)):
                if index == 0:
                    for copy in waits_nb[file * groups + start : file * groups + stop]:
                        copy.wait()
                at = slice(file * size + start * per, file * size + stop * per)
                kv_ref[index, at, :] = mm(nb_ref[at, :], w_ref[index], NN).astype(BF)

    zero = jnp.zeros((GROUP, HD), BF)

    def diagonal(block):
        return jnp.concatenate(
            [
                jnp.concatenate([block[:, :HD], zero], 1),
                jnp.concatenate([zero, block[:, HD:]], 1),
            ],
            0,
        )

    row = lax.broadcasted_iota(jnp.int32, (per, 2 * GROUP), 0).astype(F32)

    def first(index, file, u):
        unit = file * groups + u
        at = slice(unit * per, (unit + 1) * per)
        tok = slice(u * GROUP, (u + 1) * GROUP)
        cols = slice(index * PAIR, (index + 1) * PAIR)
        keys, values = kv_ref[index, at, :PAIR], kv_ref[index, at, PAIR:]
        queries, grads = diagonal(q_ref[file, tok, cols]), diagonal(g_ref[file, tok, cols])
        return keys, values, queries, grads, mm(keys, queries, NT), mm(values, grads, NT)

    def second(index, file, u, state):
        keys, values, queries, grads, scores, prob_grad = state
        if u == 0:
            count = tail_ref[file, groups - 1 : groups, :].astype(F32)
        elif file:
            count = tail_ref[2, u - 1 : u, :].astype(F32)
        else:
            count = count_ref[u - 1].astype(F32)
        scores = jnp.where(row < count * RLEN, scores, NEG)
        peak = jnp.max(scores, axis=0, keepdims=True)
        weight = jnp.exp2((scores - peak) * (SCALE * LOG2E))
        total = jnp.sum(weight, axis=0, keepdims=True)
        inverse = jnp.where(count > 0, 1.0 / total, 0.0)
        probs = weight * inverse
        delta = jnp.sum(probs * prob_grad, axis=0, keepdims=True)
        score_grad = (probs * (prob_grad - delta)).astype(BF)
        return keys, values, queries, grads, probs.astype(BF), score_grad

    def third(index, file, u, state):
        keys, values, queries, grads, low, score_grad = state
        unit = file * groups + u
        at = slice(unit * per, (unit + 1) * per)
        tok = slice(u * GROUP, (u + 1) * GROUP)
        out = mm(low, values, TN).astype(BF)
        dq = (mm(score_grad, keys, TN) * SCALE).astype(BF)
        for which, value in enumerate((out, dq)):
            out_ref[file, which, tok, index * PAIR : index * PAIR + HD] = value[:GROUP, :HD]
            out_ref[file, which, tok, index * PAIR + HD : (index + 1) * PAIR] = value[GROUP:, HD:]
        dkv_ref[index, at, :PAIR] = (mm(score_grad, queries, NN) * SCALE).astype(BF)
        dkv_ref[index, at, PAIR:] = mm(low, grads, NN).astype(BF)

    half = enc // 2
    bit = (shard // 2) % 2

    def weigh(index, targets):
        for slot, target, which in targets:
            at = pl.ds(pl.multiple_of(which * half, 16), half)
            dw_ref[slot, index] = mm(turned_ref[at, :], dkv_ref[index], NN).astype(BF)
            store(dw_ref.at[slot, index], target.at[index])

    both = ((0, send_out, 1 - bit), (1, keep_out, bit))
    project(0)
    for copy in waits_q:
        copy.wait()
    for index in range(TOGETHER):
        units = [(index, file, u) for file in (0, 1) for u in range(groups)]
        ready, late = first(*units[0]), None
        for number, unit in enumerate(units):
            upcoming = first(*units[number + 1]) if number + 1 < len(units) else None
            done = second(*unit, ready)
            if late:
                third(*late)
            ready, late = upcoming, (*unit, done)
        third(*late)
        if index + 1 < TOGETHER:
            project(index + 1)
        if index == 0:
            wait_turn.wait()
            if turns:
                turned_ref[...] = mm(pick_ref[...], nb_ref[...], NT).astype(BF)
                store(turned_ref, turned_out)
        if index + 1 == TOGETHER:
            for which, target in enumerate(token_outs):
                store(out_ref.at[which // 2, which % 2], target.at[:, there])
        weigh(index, both)
    for copy in stores:
        copy.wait()


def cross(group, info, counts, turn, nbs, weights, cq, do, peer, held):
    tokens, half = peer.shape[1] - 16, peer.shape[2]
    groups, per, enc = nbs[1].shape
    size = 2 * groups * per
    turns = group == 0
    smem = pl.BlockSpec(memory_space=pltpu.SMEM)
    operands = [info, counts, turn, *nbs, *weights, cq, do, peer]
    shapes = [jax.ShapeDtypeStruct((tokens, half), BF)] * 4
    shapes += [jax.ShapeDtypeStruct((TOGETHER, enc // 2, 2 * PAIR), BF)] * 2
    if turns:
        shapes.append(jax.ShapeDtypeStruct((enc, size), BF))
    return pl.pallas_call(
        functools.partial(cross_kernel, group, turns, len(weights), len(held)),
        in_specs=[smem, smem] + [ANY] * (len(operands) - 2 + len(held)),
        out_specs=[ANY] * len(shapes),
        out_shape=shapes,
        scratch_shapes=[
            pltpu.VMEM((TOGETHER, enc, 2 * PAIR), BF),
            pltpu.VMEM((size, enc), BF),
            pltpu.VMEM((enc, size), BF),
            pltpu.VMEM((TOGETHER, size, 2 * PAIR), BF),
            pltpu.VMEM((TOGETHER, size, 2 * PAIR), BF),
            pltpu.VMEM((2, tokens, TOGETHER * PAIR), BF),
            pltpu.VMEM((2, tokens, TOGETHER * PAIR), BF),
            pltpu.VMEM((3, 16, 2 * GROUP), BF),
            pltpu.VMEM((2, 2, tokens, TOGETHER * PAIR), BF),
            pltpu.VMEM((2, TOGETHER, enc // 2, 2 * PAIR), BF),
            pltpu.VMEM((enc, enc) if turns else (16, 128), BF),
            pltpu.SemaphoreType.DMA((2 * groups + 8 + TOGETHER * 2 * len(weights),)),
            pltpu.SemaphoreType.DMA((5 + 2 * TOGETHER,)),
        ],
        input_output_aliases={len(operands) + i: i for i in range(len(held))},
        compiler_params=pltpu.CompilerParams(vmem_limit_bytes=VMEM),
        cost_estimate=cost(9),
    )(*operands, *held)


def self_kernel(
    heads, info_ref, q_ref, do_ref, ko_ref, vo_ref, one_ref, two_ref, three_ref, *refs
):
    own_ref, own_grad, back_ref, back_grad, *refs = refs
    out_ref, dq_ref, cross_ref, dk_ref, dv_ref, stat_ref = refs
    first_half = pl.program_id(0) < pl.num_programs(0) // 2
    crossed = jnp.where(first_half, own_ref[...], back_ref[...])
    cross_ref[...] = jnp.where(first_half, own_grad[...], back_grad[...])
    odd = info_ref[1] % 2 == 1
    keys_before = jnp.where(odd, one_ref[...], two_ref[...])
    values_before = jnp.where(odd, two_ref[...], three_ref[...])
    later = info_ref[1] > 0
    tokens = q_ref.shape[0]
    half = tokens // 2
    key_at = lax.broadcasted_iota(jnp.int32, (half, half), 0)
    query_at = lax.broadcasted_iota(jnp.int32, (half, half), 1)
    above = jnp.logical_and(key_at > query_at, later)
    below = key_at <= query_at
    zero = jnp.zeros((half, half), BF)
    lo, hi = slice(0, half), slice(half, None)

    def first(head):
        at = slice(head * HD, (head + 1) * HD)
        queries, grads = q_ref[:, at], do_ref[:, at]
        kp, vp = keys_before[:, at], values_before[:, at]
        ko, vo = ko_ref[:, at], vo_ref[:, at]
        return (
            (queries, grads, kp, vp, ko, vo),
            (mm(kp, queries, NT), mm(ko, queries, NT)),
            (mm(vp, grads, NT), mm(vo, grads, NT)),
        )

    def second(head, state):
        inputs, (sp, so), (gp, go) = state
        rows = []
        for a in (0, 1):
            if a == 0:
                blocks = (sp[lo, lo], sp[hi, lo], so[lo, lo])
                pgrads = (gp[lo, lo], gp[hi, lo], go[lo, lo])
                middle = jnp.where(later, blocks[1], NEG)
            else:
                blocks = (sp[hi, hi], so[lo, hi], so[hi, hi])
                pgrads = (gp[hi, hi], go[lo, hi], go[hi, hi])
                middle = blocks[1]
            scores = (jnp.where(above, blocks[0], NEG), middle, jnp.where(below, blocks[2], NEG))
            peak = jnp.max(
                jnp.maximum(jnp.maximum(scores[0], scores[1]), scores[2]), axis=0, keepdims=True
            )
            weight = [jnp.exp2((s - peak) * (SCALE * LOG2E)) for s in scores]
            total = jnp.sum(weight[0] + weight[1] + weight[2], axis=0, keepdims=True)
            inverse = 1.0 / total
            probs = [w * inverse for w in weight]
            delta = jnp.sum(
                probs[0] * pgrads[0] + probs[1] * pgrads[1] + probs[2] * pgrads[2],
                axis=0,
                keepdims=True,
            )
            score_grad = [(p * (g - delta)).astype(BF) for p, g in zip(probs, pgrads)]
            rows.append(([p.astype(BF) for p in probs], score_grad))
            lanes = slice(a * half, (a + 1) * half)
            stat_ref[head, 0:1, lanes] = peak * (SCALE * LOG2E) + jnp.log2(total)
            stat_ref[head, 1:2, lanes] = delta

        def spread(which):
            one, two = rows[0][which], rows[1][which]
            before = jnp.concatenate(
                [jnp.concatenate([one[0], zero], 1), jnp.concatenate([one[1], two[0]], 1)], 0
            )
            own = jnp.concatenate(
                [jnp.concatenate([one[2], two[1]], 1), jnp.concatenate([zero, two[2]], 1)], 0
            )
            return before, own

        return inputs, spread(0), spread(1)

    def third(head, state):
        at = slice(head * HD, (head + 1) * HD)
        (queries, grads, kp, vp, ko, vo), (pp, po), (dp, do) = state
        out = mm(pp, vp, TN) + mm(po, vo, TN) + crossed[:, at].astype(F32)
        out_ref[:, at] = out.astype(BF)
        dq_ref[:, at] = ((mm(dp, kp, TN) + mm(do, ko, TN)) * SCALE).astype(BF)
        dk_ref[:, at] = mm(do, queries, NN) * SCALE
        dv_ref[:, at] = mm(po, grads, NN)

    ready = first(0)
    for head in range(heads):
        upcoming = first(head + 1) if head + 1 < heads else None
        third(head, second(head, ready))
        ready = upcoming


def self_part(info, q, do, k, v, one, two, three, own, back):
    heads = 4
    tokens, width = q.shape
    steps = width // (heads * HD)
    half = steps // 2
    shape = (tokens, heads * HD)

    def place(p, info):
        return (p + (info[0] & 1) * half) % steps

    spec = pl.BlockSpec(shape, lambda p, info: (0, place(p, info)))
    own_spec = pl.BlockSpec(shape, lambda p, info: (0, jnp.minimum(p, half - 1)))
    back_spec = pl.BlockSpec(shape, lambda p, info: (0, jnp.maximum(p - half, 0)))
    stat_spec = pl.BlockSpec((heads, 2, tokens), lambda p, info: (place(p, info), 0, 0))
    full = jax.ShapeDtypeStruct(q.shape, BF)
    wide = jax.ShapeDtypeStruct(q.shape, F32)
    stats = jax.ShapeDtypeStruct((width // HD, 2, tokens), F32)
    return pl.pallas_call(
        functools.partial(self_kernel, heads),
        grid_spec=pltpu.PrefetchScalarGridSpec(
            num_scalar_prefetch=1,
            grid=(steps,),
            in_specs=[spec] * 7 + [own_spec] * 2 + [back_spec] * 2,
            out_specs=[spec] * 5 + [stat_spec],
        ),
        out_shape=[full] * 3 + [wide] * 2 + [stats],
        compiler_params=pltpu.CompilerParams(vmem_limit_bytes=VMEM),
        cost_estimate=cost(14),
    )(info, q, do, k, v, one, two, three, *own, *back)


def next_kernel(
    heads, info_ref, one_ref, three_ref, do_ref, k_ref, v_ref, stat_ref, dkp_ref, dvp_ref,
    dk_ref, dv_ref,
):
    all_queries = jnp.where(info_ref[1] % 2 == 1, three_ref[...], one_ref[...])
    tokens = do_ref.shape[0]
    half = tokens // 2
    key_at = lax.broadcasted_iota(jnp.int32, (half, half), 0)
    query_at = lax.broadcasted_iota(jnp.int32, (half, half), 1)
    above = key_at > query_at
    zero = jnp.zeros((half, half), BF)
    lo, hi = slice(0, half), slice(half, None)

    def first(head):
        at = slice(head * HD, (head + 1) * HD)
        queries, grads = all_queries[:, at], do_ref[:, at]
        return queries, grads, mm(k_ref[:, at], queries, NT), mm(v_ref[:, at], grads, NT)

    def second(head, state):
        at = slice(head * HD, (head + 1) * HD)
        queries, grads, scores, prob_grad = state
        level, delta = stat_ref[head, 0:1, :], stat_ref[head, 1:2, :]

        def block(rows, lanes, mask):
            exponent = scores[rows, lanes] * (SCALE * LOG2E) - level[:, lanes]
            if mask:
                exponent = jnp.where(above, exponent, NEG)
            probs = jnp.exp2(exponent)
            return probs.astype(BF), (probs * (prob_grad[rows, lanes] - delta[:, lanes])).astype(BF)

        one, middle, last = block(lo, lo, True), block(hi, lo, False), block(hi, hi, True)
        low, score_grad = [
            jnp.concatenate(
                [
                    jnp.concatenate([one[i], zero], 1),
                    jnp.concatenate([middle[i], last[i]], 1),
                ],
                0,
            )
            for i in (0, 1)
        ]
        dk_ref[:, at] = (dkp_ref[:, at] + mm(score_grad, queries, NN) * SCALE).astype(BF)
        dv_ref[:, at] = (dvp_ref[:, at] + mm(low, grads, NN)).astype(BF)

    ready = first(0)
    for head in range(heads):
        upcoming = first(head + 1) if head + 1 < heads else None
        second(head, ready)
        ready = upcoming


def next_part(info, one, three, do, k, v, stats, dk, dv):
    heads = 8
    tokens, width = k.shape
    spec = pl.BlockSpec((tokens, heads * HD), lambda p: (0, p))
    stat_spec = pl.BlockSpec((heads, 2, tokens), lambda p: (p, 0, 0))
    full = jax.ShapeDtypeStruct(k.shape, BF)
    return pl.pallas_call(
        functools.partial(next_kernel, heads),
        grid=(width // (heads * HD),),
        in_specs=[pl.BlockSpec(memory_space=pltpu.SMEM)]
        + [spec] * 5
        + [stat_spec]
        + [spec] * 2,
        out_specs=[spec] * 2,
        out_shape=[full] * 2,
        compiler_params=pltpu.CompilerParams(vmem_limit_bytes=VMEM),
        cost_estimate=cost(8),
    )(info, one, three, do, k, v, stats, dk, dv)


def halving_order(fsdp, seq):
    bits = [("fsdp", 1 << i) for i in range(1, fsdp.bit_length() - 1)]
    seq_bits = [("seq", 1 << i) for i in range(seq.bit_length() - 1)]
    return bits + seq_bits[1:] + seq_bits[:1]


def row_order(fsdp, seq, rows):
    index = np.arange(rows).reshape(seq * fsdp, -1)
    block = np.arange(seq * fsdp)
    keys = []
    for axis, bit in halving_order(fsdp, seq) + [("fsdp", 1)]:
        value = block % fsdp if axis == "fsdp" else block // fsdp
        keys.append((value // bit) % 2)
    order = np.lexsort(keys[::-1])
    return index[order].reshape(-1)


def take_half(value, upper):
    half = value.shape[0] // 2
    return lax.dynamic_slice_in_dim(value, upper * half, half, 0)


def halve_kernel(spans, axis, bit, info_ref, *refs):
    sources, (mine_ref, other_ref) = refs[:-2], refs[-2:]
    count = len(sources) // 2
    half = mine_ref.shape[0]
    upper = (info_ref[0 if axis == "fsdp" else 1] // bit) % 2
    for ref, which in ((mine_ref, upper), (other_ref, 1 - upper)):
        at = pl.ds(pl.multiple_of(which * half, 16), half)
        start = 0
        for keep, got, parts in zip(sources[:count], sources[count:], spans):
            width = keep.shape[-1]
            for part in range(parts):
                where = (part, at) if len(keep.shape) == 3 else (at,)
                total = keep[where].astype(F32) + got[where].astype(F32)
                ref[:, start : start + width] = total.astype(BF)
                start += width


def halve(info, keeps, received, stage):
    axis, bit = stage
    spans = [x.shape[0] if x.ndim == 3 else 1 for x in keeps]
    rows = keeps[0].shape[-2]
    width = sum(parts * x.shape[-1] for parts, x in zip(spans, keeps))
    if rows // 2 % 16:
        upper = (info[0 if axis == "fsdp" else 1] // bit) % 2
        sums = [
            (x.astype(F32) + y.astype(F32)).reshape(-1, rows, x.shape[-1])
            for x, y in zip(keeps, received)
        ]
        total = jnp.concatenate([part for x in sums for part in x], -1)
        return take_half(total, upper).astype(BF), take_half(total, 1 - upper).astype(BF)
    return pl.pallas_call(
        functools.partial(halve_kernel, spans, axis, bit),
        in_specs=[pl.BlockSpec(memory_space=pltpu.SMEM)]
        + [pl.BlockSpec(memory_space=pltpu.VMEM)] * (2 * len(keeps)),
        out_shape=[jax.ShapeDtypeStruct((rows // 2, width), BF)] * 2,
        compiler_params=pltpu.CompilerParams(vmem_limit_bytes=VMEM),
        cost_estimate=cost(1),
    )(info, *keeps, *received)


def on_device(
    self_query, self_key, self_value, cross_query, neighbours, neighbour_count, kv_weight, out_grad
):
    fsdp, seq = lax.axis_size("fsdp"), lax.axis_size("seq")
    shard, slab = lax.axis_index("fsdp"), lax.axis_index("seq")
    q, k, v, cq, do = (x[0] for x in (self_query, self_key, self_value, cross_query, out_grad))
    nb, counts = neighbours[0], neighbour_count[0]
    tokens, width = q.shape
    groups, per, enc = nb.shape
    info = jnp.stack([shard, slab]).astype(jnp.int32)

    last = pack(nb, counts)
    nb_last = shift(last, "seq", 1)

    nb_peer = swap(nb, "fsdp", 1)
    mine, other, pair = cut(after(info, last, nb_peer), counts, kv_weight, cq, do)
    near = swap(other, "fsdp", 1)
    weights = [
        [here, near, *[swap(x, "fsdp", piece) for piece in range(2, fsdp, 2)]]
        for here, x in zip(mine, stack(mine, near))
    ]
    peer = swap(pair, "fsdp", 1)

    even = slab % 2 == 0

    def pick(when_even, when_odd, *others):
        return jnp.where(after(even, nb_last, *others), when_even, when_odd)

    def hop(value):
        odds = [(i, i + 2) for i in range(1, seq - 2, 2)]
        return lax.ppermute(value, "seq", odds + [(i, i - 2) for i in range(2, seq, 2)])

    far_one = hop(pick(q, k))
    one = swap(pick(k, q), "seq", 1)
    far_two = hop(pick(do, v))

    nb_last = after(nb_last, peer)
    peer_last = swap(nb_last, "fsdp", 1)
    nbs = [nb_last, nb, peer_last, nb_peer]

    stages = halving_order(fsdp, seq)
    split_at = fsdp.bit_length() - 2

    turn = jnp.asarray(np.eye(enc)[row_order(fsdp, seq, enc)], BF)
    held, pairs = [], []
    for group in range(CHUNKS // TOGETHER):
        results = cross(group, info, counts, turn, nbs, weights[group], cq, do, peer, held)
        held, (keep, send) = results[:4], results[4:6]
        if not group:
            turn = results[6]
            second_load = pick(v, far_one, turn)
            two = swap(second_load, "seq", 1)
        received = swap(send, *stages[0])
        for stage in range(1, split_at):
            keep, send = halve(info, [keep], [received], stages[stage])
            received = swap(send, *stages[stage])
        pairs.append((keep, received))
    own = held[:2]
    back = [swap(x, "fsdp", 1) for x in after(held[2:], pairs[0][1], one, two)]
    third = pick(far_one, far_two, pairs[-1][0], second_load)
    three = swap(third, "seq", 1)

    halves = [halve(info, [pairs[0][0]], [pairs[0][1]], stages[split_at])]
    got = [swap(halves[0][1], *stages[split_at])]
    halves.append(
        halve(after(info, halves[0][1], *back), [pairs[1][0]], [pairs[1][1]], stages[split_at])
    )
    got.append(swap(halves[1][1], *stages[split_at]))
    four = swap(pick(far_two, do, halves[1][1], third), "seq", 1)
    keeps = [keep for keep, _ in halves]
    keep, send = halve(info, keeps, got, stages[split_at + 1])
    keeps, got = [keep], [swap(send, *stages[split_at + 1])]
    block_out, query_grad, cross_grad, dk, dv, stats = self_part(
        after(info, send), q, do, k, v, one, two, three, own, back
    )
    stats_after = shift(stats, "seq", -1)
    key_grad, value_grad = next_part(info, one, three, four, k, v, stats_after, dk, dv)

    for stage in range(split_at + 2, len(stages)):
        keep, send = halve(after(info, stats), keeps, got, stages[stage])
        keeps, got = [keep], [swap(send, *stages[stage])]
    total = keeps[0].astype(F32) + after(got[0], key_grad).astype(F32)
    core = shard % 2
    away = swap(take_half(total, 1 - core).astype(BF), "fsdp", 1).astype(F32)
    nearby = take_half(total, core)
    key_mine, key_away, value_mine, value_away = [
        jnp.concatenate(
            [x[:, (2 * c + part) * PAIR : (2 * c + part + 1) * PAIR] for c in range(CHUNKS)], -1
        )
        for part in (0, 1)
        for x in (nearby, away)
    ]
    low = shard % 2 == 0
    weight_grad = jnp.concatenate(
        [
            jnp.where(low, key_mine, key_away),
            jnp.where(low, key_away, key_mine),
            jnp.where(low, value_mine, value_away),
            jnp.where(low, value_away, value_mine),
        ],
        -1,
    )

    return (
        block_out[None],
        query_grad[None],
        key_grad[None],
        value_grad[None],
        cross_grad[None],
        weight_grad,
    )


def solution(mesh):
    in_specs = (
        P("fsdp", "seq", None),
        P("fsdp", "seq", None),
        P("fsdp", "seq", None),
        P("fsdp", "seq", None),
        P("fsdp", "seq", None, None),
        P("fsdp", "seq"),
        P("fsdp", None),
        P("fsdp", "seq", None),
    )
    out_specs = (
        P("fsdp", "seq", None),
        P("fsdp", "seq", None),
        P("fsdp", "seq", None),
        P("fsdp", "seq", None),
        P("fsdp", "seq", None),
        P(("seq", "fsdp"), None),
    )
    return jax.shard_map(
        on_device, mesh=mesh, in_specs=in_specs, out_specs=out_specs, check_vma=False
    )
```

```python
import functools

import numpy as np
import jax
import jax.numpy as jnp
from jax import lax
from jax.experimental import pallas as pl
from jax.experimental.pallas import tpu as pltpu
from jax.sharding import PartitionSpec as P

HEADS = 16
HD = 128
GROUP = 64
RLEN = 128
PAIR = 2 * HD
CHUNKS = HEADS // 4
TOGETHER = 2
VMEM = 60 * 2**20
SCALE = HD ** (-0.5)
LOG2E = 1.4426950408889634
NEG = -1e30
BF = jnp.bfloat16
F32 = jnp.float32
ANY = pl.BlockSpec(memory_space=pl.ANY)

NT = (((1,), (1,)), ((), ()))
TN = (((0,), (0,)), ((), ()))
NN = (((1,), (0,)), ((), ()))


def cost(micros):
    return pl.CostEstimate(flops=int(micros * 1e9), bytes_accessed=1000, transcendentals=0)


def mm(a, b, dims):
    return lax.dot_general(a, b, dims, preferred_element_type=F32)


def shift(value, axis, steps):
    count = lax.axis_size(axis)
    first, last = max(0, -steps), min(count, count - steps)
    return lax.ppermute(value, axis, [(i, i + steps) for i in range(first, last)])


def after(value, *others):
    return lax.optimization_barrier((value, *others))[0]


def swap(value, axis, bit):
    return lax.ppermute(value, axis, [(i, i ^ bit) for i in range(lax.axis_size(axis))])


def count_rows(count_ref, width):
    row = lax.broadcasted_iota(jnp.int32, (16, width), 0)
    tail = jnp.zeros((16, width), F32)
    for u in range(count_ref.shape[0]):
        tail = jnp.where(row == u, count_ref[u].astype(F32), tail)
    return tail.astype(BF)


def pack_kernel(count_ref, nb_ref, out_ref):
    per, enc = nb_ref.shape[1:]
    out_ref[:per, :] = nb_ref[0]
    out_ref[per:, :] = count_rows(count_ref, enc)


def pack(nb, counts):
    groups, per, enc = nb.shape
    return pl.pallas_call(
        pack_kernel,
        grid=(1,),
        in_specs=[
            pl.BlockSpec(memory_space=pltpu.SMEM),
            pl.BlockSpec((1, per, enc), lambda p: (groups - 1, 0, 0)),
        ],
        out_specs=pl.BlockSpec((per + 16, enc), lambda p: (0, 0)),
        out_shape=jax.ShapeDtypeStruct((per + 16, enc), BF),
        compiler_params=pltpu.CompilerParams(vmem_limit_bytes=VMEM),
        cost_estimate=cost(2),
    )(counts, nb)


def cut_kernel(info_ref, count_ref, *refs):
    sources, parts, other_ref, pair_ref = refs[:6], refs[6:-2], refs[-2], refs[-1]
    for which in (0, 1):
        keys, values = sources[2 * which : 2 * which + 2]
        for chunk in range(CHUNKS):
            at = slice(chunk * PAIR, (chunk + 1) * PAIR)
            ref = other_ref if which else parts[chunk // TOGETHER]
            where = chunk if which else chunk % TOGETHER
            ref[where, :, :PAIR] = keys[:, at]
            ref[where, :, PAIR:] = values[:, at]
    tokens, width = sources[4].shape
    for index in (0, 1):
        pair_ref[index, :tokens, :] = sources[4 + index][...]
        pair_ref[index, tokens:, :] = count_rows(count_ref, width)


def cut(info, counts, weight, cq, do):
    rows = weight.shape[0]
    tokens, width = cq.shape
    count = CHUNKS // TOGETHER
    part = jax.ShapeDtypeStruct((TOGETHER, rows, 2 * PAIR), BF)
    parts = jax.ShapeDtypeStruct((CHUNKS, rows, 2 * PAIR), BF)
    half = jax.ShapeDtypeStruct((2, tokens + 16, width // 2), BF)

    def columns(height, other, value):
        return pl.BlockSpec(
            (height, width // 2), lambda p, info: (0, 2 * value + ((info[0] & 1) ^ other))
        )

    *mine, other, pair = pl.pallas_call(
        cut_kernel,
        grid_spec=pltpu.PrefetchScalarGridSpec(
            num_scalar_prefetch=1,
            grid=(1,),
            in_specs=[pl.BlockSpec(memory_space=pltpu.SMEM)]
            + [columns(rows, other, value) for other in (0, 1) for value in (0, 1)]
            + [columns(tokens, 1, 0)] * 2,
            out_specs=[
                pl.BlockSpec(x.shape, lambda p, info: (0, 0, 0))
                for x in [part] * count + [parts, half]
            ],
        ),
        out_shape=[part] * count + [parts, half],
        compiler_params=pltpu.CompilerParams(vmem_limit_bytes=VMEM),
        cost_estimate=cost(3),
    )(info, counts, weight, weight, weight, weight, cq, do)
    return mine, other, pair


def stack_kernel(*refs):
    count = CHUNKS // TOGETHER
    mine, near_ref, outs = refs[:count], refs[count], refs[count + 1 :]
    rows = near_ref.shape[1]
    for group, (ref, out) in enumerate(zip(mine, outs)):
        out[:, :rows, :] = ref[...]
        out[:, rows:, :] = near_ref[group * TOGETHER : (group + 1) * TOGETHER]


def stack(mine, near):
    together, rows, width = mine[0].shape
    return pl.pallas_call(
        stack_kernel,
        out_shape=[jax.ShapeDtypeStruct((together, 2 * rows, width), BF)] * len(mine),
        compiler_params=pltpu.CompilerParams(vmem_limit_bytes=VMEM),
        cost_estimate=cost(2),
    )(*mine, near)


def cross_kernel(group, turns, pieces, held, info_ref, count_ref, *refs):
    (turn_ref, nb_last, nb_own, peer_last, nb_peer), refs = refs[:5], refs[5:]
    weights, refs = refs[:pieces], refs[pieces:]
    (cq_ref, do_ref, peer_ref), refs = refs[:3], refs[3 + held :]
    token_outs, (keep_out, send_out), refs = refs[:4], refs[4:6], refs[6:]
    turned_out, refs = (refs[0], refs[1:]) if turns else (None, refs)
    (w_ref, nb_ref, turned_ref, kv_ref, dkv_ref, q_ref, g_ref, tail_ref), refs = refs[:8], refs[8:]
    out_ref, dw_ref, pick_ref, sem, out_sem = refs
    shard = info_ref[0]
    enc = nb_ref.shape[1]
    tokens = q_ref.shape[1]
    groups = tokens // GROUP
    per = 2 * RLEN
    size = groups * per
    rows = weights[0].shape[1]
    wide = TOGETHER * PAIR
    loads, stores = [], []

    def load(source, target):
        copy = pltpu.make_async_copy(source, target, sem.at[len(loads)])
        copy.start()
        loads.append(copy)
        return copy

    def store(source, target):
        copy = pltpu.make_async_copy(source, target, out_sem.at[len(stores)])
        copy.start()
        stores.append(copy)

    def load_weight(index):
        sources = [weights[0].at[index], weights[1].at[group * TOGETHER + index]]
        for ref in weights[2:]:
            sources += [ref.at[index, :rows, :], ref.at[index, rows:, :]]
        waits = []
        for piece, source in enumerate(sources):
            at = pl.ds(pl.multiple_of((shard ^ piece) * rows, 16), rows)
            waits.append(load(source, w_ref.at[index, at, :]))
        return waits

    waits_w = [load_weight(0)]
    waits_nb = [
        load(nb_last.at[:per, :], nb_ref.at[:per, :]),
        *[load(nb_own.at[u - 1], nb_ref.at[u * per : (u + 1) * per, :]) for u in range(1, groups)],
        load(peer_last.at[:per, :], nb_ref.at[size : size + per, :]),
        *[
            load(nb_peer.at[u - 1], nb_ref.at[size + u * per : size + (u + 1) * per, :])
            for u in range(1, groups)
        ],
    ]
    lanes = pl.ds(pl.multiple_of(((shard & 1) * CHUNKS + group * TOGETHER) * PAIR, PAIR), wide)
    there = slice(group * wide, (group + 1) * wide)
    waits_q = [
        load(cq_ref.at[:, lanes], q_ref.at[0]),
        load(do_ref.at[:, lanes], g_ref.at[0]),
        load(peer_ref.at[0, :tokens, there], q_ref.at[1]),
        load(peer_ref.at[1, :tokens, there], g_ref.at[1]),
        load(nb_last.at[per:, : 2 * GROUP], tail_ref.at[0]),
        load(peer_last.at[per:, : 2 * GROUP], tail_ref.at[1]),
        load(peer_ref.at[0, tokens:, : 2 * GROUP], tail_ref.at[2]),
    ]
    wait_turn = load(turn_ref, pick_ref if turns else turned_ref)
    for index in range(1, TOGETHER):
        waits_w.append(load_weight(index))

    def project(index):
        for copy in waits_w[index]:
            copy.wait()
        for file in (0, 1):
            for start, stop in ((0, 1), (1, groups)):
                if index == 0:
                    for copy in waits_nb[file * groups + start : file * groups + stop]:
                        copy.wait()
                at = slice(file * size + start * per, file * size + stop * per)
                kv_ref[index, at, :] = mm(nb_ref[at, :], w_ref[index], NN).astype(BF)

    zero = jnp.zeros((GROUP, HD), BF)

    def diagonal(block):
        return jnp.concatenate(
            [
                jnp.concatenate([block[:, :HD], zero], 1),
                jnp.concatenate([zero, block[:, HD:]], 1),
            ],
            0,
        )

    row = lax.broadcasted_iota(jnp.int32, (per, 2 * GROUP), 0).astype(F32)

    def first(index, file, u):
        unit = file * groups + u
        at = slice(unit * per, (unit + 1) * per)
        tok = slice(u * GROUP, (u + 1) * GROUP)
        cols = slice(index * PAIR, (index + 1) * PAIR)
        keys, values = kv_ref[index, at, :PAIR], kv_ref[index, at, PAIR:]
        queries, grads = diagonal(q_ref[file, tok, cols]), diagonal(g_ref[file, tok, cols])
        return keys, values, queries, grads, mm(keys, queries, NT), mm(values, grads, NT)

    def second(index, file, u, state):
        keys, values, queries, grads, scores, prob_grad = state
        if u == 0:
            count = tail_ref[file, groups - 1 : groups, :].astype(F32)
        elif file:
            count = tail_ref[2, u - 1 : u, :].astype(F32)
        else:
            count = count_ref[u - 1].astype(F32)
        scores = jnp.where(row < count * RLEN, scores, NEG)
        peak = jnp.max(scores, axis=0, keepdims=True)
        weight = jnp.exp2((scores - peak) * (SCALE * LOG2E))
        total = jnp.sum(weight, axis=0, keepdims=True)
        inverse = jnp.where(count > 0, 1.0 / total, 0.0)
        probs = weight * inverse
        delta = jnp.sum(probs * prob_grad, axis=0, keepdims=True)
        score_grad = (probs * (prob_grad - delta)).astype(BF)
        return keys, values, queries, grads, probs.astype(BF), score_grad

    def third(index, file, u, state):
        keys, values, queries, grads, low, score_grad = state
        unit = file * groups + u
        at = slice(unit * per, (unit + 1) * per)
        tok = slice(u * GROUP, (u + 1) * GROUP)
        out = mm(low, values, TN).astype(BF)
        dq = (mm(score_grad, keys, TN) * SCALE).astype(BF)
        for which, value in enumerate((out, dq)):
            out_ref[file, which, tok, index * PAIR : index * PAIR + HD] = value[:GROUP, :HD]
            out_ref[file, which, tok, index * PAIR + HD : (index + 1) * PAIR] = value[GROUP:, HD:]
        dkv_ref[index, at, :PAIR] = (mm(score_grad, queries, NN) * SCALE).astype(BF)
        dkv_ref[index, at, PAIR:] = mm(low, grads, NN).astype(BF)

    half = enc // 2
    bit = (shard // 2) % 2

    def weigh(index, targets):
        for slot, target, which in targets:
            at = pl.ds(pl.multiple_of(which * half, 16), half)
            dw_ref[slot, index] = mm(turned_ref[at, :], dkv_ref[index], NN).astype(BF)
            store(dw_ref.at[slot, index], target.at[index])

    both = ((0, send_out, 1 - bit), (1, keep_out, bit))
    project(0)
    for copy in waits_q:
        copy.wait()
    for index in range(TOGETHER):
        units = [(index, file, u) for file in (0, 1) for u in range(groups)]
        ready, late = first(*units[0]), None
        for number, unit in enumerate(units):
            upcoming = first(*units[number + 1]) if number + 1 < len(units) else None
            done = second(*unit, ready)
            if late:
                third(*late)
            ready, late = upcoming, (*unit, done)
        third(*late)
        if index + 1 < TOGETHER:
            project(index + 1)
        if index == 0:
            wait_turn.wait()
            if turns:
                turned_ref[...] = mm(pick_ref[...], nb_ref[...], NT).astype(BF)
                store(turned_ref, turned_out)
        if index + 1 == TOGETHER:
            for which, target in enumerate(token_outs):
                store(out_ref.at[which // 2, which % 2], target.at[:, there])
        weigh(index, both)
    for copy in stores:
        copy.wait()


def cross(group, info, counts, turn, nbs, weights, cq, do, peer, held):
    tokens, half = peer.shape[1] - 16, peer.shape[2]
    groups, per, enc = nbs[1].shape
    size = 2 * groups * per
    turns = group == 0
    smem = pl.BlockSpec(memory_space=pltpu.SMEM)
    operands = [info, counts, turn, *nbs, *weights, cq, do, peer]
    shapes = [jax.ShapeDtypeStruct((tokens, half), BF)] * 4
    shapes += [jax.ShapeDtypeStruct((TOGETHER, enc // 2, 2 * PAIR), BF)] * 2
    if turns:
        shapes.append(jax.ShapeDtypeStruct((enc, size), BF))
    return pl.pallas_call(
        functools.partial(cross_kernel, group, turns, len(weights), len(held)),
        in_specs=[smem, smem] + [ANY] * (len(operands) - 2 + len(held)),
        out_specs=[ANY] * len(shapes),
        out_shape=shapes,
        scratch_shapes=[
            pltpu.VMEM((TOGETHER, enc, 2 * PAIR), BF),
            pltpu.VMEM((size, enc), BF),
            pltpu.VMEM((enc, size), BF),
            pltpu.VMEM((TOGETHER, size, 2 * PAIR), BF),
            pltpu.VMEM((TOGETHER, size, 2 * PAIR), BF),
            pltpu.VMEM((2, tokens, TOGETHER * PAIR), BF),
            pltpu.VMEM((2, tokens, TOGETHER * PAIR), BF),
            pltpu.VMEM((3, 16, 2 * GROUP), BF),
            pltpu.VMEM((2, 2, tokens, TOGETHER * PAIR), BF),
            pltpu.VMEM((2, TOGETHER, enc // 2, 2 * PAIR), BF),
            pltpu.VMEM((enc, enc) if turns else (16, 128), BF),
            pltpu.SemaphoreType.DMA((2 * groups + 8 + TOGETHER * 2 * len(weights),)),
            pltpu.SemaphoreType.DMA((5 + 2 * TOGETHER,)),
        ],
        input_output_aliases={len(operands) + i: i for i in range(len(held))},
        compiler_params=pltpu.CompilerParams(vmem_limit_bytes=VMEM),
        cost_estimate=cost(9),
    )(*operands, *held)


def self_kernel(
    heads, info_ref, q_ref, do_ref, ko_ref, vo_ref, one_ref, two_ref, three_ref, *refs
):
    own_ref, own_grad, back_ref, back_grad, *refs = refs
    out_ref, dq_ref, cross_ref, dk_ref, dv_ref, stat_ref = refs
    first_half = pl.program_id(0) < pl.num_programs(0) // 2
    crossed = jnp.where(first_half, own_ref[...], back_ref[...])
    cross_ref[...] = jnp.where(first_half, own_grad[...], back_grad[...])
    odd = info_ref[1] % 2 == 1
    keys_before = jnp.where(odd, one_ref[...], two_ref[...])
    values_before = jnp.where(odd, two_ref[...], three_ref[...])
    later = info_ref[1] > 0
    tokens = q_ref.shape[0]
    half = tokens // 2
    key_at = lax.broadcasted_iota(jnp.int32, (half, half), 0)
    query_at = lax.broadcasted_iota(jnp.int32, (half, half), 1)
    above = jnp.logical_and(key_at > query_at, later)
    below = key_at <= query_at
    zero = jnp.zeros((half, half), BF)
    lo, hi = slice(0, half), slice(half, None)

    def first(head):
        at = slice(head * HD, (head + 1) * HD)
        queries, grads = q_ref[:, at], do_ref[:, at]
        kp, vp = keys_before[:, at], values_before[:, at]
        ko, vo = ko_ref[:, at], vo_ref[:, at]
        return (
            (queries, grads, kp, vp, ko, vo),
            (mm(kp, queries, NT), mm(ko, queries, NT)),
            (mm(vp, grads, NT), mm(vo, grads, NT)),
        )

    def second(head, state):
        inputs, (sp, so), (gp, go) = state
        rows = []
        for a in (0, 1):
            if a == 0:
                blocks = (sp[lo, lo], sp[hi, lo], so[lo, lo])
                pgrads = (gp[lo, lo], gp[hi, lo], go[lo, lo])
                middle = jnp.where(later, blocks[1], NEG)
            else:
                blocks = (sp[hi, hi], so[lo, hi], so[hi, hi])
                pgrads = (gp[hi, hi], go[lo, hi], go[hi, hi])
                middle = blocks[1]
            scores = (jnp.where(above, blocks[0], NEG), middle, jnp.where(below, blocks[2], NEG))
            peak = jnp.max(
                jnp.maximum(jnp.maximum(scores[0], scores[1]), scores[2]), axis=0, keepdims=True
            )
            weight = [jnp.exp2((s - peak) * (SCALE * LOG2E)) for s in scores]
            total = jnp.sum(weight[0] + weight[1] + weight[2], axis=0, keepdims=True)
            inverse = 1.0 / total
            probs = [w * inverse for w in weight]
            delta = jnp.sum(
                probs[0] * pgrads[0] + probs[1] * pgrads[1] + probs[2] * pgrads[2],
                axis=0,
                keepdims=True,
            )
            score_grad = [(p * (g - delta)).astype(BF) for p, g in zip(probs, pgrads)]
            rows.append(([p.astype(BF) for p in probs], score_grad))
            lanes = slice(a * half, (a + 1) * half)
            stat_ref[head, 0:1, lanes] = peak * (SCALE * LOG2E) + jnp.log2(total)
            stat_ref[head, 1:2, lanes] = delta

        def spread(which):
            one, two = rows[0][which], rows[1][which]
            before = jnp.concatenate(
                [jnp.concatenate([one[0], zero], 1), jnp.concatenate([one[1], two[0]], 1)], 0
            )
            own = jnp.concatenate(
                [jnp.concatenate([one[2], two[1]], 1), jnp.concatenate([zero, two[2]], 1)], 0
            )
            return before, own

        return inputs, spread(0), spread(1)

    def third(head, state):
        at = slice(head * HD, (head + 1) * HD)
        (queries, grads, kp, vp, ko, vo), (pp, po), (dp, do) = state
        out = mm(pp, vp, TN) + mm(po, vo, TN) + crossed[:, at].astype(F32)
        out_ref[:, at] = out.astype(BF)
        dq_ref[:, at] = ((mm(dp, kp, TN) + mm(do, ko, TN)) * SCALE).astype(BF)
        dk_ref[:, at] = mm(do, queries, NN) * SCALE
        dv_ref[:, at] = mm(po, grads, NN)

    ready = first(0)
    for head in range(heads):
        upcoming = first(head + 1) if head + 1 < heads else None
        third(head, second(head, ready))
        ready = upcoming


def self_part(info, q, do, k, v, one, two, three, own, back):
    heads = 4
    tokens, width = q.shape
    steps = width // (heads * HD)
    half = steps // 2
    shape = (tokens, heads * HD)

    def place(p, info):
        return (p + (info[0] & 1) * half) % steps

    spec = pl.BlockSpec(shape, lambda p, info: (0, place(p, info)))
    own_spec = pl.BlockSpec(shape, lambda p, info: (0, jnp.minimum(p, half - 1)))
    back_spec = pl.BlockSpec(shape, lambda p, info: (0, jnp.maximum(p - half, 0)))
    stat_spec = pl.BlockSpec((heads, 2, tokens), lambda p, info: (place(p, info), 0, 0))
    full = jax.ShapeDtypeStruct(q.shape, BF)
    wide = jax.ShapeDtypeStruct(q.shape, F32)
    stats = jax.ShapeDtypeStruct((width // HD, 2, tokens), F32)
    return pl.pallas_call(
        functools.partial(self_kernel, heads),
        grid_spec=pltpu.PrefetchScalarGridSpec(
            num_scalar_prefetch=1,
            grid=(steps,),
            in_specs=[spec] * 7 + [own_spec] * 2 + [back_spec] * 2,
            out_specs=[spec] * 5 + [stat_spec],
        ),
        out_shape=[full] * 3 + [wide] * 2 + [stats],
        compiler_params=pltpu.CompilerParams(vmem_limit_bytes=VMEM),
        cost_estimate=cost(14),
    )(info, q, do, k, v, one, two, three, *own, *back)


def next_kernel(
    heads, info_ref, one_ref, three_ref, do_ref, k_ref, v_ref, stat_ref, dkp_ref, dvp_ref,
    dk_ref, dv_ref,
):
    all_queries = jnp.where(info_ref[1] % 2 == 1, three_ref[...], one_ref[...])
    tokens = do_ref.shape[0]
    half = tokens // 2
    key_at = lax.broadcasted_iota(jnp.int32, (half, half), 0)
    query_at = lax.broadcasted_iota(jnp.int32, (half, half), 1)
    above = key_at > query_at
    zero = jnp.zeros((half, half), BF)
    lo, hi = slice(0, half), slice(half, None)

    def first(head):
        at = slice(head * HD, (head + 1) * HD)
        queries, grads = all_queries[:, at], do_ref[:, at]
        return queries, grads, mm(k_ref[:, at], queries, NT), mm(v_ref[:, at], grads, NT)

    def second(head, state):
        at = slice(head * HD, (head + 1) * HD)
        queries, grads, scores, prob_grad = state
        level, delta = stat_ref[head, 0:1, :], stat_ref[head, 1:2, :]

        def block(rows, lanes, mask):
            exponent = scores[rows, lanes] * (SCALE * LOG2E) - level[:, lanes]
            if mask:
                exponent = jnp.where(above, exponent, NEG)
            probs = jnp.exp2(exponent)
            return probs.astype(BF), (probs * (prob_grad[rows, lanes] - delta[:, lanes])).astype(BF)

        one, middle, last = block(lo, lo, True), block(hi, lo, False), block(hi, hi, True)
        low, score_grad = [
            jnp.concatenate(
                [
                    jnp.concatenate([one[i], zero], 1),
                    jnp.concatenate([middle[i], last[i]], 1),
                ],
                0,
            )
            for i in (0, 1)
        ]
        dk_ref[:, at] = (dkp_ref[:, at] + mm(score_grad, queries, NN) * SCALE).astype(BF)
        dv_ref[:, at] = (dvp_ref[:, at] + mm(low, grads, NN)).astype(BF)

    ready = first(0)
    for head in range(heads):
        upcoming = first(head + 1) if head + 1 < heads else None
        second(head, ready)
        ready = upcoming


def next_part(info, one, three, do, k, v, stats, dk, dv):
    heads = 8
    tokens, width = k.shape
    spec = pl.BlockSpec((tokens, heads * HD), lambda p: (0, p))
    stat_spec = pl.BlockSpec((heads, 2, tokens), lambda p: (p, 0, 0))
    full = jax.ShapeDtypeStruct(k.shape, BF)
    return pl.pallas_call(
        functools.partial(next_kernel, heads),
        grid=(width // (heads * HD),),
        in_specs=[pl.BlockSpec(memory_space=pltpu.SMEM)]
        + [spec] * 5
        + [stat_spec]
        + [spec] * 2,
        out_specs=[spec] * 2,
        out_shape=[full] * 2,
        compiler_params=pltpu.CompilerParams(vmem_limit_bytes=VMEM),
        cost_estimate=cost(8),
    )(info, one, three, do, k, v, stats, dk, dv)


def halving_order(fsdp, seq):
    bits = [("fsdp", 1 << i) for i in range(1, fsdp.bit_length() - 1)]
    seq_bits = [("seq", 1 << i) for i in range(seq.bit_length() - 1)]
    return bits + seq_bits[1:] + seq_bits[:1]


def row_order(fsdp, seq, rows):
    index = np.arange(rows).reshape(seq * fsdp, -1)
    block = np.arange(seq * fsdp)
    keys = []
    for axis, bit in halving_order(fsdp, seq) + [("fsdp", 1)]:
        value = block % fsdp if axis == "fsdp" else block // fsdp
        keys.append((value // bit) % 2)
    order = np.lexsort(keys[::-1])
    return index[order].reshape(-1)


def take_half(value, upper):
    half = value.shape[0] // 2
    return lax.dynamic_slice_in_dim(value, upper * half, half, 0)


def halve_kernel(spans, axis, bit, info_ref, *refs):
    sources, (mine_ref, other_ref) = refs[:-2], refs[-2:]
    count = len(sources) // 2
    half = mine_ref.shape[0]
    upper = (info_ref[0 if axis == "fsdp" else 1] // bit) % 2
    for ref, which in ((mine_ref, upper), (other_ref, 1 - upper)):
        at = pl.ds(pl.multiple_of(which * half, 16), half)
        start = 0
        for keep, got, parts in zip(sources[:count], sources[count:], spans):
            width = keep.shape[-1]
            for part in range(parts):
                where = (part, at) if len(keep.shape) == 3 else (at,)
                total = keep[where].astype(F32) + got[where].astype(F32)
                ref[:, start : start + width] = total.astype(BF)
                start += width


def halve(info, keeps, received, stage):
    axis, bit = stage
    spans = [x.shape[0] if x.ndim == 3 else 1 for x in keeps]
    rows = keeps[0].shape[-2]
    width = sum(parts * x.shape[-1] for parts, x in zip(spans, keeps))
    if rows // 2 % 16:
        upper = (info[0 if axis == "fsdp" else 1] // bit) % 2
        sums = [
            (x.astype(F32) + y.astype(F32)).reshape(-1, rows, x.shape[-1])
            for x, y in zip(keeps, received)
        ]
        total = jnp.concatenate([part for x in sums for part in x], -1)
        return take_half(total, upper).astype(BF), take_half(total, 1 - upper).astype(BF)
    return pl.pallas_call(
        functools.partial(halve_kernel, spans, axis, bit),
        in_specs=[pl.BlockSpec(memory_space=pltpu.SMEM)]
        + [pl.BlockSpec(memory_space=pltpu.VMEM)] * (2 * len(keeps)),
        out_shape=[jax.ShapeDtypeStruct((rows // 2, width), BF)] * 2,
        compiler_params=pltpu.CompilerParams(vmem_limit_bytes=VMEM),
        cost_estimate=cost(1),
    )(info, *keeps, *received)


def on_device(
    self_query, self_key, self_value, cross_query, neighbours, neighbour_count, kv_weight, out_grad
):
    fsdp, seq = lax.axis_size("fsdp"), lax.axis_size("seq")
    shard, slab = lax.axis_index("fsdp"), lax.axis_index("seq")
    q, k, v, cq, do = (x[0] for x in (self_query, self_key, self_value, cross_query, out_grad))
    nb, counts = neighbours[0], neighbour_count[0]
    tokens, width = q.shape
    groups, per, enc = nb.shape
    info = jnp.stack([shard, slab]).astype(jnp.int32)

    last = pack(nb, counts)
    nb_last = shift(last, "seq", 1)

    nb_peer = swap(nb, "fsdp", 1)
    mine, other, pair = cut(after(info, last), counts, kv_weight, cq, do)
    near = swap(other, "fsdp", 1)
    weights = [
        [here, near, *[swap(x, "fsdp", piece) for piece in range(2, fsdp, 2)]]
        for here, x in zip(mine, stack(mine, near))
    ]
    peer = swap(pair, "fsdp", 1)

    even = slab % 2 == 0

    def pick(when_even, when_odd, *others):
        return jnp.where(after(even, nb_last, *others), when_even, when_odd)

    def hop(value):
        odds = [(i, i + 2) for i in range(1, seq - 2, 2)]
        return lax.ppermute(value, "seq", odds + [(i, i - 2) for i in range(2, seq, 2)])

    far_one = hop(pick(q, k))
    one = swap(pick(k, q), "seq", 1)
    far_two = hop(pick(do, v))

    nb_last = after(nb_last, peer, nb_peer)
    peer_last = swap(nb_last, "fsdp", 1)
    nbs = [nb_last, nb, peer_last, nb_peer]

    stages = halving_order(fsdp, seq)
    split_at = fsdp.bit_length() - 2

    turn = jnp.asarray(np.eye(enc)[row_order(fsdp, seq, enc)], BF)
    held, pairs = [], []
    for group in range(CHUNKS // TOGETHER):
        results = cross(group, info, counts, turn, nbs, weights[group], cq, do, peer, held)
        held, (keep, send) = results[:4], results[4:6]
        if not group:
            turn = results[6]
            second_load = pick(v, far_one, turn)
            two = swap(second_load, "seq", 1)
        received = swap(send, *stages[0])
        for stage in range(1, split_at):
            keep, send = halve(info, [keep], [received], stages[stage])
            received = swap(send, *stages[stage])
        pairs.append((keep, received))
    own = held[:2]
    back = [swap(x, "fsdp", 1) for x in after(held[2:], pairs[0][1], one, two)]
    third = pick(far_one, far_two, pairs[-1][0], second_load)
    three = swap(third, "seq", 1)

    halves = [halve(info, [pairs[0][0]], [pairs[0][1]], stages[split_at])]
    got = [swap(halves[0][1], *stages[split_at])]
    halves.append(
        halve(after(info, halves[0][1], *back), [pairs[1][0]], [pairs[1][1]], stages[split_at])
    )
    got.append(swap(halves[1][1], *stages[split_at]))
    four = swap(pick(far_two, do, halves[1][1], third), "seq", 1)
    keeps = [keep for keep, _ in halves]
    keep, send = halve(info, keeps, got, stages[split_at + 1])
    keeps, got = [keep], [swap(send, *stages[split_at + 1])]
    block_out, query_grad, cross_grad, dk, dv, stats = self_part(
        after(info, send), q, do, k, v, one, two, three, own, back
    )
    stats_after = shift(stats, "seq", -1)
    key_grad, value_grad = next_part(info, one, three, four, k, v, stats_after, dk, dv)

    for stage in range(split_at + 2, len(stages)):
        keep, send = halve(after(info, stats), keeps, got, stages[stage])
        keeps, got = [keep], [swap(send, *stages[stage])]
    total = keeps[0].astype(F32) + after(got[0], key_grad).astype(F32)
    core = shard % 2
    away = swap(take_half(total, 1 - core).astype(BF), "fsdp", 1).astype(F32)
    nearby = take_half(total, core)
    key_mine, key_away, value_mine, value_away = [
        jnp.concatenate(
            [x[:, (2 * c + part) * PAIR : (2 * c + part + 1) * PAIR] for c in range(CHUNKS)], -1
        )
        for part in (0, 1)
        for x in (nearby, away)
    ]
    low = shard % 2 == 0
    weight_grad = jnp.concatenate(
        [
            jnp.where(low, key_mine, key_away),
            jnp.where(low, key_away, key_mine),
            jnp.where(low, value_mine, value_away),
            jnp.where(low, value_away, value_mine),
        ],
        -1,
    )

    return (
        block_out[None],
        query_grad[None],
        key_grad[None],
        value_grad[None],
        cross_grad[None],
        weight_grad,
    )


def solution(mesh):
    in_specs = (
        P("fsdp", "seq", None),
        P("fsdp", "seq", None),
        P("fsdp", "seq", None),
        P("fsdp", "seq", None),
        P("fsdp", "seq", None, None),
        P("fsdp", "seq"),
        P("fsdp", None),
        P("fsdp", "seq", None),
    )
    out_specs = (
        P("fsdp", "seq", None),
        P("fsdp", "seq", None),
        P("fsdp", "seq", None),
        P("fsdp", "seq", None),
        P("fsdp", "seq", None),
        P(("seq", "fsdp"), None),
    )
    return jax.shard_map(
        on_device, mesh=mesh, in_specs=in_specs, out_specs=out_specs, check_vma=False
    )
```

```python
import functools

import numpy as np
import jax
import jax.numpy as jnp
from jax import lax
from jax.experimental import pallas as pl
from jax.experimental.pallas import tpu as pltpu
from jax.sharding import PartitionSpec as P

HEADS = 16
HD = 128
GROUP = 64
RLEN = 128
PAIR = 2 * HD
CHUNKS = HEADS // 4
TOGETHER = 2
VMEM = 60 * 2**20
SCALE = HD ** (-0.5)
LOG2E = 1.4426950408889634
NEG = -1e30
BF = jnp.bfloat16
F32 = jnp.float32
ANY = pl.BlockSpec(memory_space=pl.ANY)

NT = (((1,), (1,)), ((), ()))
TN = (((0,), (0,)), ((), ()))
NN = (((1,), (0,)), ((), ()))


def cost(micros):
    return pl.CostEstimate(flops=int(micros * 1e9), bytes_accessed=1000, transcendentals=0)


def mm(a, b, dims):
    return lax.dot_general(a, b, dims, preferred_element_type=F32)


def shift(value, axis, steps):
    count = lax.axis_size(axis)
    first, last = max(0, -steps), min(count, count - steps)
    return lax.ppermute(value, axis, [(i, i + steps) for i in range(first, last)])


def after(value, *others):
    return lax.optimization_barrier((value, *others))[0]


def swap(value, axis, bit):
    return lax.ppermute(value, axis, [(i, i ^ bit) for i in range(lax.axis_size(axis))])


def count_rows(count_ref, width):
    row = lax.broadcasted_iota(jnp.int32, (16, width), 0)
    tail = jnp.zeros((16, width), F32)
    for u in range(count_ref.shape[0]):
        tail = jnp.where(row == u, count_ref[u].astype(F32), tail)
    return tail.astype(BF)


def pack_kernel(count_ref, nb_ref, out_ref):
    per, enc = nb_ref.shape[1:]
    out_ref[:per, :] = nb_ref[0]
    out_ref[per:, :] = count_rows(count_ref, enc)


def pack(nb, counts):
    groups, per, enc = nb.shape
    return pl.pallas_call(
        pack_kernel,
        grid=(1,),
        in_specs=[
            pl.BlockSpec(memory_space=pltpu.SMEM),
            pl.BlockSpec((1, per, enc), lambda p: (groups - 1, 0, 0)),
        ],
        out_specs=pl.BlockSpec((per + 16, enc), lambda p: (0, 0)),
        out_shape=jax.ShapeDtypeStruct((per + 16, enc), BF),
        compiler_params=pltpu.CompilerParams(vmem_limit_bytes=VMEM),
        cost_estimate=cost(2),
    )(counts, nb)


def cut_kernel(info_ref, count_ref, *refs):
    sources, parts, other_ref, pair_ref = refs[:6], refs[6:-2], refs[-2], refs[-1]
    for which in (0, 1):
        keys, values = sources[2 * which : 2 * which + 2]
        for chunk in range(CHUNKS):
            at = slice(chunk * PAIR, (chunk + 1) * PAIR)
            ref = other_ref if which else parts[chunk // TOGETHER]
            where = chunk if which else chunk % TOGETHER
            ref[where, :, :PAIR] = keys[:, at]
            ref[where, :, PAIR:] = values[:, at]
    tokens, width = sources[4].shape
    for index in (0, 1):
        pair_ref[index, :tokens, :] = sources[4 + index][...]
        pair_ref[index, tokens:, :] = count_rows(count_ref, width)


def cut(info, counts, weight, cq, do):
    rows = weight.shape[0]
    tokens, width = cq.shape
    count = CHUNKS // TOGETHER
    part = jax.ShapeDtypeStruct((TOGETHER, rows, 2 * PAIR), BF)
    parts = jax.ShapeDtypeStruct((CHUNKS, rows, 2 * PAIR), BF)
    half = jax.ShapeDtypeStruct((2, tokens + 16, width // 2), BF)

    def columns(height, other, value):
        return pl.BlockSpec(
            (height, width // 2), lambda p, info: (0, 2 * value + ((info[0] & 1) ^ other))
        )

    *mine, other, pair = pl.pallas_call(
        cut_kernel,
        grid_spec=pltpu.PrefetchScalarGridSpec(
            num_scalar_prefetch=1,
            grid=(1,),
            in_specs=[pl.BlockSpec(memory_space=pltpu.SMEM)]
            + [columns(rows, other, value) for other in (0, 1) for value in (0, 1)]
            + [columns(tokens, 1, 0)] * 2,
            out_specs=[
                pl.BlockSpec(x.shape, lambda p, info: (0, 0, 0))
                for x in [part] * count + [parts, half]
            ],
        ),
        out_shape=[part] * count + [parts, half],
        compiler_params=pltpu.CompilerParams(vmem_limit_bytes=VMEM),
        cost_estimate=cost(3),
    )(info, counts, weight, weight, weight, weight, cq, do)
    return mine, other, pair


def stack_kernel(*refs):
    count = CHUNKS // TOGETHER
    mine, near_ref, outs = refs[:count], refs[count], refs[count + 1 :]
    rows = near_ref.shape[1]
    for group, (ref, out) in enumerate(zip(mine, outs)):
        out[:, :rows, :] = ref[...]
        out[:, rows:, :] = near_ref[group * TOGETHER : (group + 1) * TOGETHER]


def stack(mine, near):
    together, rows, width = mine[0].shape
    return pl.pallas_call(
        stack_kernel,
        out_shape=[jax.ShapeDtypeStruct((together, 2 * rows, width), BF)] * len(mine),
        compiler_params=pltpu.CompilerParams(vmem_limit_bytes=VMEM),
        cost_estimate=cost(2),
    )(*mine, near)


def cross_kernel(group, turns, pieces, held, info_ref, count_ref, *refs):
    (turn_ref, nb_last, nb_own, peer_last, nb_peer), refs = refs[:5], refs[5:]
    weights, refs = refs[:pieces], refs[pieces:]
    (cq_ref, do_ref, peer_ref), refs = refs[:3], refs[3 + held :]
    token_outs, (keep_out, send_out), refs = refs[:4], refs[4:6], refs[6:]
    turned_out, refs = (refs[0], refs[1:]) if turns else (None, refs)
    (w_ref, nb_ref, turned_ref, kv_ref, dkv_ref, q_ref, g_ref, tail_ref), refs = refs[:8], refs[8:]
    out_ref, dw_ref, pick_ref, sem, out_sem = refs
    shard = info_ref[0]
    enc = nb_ref.shape[1]
    tokens = q_ref.shape[1]
    groups = tokens // GROUP
    per = 2 * RLEN
    size = groups * per
    rows = weights[0].shape[1]
    wide = TOGETHER * PAIR
    loads, stores = [], []

    def load(source, target):
        copy = pltpu.make_async_copy(source, target, sem.at[len(loads)])
        copy.start()
        loads.append(copy)
        return copy

    def store(source, target):
        copy = pltpu.make_async_copy(source, target, out_sem.at[len(stores)])
        copy.start()
        stores.append(copy)

    def load_weight(index):
        sources = [weights[0].at[index], weights[1].at[group * TOGETHER + index]]
        for ref in weights[2:]:
            sources += [ref.at[index, :rows, :], ref.at[index, rows:, :]]
        waits = []
        for piece, source in enumerate(sources):
            at = pl.ds(pl.multiple_of((shard ^ piece) * rows, 16), rows)
            waits.append(load(source, w_ref.at[index, at, :]))
        return waits

    waits_w = [load_weight(0)]
    waits_nb = [
        load(nb_last.at[:per, :], nb_ref.at[:per, :]),
        *[load(nb_own.at[u - 1], nb_ref.at[u * per : (u + 1) * per, :]) for u in range(1, groups)],
        load(peer_last.at[:per, :], nb_ref.at[size : size + per, :]),
        *[
            load(nb_peer.at[u - 1], nb_ref.at[size + u * per : size + (u + 1) * per, :])
            for u in range(1, groups)
        ],
    ]
    lanes = pl.ds(pl.multiple_of(((shard & 1) * CHUNKS + group * TOGETHER) * PAIR, PAIR), wide)
    there = slice(group * wide, (group + 1) * wide)
    waits_q = [
        load(cq_ref.at[:, lanes], q_ref.at[0]),
        load(do_ref.at[:, lanes], g_ref.at[0]),
        load(peer_ref.at[0, :tokens, there], q_ref.at[1]),
        load(peer_ref.at[1, :tokens, there], g_ref.at[1]),
        load(nb_last.at[per:, : 2 * GROUP], tail_ref.at[0]),
        load(peer_last.at[per:, : 2 * GROUP], tail_ref.at[1]),
        load(peer_ref.at[0, tokens:, : 2 * GROUP], tail_ref.at[2]),
    ]
    wait_turn = load(turn_ref, pick_ref if turns else turned_ref)
    for index in range(1, TOGETHER):
        waits_w.append(load_weight(index))

    def project(index):
        for copy in waits_w[index]:
            copy.wait()
        for file in (0, 1):
            for start, stop in ((0, 1), (1, groups)):
                if index == 0:
                    for copy in waits_nb[file * groups + start : file * groups + stop]:
                        copy.wait()
                at = slice(file * size + start * per, file * size + stop * per)
                kv_ref[index, at, :] = mm(nb_ref[at, :], w_ref[index], NN).astype(BF)

    zero = jnp.zeros((GROUP, HD), BF)

    def diagonal(block):
        return jnp.concatenate(
            [
                jnp.concatenate([block[:, :HD], zero], 1),
                jnp.concatenate([zero, block[:, HD:]], 1),
            ],
            0,
        )

    row = lax.broadcasted_iota(jnp.int32, (per, 2 * GROUP), 0).astype(F32)

    def first(index, file, u):
        unit = file * groups + u
        at = slice(unit * per, (unit + 1) * per)
        tok = slice(u * GROUP, (u + 1) * GROUP)
        cols = slice(index * PAIR, (index + 1) * PAIR)
        keys, values = kv_ref[index, at, :PAIR], kv_ref[index, at, PAIR:]
        queries, grads = diagonal(q_ref[file, tok, cols]), diagonal(g_ref[file, tok, cols])
        return keys, values, queries, grads, mm(keys, queries, NT), mm(values, grads, NT)

    def second(index, file, u, state):
        keys, values, queries, grads, scores, prob_grad = state
        if u == 0:
            count = tail_ref[file, groups - 1 : groups, :].astype(F32)
        elif file:
            count = tail_ref[2, u - 1 : u, :].astype(F32)
        else:
            count = count_ref[u - 1].astype(F32)
        scores = jnp.where(row < count * RLEN, scores, NEG)
        peak = jnp.max(scores, axis=0, keepdims=True)
        weight = jnp.exp2((scores - peak) * (SCALE * LOG2E))
        total = jnp.sum(weight, axis=0, keepdims=True)
        inverse = jnp.where(count > 0, 1.0 / total, 0.0)
        probs = weight * inverse
        delta = jnp.sum(probs * prob_grad, axis=0, keepdims=True)
        score_grad = (probs * (prob_grad - delta)).astype(BF)
        return keys, values, queries, grads, probs.astype(BF), score_grad

    def third(index, file, u, state):
        keys, values, queries, grads, low, score_grad = state
        unit = file * groups + u
        at = slice(unit * per, (unit + 1) * per)
        tok = slice(u * GROUP, (u + 1) * GROUP)
        out = mm(low, values, TN).astype(BF)
        dq = (mm(score_grad, keys, TN) * SCALE).astype(BF)
        for which, value in enumerate((out, dq)):
            out_ref[file, which, tok, index * PAIR : index * PAIR + HD] = value[:GROUP, :HD]
            out_ref[file, which, tok, index * PAIR + HD : (index + 1) * PAIR] = value[GROUP:, HD:]
        dkv_ref[index, at, :PAIR] = (mm(score_grad, queries, NN) * SCALE).astype(BF)
        dkv_ref[index, at, PAIR:] = mm(low, grads, NN).astype(BF)

    half = enc // 2
    bit = (shard // 2) % 2

    def weigh(index, targets):
        for slot, target, which in targets:
            at = pl.ds(pl.multiple_of(which * half, 16), half)
            dw_ref[slot, index] = mm(turned_ref[at, :], dkv_ref[index], NN).astype(BF)
            store(dw_ref.at[slot, index], target.at[index])

    both = ((0, send_out, 1 - bit), (1, keep_out, bit))
    project(0)
    for copy in waits_q:
        copy.wait()
    for index in range(TOGETHER):
        units = [(index, file, u) for file in (0, 1) for u in range(groups)]
        ready, late = first(*units[0]), None
        for number, unit in enumerate(units):
            upcoming = first(*units[number + 1]) if number + 1 < len(units) else None
            done = second(*unit, ready)
            if late:
                third(*late)
            ready, late = upcoming, (*unit, done)
        third(*late)
        if index + 1 < TOGETHER:
            project(index + 1)
        if index == 0:
            wait_turn.wait()
            if turns:
                turned_ref[...] = mm(pick_ref[...], nb_ref[...], NT).astype(BF)
                store(turned_ref, turned_out)
        if index + 1 == TOGETHER:
            for which, target in enumerate(token_outs):
                store(out_ref.at[which // 2, which % 2], target.at[:, there])
        weigh(index, both)
    for copy in stores:
        copy.wait()


def cross(group, info, counts, turn, nbs, weights, cq, do, peer, held):
    tokens, half = peer.shape[1] - 16, peer.shape[2]
    groups, per, enc = nbs[1].shape
    size = 2 * groups * per
    turns = group == 0
    smem = pl.BlockSpec(memory_space=pltpu.SMEM)
    operands = [info, counts, turn, *nbs, *weights, cq, do, peer]
    shapes = [jax.ShapeDtypeStruct((tokens, half), BF)] * 4
    shapes += [jax.ShapeDtypeStruct((TOGETHER, enc // 2, 2 * PAIR), BF)] * 2
    if turns:
        shapes.append(jax.ShapeDtypeStruct((enc, size), BF))
    return pl.pallas_call(
        functools.partial(cross_kernel, group, turns, len(weights), len(held)),
        in_specs=[smem, smem] + [ANY] * (len(operands) - 2 + len(held)),
        out_specs=[ANY] * len(shapes),
        out_shape=shapes,
        scratch_shapes=[
            pltpu.VMEM((TOGETHER, enc, 2 * PAIR), BF),
            pltpu.VMEM((size, enc), BF),
            pltpu.VMEM((enc, size), BF),
            pltpu.VMEM((TOGETHER, size, 2 * PAIR), BF),
            pltpu.VMEM((TOGETHER, size, 2 * PAIR), BF),
            pltpu.VMEM((2, tokens, TOGETHER * PAIR), BF),
            pltpu.VMEM((2, tokens, TOGETHER * PAIR), BF),
            pltpu.VMEM((3, 16, 2 * GROUP), BF),
            pltpu.VMEM((2, 2, tokens, TOGETHER * PAIR), BF),
            pltpu.VMEM((2, TOGETHER, enc // 2, 2 * PAIR), BF),
            pltpu.VMEM((enc, enc) if turns else (16, 128), BF),
            pltpu.SemaphoreType.DMA((2 * groups + 8 + TOGETHER * 2 * len(weights),)),
            pltpu.SemaphoreType.DMA((5 + 2 * TOGETHER,)),
        ],
        input_output_aliases={len(operands) + i: i for i in range(len(held))},
        compiler_params=pltpu.CompilerParams(vmem_limit_bytes=VMEM),
        cost_estimate=cost(9),
    )(*operands, *held)


def self_kernel(
    heads, info_ref, q_ref, do_ref, ko_ref, vo_ref, one_ref, two_ref, three_ref, *refs
):
    own_ref, own_grad, back_ref, back_grad, *refs = refs
    out_ref, dq_ref, cross_ref, dk_ref, dv_ref, stat_ref = refs
    first_half = pl.program_id(0) < pl.num_programs(0) // 2
    crossed = jnp.where(first_half, own_ref[...], back_ref[...])
    cross_ref[...] = jnp.where(first_half, own_grad[...], back_grad[...])
    odd = info_ref[1] % 2 == 1
    keys_before = jnp.where(odd, one_ref[...], two_ref[...])
    values_before = jnp.where(odd, two_ref[...], three_ref[...])
    later = info_ref[1] > 0
    tokens = q_ref.shape[0]
    half = tokens // 2
    key_at = lax.broadcasted_iota(jnp.int32, (half, half), 0)
    query_at = lax.broadcasted_iota(jnp.int32, (half, half), 1)
    above = jnp.logical_and(key_at > query_at, later)
    below = key_at <= query_at
    zero = jnp.zeros((half, half), BF)
    lo, hi = slice(0, half), slice(half, None)

    def first(head):
        at = slice(head * HD, (head + 1) * HD)
        queries, grads = q_ref[:, at], do_ref[:, at]
        kp, vp = keys_before[:, at], values_before[:, at]
        ko, vo = ko_ref[:, at], vo_ref[:, at]
        return (
            (queries, grads, kp, vp, ko, vo),
            (mm(kp, queries, NT), mm(ko, queries, NT)),
            (mm(vp, grads, NT), mm(vo, grads, NT)),
        )

    def second(head, state):
        inputs, (sp, so), (gp, go) = state
        rows = []
        for a in (0, 1):
            if a == 0:
                blocks = (sp[lo, lo], sp[hi, lo], so[lo, lo])
                pgrads = (gp[lo, lo], gp[hi, lo], go[lo, lo])
                middle = jnp.where(later, blocks[1], NEG)
            else:
                blocks = (sp[hi, hi], so[lo, hi], so[hi, hi])
                pgrads = (gp[hi, hi], go[lo, hi], go[hi, hi])
                middle = blocks[1]
            scores = (jnp.where(above, blocks[0], NEG), middle, jnp.where(below, blocks[2], NEG))
            peak = jnp.max(
                jnp.maximum(jnp.maximum(scores[0], scores[1]), scores[2]), axis=0, keepdims=True
            )
            weight = [jnp.exp2((s - peak) * (SCALE * LOG2E)) for s in scores]
            total = jnp.sum(weight[0] + weight[1] + weight[2], axis=0, keepdims=True)
            inverse = 1.0 / total
            probs = [w * inverse for w in weight]
            delta = jnp.sum(
                probs[0] * pgrads[0] + probs[1] * pgrads[1] + probs[2] * pgrads[2],
                axis=0,
                keepdims=True,
            )
            score_grad = [(p * (g - delta)).astype(BF) for p, g in zip(probs, pgrads)]
            rows.append(([p.astype(BF) for p in probs], score_grad))
            lanes = slice(a * half, (a + 1) * half)
            stat_ref[head, 0:1, lanes] = peak * (SCALE * LOG2E) + jnp.log2(total)
            stat_ref[head, 1:2, lanes] = delta

        def spread(which):
            one, two = rows[0][which], rows[1][which]
            before = jnp.concatenate(
                [jnp.concatenate([one[0], zero], 1), jnp.concatenate([one[1], two[0]], 1)], 0
            )
            own = jnp.concatenate(
                [jnp.concatenate([one[2], two[1]], 1), jnp.concatenate([zero, two[2]], 1)], 0
            )
            return before, own

        return inputs, spread(0), spread(1)

    def third(head, state):
        at = slice(head * HD, (head + 1) * HD)
        (queries, grads, kp, vp, ko, vo), (pp, po), (dp, do) = state
        out = mm(pp, vp, TN) + mm(po, vo, TN) + crossed[:, at].astype(F32)
        out_ref[:, at] = out.astype(BF)
        dq_ref[:, at] = ((mm(dp, kp, TN) + mm(do, ko, TN)) * SCALE).astype(BF)
        dk_ref[:, at] = mm(do, queries, NN) * SCALE
        dv_ref[:, at] = mm(po, grads, NN)

    ready = first(0)
    for head in range(heads):
        upcoming = first(head + 1) if head + 1 < heads else None
        third(head, second(head, ready))
        ready = upcoming


def self_part(info, q, do, k, v, one, two, three, own, back):
    heads = 4
    tokens, width = q.shape
    steps = width // (heads * HD)
    half = steps // 2
    shape = (tokens, heads * HD)

    def place(p, info):
        return (p + (info[0] & 1) * half) % steps

    spec = pl.BlockSpec(shape, lambda p, info: (0, place(p, info)))
    own_spec = pl.BlockSpec(shape, lambda p, info: (0, jnp.minimum(p, half - 1)))
    back_spec = pl.BlockSpec(shape, lambda p, info: (0, jnp.maximum(p - half, 0)))
    stat_spec = pl.BlockSpec((heads, 2, tokens), lambda p, info: (place(p, info), 0, 0))
    full = jax.ShapeDtypeStruct(q.shape, BF)
    wide = jax.ShapeDtypeStruct(q.shape, F32)
    stats = jax.ShapeDtypeStruct((width // HD, 2, tokens), F32)
    return pl.pallas_call(
        functools.partial(self_kernel, heads),
        grid_spec=pltpu.PrefetchScalarGridSpec(
            num_scalar_prefetch=1,
            grid=(steps,),
            in_specs=[spec] * 7 + [own_spec] * 2 + [back_spec] * 2,
            out_specs=[spec] * 5 + [stat_spec],
        ),
        out_shape=[full] * 3 + [wide] * 2 + [stats],
        compiler_params=pltpu.CompilerParams(vmem_limit_bytes=VMEM),
        cost_estimate=cost(14),
    )(info, q, do, k, v, one, two, three, *own, *back)


def next_kernel(
    heads, info_ref, one_ref, three_ref, do_ref, k_ref, v_ref, stat_ref, dkp_ref, dvp_ref,
    dk_ref, dv_ref,
):
    all_queries = jnp.where(info_ref[1] % 2 == 1, three_ref[...], one_ref[...])
    tokens = do_ref.shape[0]
    half = tokens // 2
    key_at = lax.broadcasted_iota(jnp.int32, (half, half), 0)
    query_at = lax.broadcasted_iota(jnp.int32, (half, half), 1)
    above = key_at > query_at
    zero = jnp.zeros((half, half), BF)
    lo, hi = slice(0, half), slice(half, None)

    def first(head):
        at = slice(head * HD, (head + 1) * HD)
        queries, grads = all_queries[:, at], do_ref[:, at]
        return queries, grads, mm(k_ref[:, at], queries, NT), mm(v_ref[:, at], grads, NT)

    def second(head, state):
        at = slice(head * HD, (head + 1) * HD)
        queries, grads, scores, prob_grad = state
        level, delta = stat_ref[head, 0:1, :], stat_ref[head, 1:2, :]

        def block(rows, lanes, mask):
            exponent = scores[rows, lanes] * (SCALE * LOG2E) - level[:, lanes]
            if mask:
                exponent = jnp.where(above, exponent, NEG)
            probs = jnp.exp2(exponent)
            return probs.astype(BF), (probs * (prob_grad[rows, lanes] - delta[:, lanes])).astype(BF)

        one, middle, last = block(lo, lo, True), block(hi, lo, False), block(hi, hi, True)
        low, score_grad = [
            jnp.concatenate(
                [
                    jnp.concatenate([one[i], zero], 1),
                    jnp.concatenate([middle[i], last[i]], 1),
                ],
                0,
            )
            for i in (0, 1)
        ]
        dk_ref[:, at] = (dkp_ref[:, at] + mm(score_grad, queries, NN) * SCALE).astype(BF)
        dv_ref[:, at] = (dvp_ref[:, at] + mm(low, grads, NN)).astype(BF)

    ready = first(0)
    for head in range(heads):
        upcoming = first(head + 1) if head + 1 < heads else None
        second(head, ready)
        ready = upcoming


def next_part(info, one, three, do, k, v, stats, dk, dv):
    heads = 8
    tokens, width = k.shape
    spec = pl.BlockSpec((tokens, heads * HD), lambda p: (0, p))
    stat_spec = pl.BlockSpec((heads, 2, tokens), lambda p: (p, 0, 0))
    full = jax.ShapeDtypeStruct(k.shape, BF)
    return pl.pallas_call(
        functools.partial(next_kernel, heads),
        grid=(width // (heads * HD),),
        in_specs=[pl.BlockSpec(memory_space=pltpu.SMEM)]
        + [spec] * 5
        + [stat_spec]
        + [spec] * 2,
        out_specs=[spec] * 2,
        out_shape=[full] * 2,
        compiler_params=pltpu.CompilerParams(vmem_limit_bytes=VMEM),
        cost_estimate=cost(8),
    )(info, one, three, do, k, v, stats, dk, dv)


def halving_order(fsdp, seq):
    bits = [("fsdp", 1 << i) for i in range(1, fsdp.bit_length() - 1)]
    seq_bits = [("seq", 1 << i) for i in range(seq.bit_length() - 1)]
    return bits + seq_bits[1:] + seq_bits[:1]


def row_order(fsdp, seq, rows):
    index = np.arange(rows).reshape(seq * fsdp, -1)
    block = np.arange(seq * fsdp)
    keys = []
    for axis, bit in halving_order(fsdp, seq) + [("fsdp", 1)]:
        value = block % fsdp if axis == "fsdp" else block // fsdp
        keys.append((value // bit) % 2)
    order = np.lexsort(keys[::-1])
    return index[order].reshape(-1)


def take_half(value, upper):
    half = value.shape[0] // 2
    return lax.dynamic_slice_in_dim(value, upper * half, half, 0)


def halve_kernel(spans, axis, bit, info_ref, *refs):
    sources, (mine_ref, other_ref) = refs[:-2], refs[-2:]
    count = len(sources) // 2
    half = mine_ref.shape[0]
    upper = (info_ref[0 if axis == "fsdp" else 1] // bit) % 2
    for ref, which in ((mine_ref, upper), (other_ref, 1 - upper)):
        at = pl.ds(pl.multiple_of(which * half, 16), half)
        start = 0
        for keep, got, parts in zip(sources[:count], sources[count:], spans):
            width = keep.shape[-1]
            for part in range(parts):
                where = (part, at) if len(keep.shape) == 3 else (at,)
                total = keep[where].astype(F32) + got[where].astype(F32)
                ref[:, start : start + width] = total.astype(BF)
                start += width


def halve(info, keeps, received, stage):
    axis, bit = stage
    spans = [x.shape[0] if x.ndim == 3 else 1 for x in keeps]
    rows = keeps[0].shape[-2]
    width = sum(parts * x.shape[-1] for parts, x in zip(spans, keeps))
    if rows // 2 % 16:
        upper = (info[0 if axis == "fsdp" else 1] // bit) % 2
        sums = [
            (x.astype(F32) + y.astype(F32)).reshape(-1, rows, x.shape[-1])
            for x, y in zip(keeps, received)
        ]
        total = jnp.concatenate([part for x in sums for part in x], -1)
        return take_half(total, upper).astype(BF), take_half(total, 1 - upper).astype(BF)
    return pl.pallas_call(
        functools.partial(halve_kernel, spans, axis, bit),
        in_specs=[pl.BlockSpec(memory_space=pltpu.SMEM)]
        + [pl.BlockSpec(memory_space=pltpu.VMEM)] * (2 * len(keeps)),
        out_shape=[jax.ShapeDtypeStruct((rows // 2, width), BF)] * 2,
        compiler_params=pltpu.CompilerParams(vmem_limit_bytes=VMEM),
        cost_estimate=cost(1),
    )(info, *keeps, *received)


def on_device(
    self_query, self_key, self_value, cross_query, neighbours, neighbour_count, kv_weight, out_grad
):
    fsdp, seq = lax.axis_size("fsdp"), lax.axis_size("seq")
    shard, slab = lax.axis_index("fsdp"), lax.axis_index("seq")
    q, k, v, cq, do = (x[0] for x in (self_query, self_key, self_value, cross_query, out_grad))
    nb, counts = neighbours[0], neighbour_count[0]
    tokens, width = q.shape
    groups, per, enc = nb.shape
    info = jnp.stack([shard, slab]).astype(jnp.int32)

    last = pack(nb, counts)
    nb_last = shift(last, "seq", 1)

    nb_peer = swap(nb, "fsdp", 1)
    mine, other, pair = cut(after(info, last), counts, kv_weight, cq, do)
    near = swap(other, "fsdp", 1)
    weights = [
        [here, near, *[swap(x, "fsdp", piece) for piece in range(2, fsdp, 2)]]
        for here, x in zip(mine, stack(mine, near))
    ]
    peer = swap(pair, "fsdp", 1)

    even = slab % 2 == 0

    def pick(when_even, when_odd, *others):
        return jnp.where(after(even, nb_last, *others), when_even, when_odd)

    def hop(value):
        odds = [(i, i + 2) for i in range(1, seq - 2, 2)]
        return lax.ppermute(value, "seq", odds + [(i, i - 2) for i in range(2, seq, 2)])

    far_one = hop(pick(q, k))
    one = swap(pick(k, q), "seq", 1)
    far_two = hop(pick(do, v))

    nb_last = after(nb_last, peer, nb_peer)
    peer_last = swap(nb_last, "fsdp", 1)
    nbs = [nb_last, nb, peer_last, nb_peer]

    stages = halving_order(fsdp, seq)
    split_at = fsdp.bit_length() - 2

    turn = jnp.asarray(np.eye(enc)[row_order(fsdp, seq, enc)], BF)
    held, pairs = [], []
    for group in range(CHUNKS // TOGETHER):
        results = cross(group, info, counts, turn, nbs, weights[group], cq, do, peer, held)
        held, (keep, send) = results[:4], results[4:6]
        if not group:
            turn = results[6]
            second_load = pick(v, far_one, turn)
            two = swap(second_load, "seq", 1)
        received = swap(send, *stages[0])
        for stage in range(1, split_at):
            keep, send = halve(info, [keep], [received], stages[stage])
            received = swap(send, *stages[stage])
        pairs.append((keep, received))
    own = held[:2]
    back = [swap(x, "fsdp", 1) for x in after(held[2:], pairs[0][1], one, two)]
    third = pick(far_one, far_two, pairs[-1][0], second_load)
    three = swap(third, "seq", 1)

    halves = [halve(info, [pairs[0][0]], [pairs[0][1]], stages[split_at])]
    got = [swap(halves[0][1], *stages[split_at])]
    halves.append(
        halve(after(info, halves[0][1], *back), [pairs[1][0]], [pairs[1][1]], stages[split_at])
    )
    got.append(swap(halves[1][1], *stages[split_at]))
    four = swap(pick(far_two, do, halves[1][1], third), "seq", 1)
    keeps, sends = zip(
        halve(after(info, halves[1][1]), [halves[0][0]], [got[0]], stages[split_at + 1]),
        halve(info, [halves[1][0]], [got[1]], stages[split_at + 1]),
    )
    got = [swap(send, *stages[split_at + 1]) for send in sends]
    block_out, query_grad, cross_grad, dk, dv, stats = self_part(
        after(info, *sends), q, do, k, v, one, two, three, own, back
    )
    stats_after = shift(stats, "seq", -1)
    key_grad, value_grad = next_part(info, one, three, four, k, v, stats_after, dk, dv)

    for stage in range(split_at + 2, len(stages)):
        keep, send = halve(after(info, stats), keeps, got, stages[stage])
        keeps, got = [keep], [swap(send, *stages[stage])]
    total = keeps[0].astype(F32) + after(got[0], key_grad).astype(F32)
    core = shard % 2
    away = swap(take_half(total, 1 - core).astype(BF), "fsdp", 1).astype(F32)
    nearby = take_half(total, core)
    key_mine, key_away, value_mine, value_away = [
        jnp.concatenate(
            [x[:, (2 * c + part) * PAIR : (2 * c + part + 1) * PAIR] for c in range(CHUNKS)], -1
        )
        for part in (0, 1)
        for x in (nearby, away)
    ]
    low = shard % 2 == 0
    weight_grad = jnp.concatenate(
        [
            jnp.where(low, key_mine, key_away),
            jnp.where(low, key_away, key_mine),
            jnp.where(low, value_mine, value_away),
            jnp.where(low, value_away, value_mine),
        ],
        -1,
    )

    return (
        block_out[None],
        query_grad[None],
        key_grad[None],
        value_grad[None],
        cross_grad[None],
        weight_grad,
    )


def solution(mesh):
    in_specs = (
        P("fsdp", "seq", None),
        P("fsdp", "seq", None),
        P("fsdp", "seq", None),
        P("fsdp", "seq", None),
        P("fsdp", "seq", None, None),
        P("fsdp", "seq"),
        P("fsdp", None),
        P("fsdp", "seq", None),
    )
    out_specs = (
        P("fsdp", "seq", None),
        P("fsdp", "seq", None),
        P("fsdp", "seq", None),
        P("fsdp", "seq", None),
        P("fsdp", "seq", None),
        P(("seq", "fsdp"), None),
    )
    return jax.shard_map(
        on_device, mesh=mesh, in_specs=in_specs, out_specs=out_specs, check_vma=False
    )
```
